32 devices in a mesh: grp: 4 (over z), blk: 8 (over y, x, core).
Axes of the slice: x: 2, y: 2, z: 4, core: 2. Of those that a mesh axis runs over, the one named last changes fastest.
Arguments:
- embeddings: bfloat16 [8192, 768], P(('grp', 'blk')), may hold values from -6 to 6
- target: int32 [8192, 1], P(('grp', 'blk')), may hold values from 0 to 31; in each aligned block of 256 rows (0 to 255, 256 to 511, ...) at most 16 rows name the same one
- cluster: int32 [8192], P(('grp', 'blk')), may hold values from 0 to 15
Outputs:
- nearest: float32 [8192], P(('grp', 'blk'))
The draws below stay inside these ranges and needn't reach their ends.
Inputs may be any that keep to these rules, and one draw needn't show every extreme that they name: The rows of one device send at most 16 rows to any one target.
All inputs are finite; a program needn't handle non-finite values.
Results may differ from the reference program's by a relative error of at most 0.0014.
Values may be sent and summed in bfloat16 or wider, within the bound.
No kernel may reach another device: no remote copies, remote signals or barrier semaphores. Data moves between devices by JAX's collectives and lax.ppermute only.
A program may use at most 64 MiB of HBM per device.

```python
import math
import jax
import jax.numpy as jnp
import numpy as np
from jax import lax

D = 768
CLUSTERS = 64
ROWS_DEV = 256
ROWS = 8192
CAP = 16
N_GRP = 4
N_BLK = 8
DEVICES = 32


def place_ends(array, key, smallest, high):
    index_at = [jax.random.randint(jax.random.fold_in(key, axis), (), 0, length) for axis, length in enumerate(array.shape)]
    longest = array.shape.index(max(array.shape))
    beside = index_at[:longest] + [(index_at[longest] + 1) % array.shape[longest]] + index_at[longest + 1:]
    return array.at[tuple(index_at)].set(smallest).at[tuple(beside)].set(high)


def block_scale(rng, extent, cuts, low, largest):
    gain = 1.0
    for axis_at, parts in cuts:
        draws = jax.random.uniform(jax.random.fold_in(jax.random.fold_in(rng, 6), axis_at), (parts,), jnp.float32, low / len(cuts), largest / len(cuts))
        gain = gain * jnp.repeat(jnp.exp(draws), extent[axis_at] // parts).reshape((-1,) + (1,) * (len(extent) - 1 - axis_at))
    return gain


def cumulative_ranks(number_of, lean):
    loads = [(1 << 20) // math.isqrt(rank ** lean) + 1 for rank in range(1, number_of + 1)]
    deviation = 1 + sum(loads) // (1 << 30)
    return np.cumsum(np.array([max(1, weight // deviation) for weight in loads]))


def ranked_ids(stream_key, extent, count, slope):
    grid = cumulative_ranks(count, slope)
    pick = jax.random.randint(jax.random.fold_in(stream_key, 1), extent, 0, int(grid[count - 1]))
    standing = jnp.searchsorted(jnp.asarray(grid, jnp.int32), pick, side="right")
    return jax.random.permutation(jax.random.fold_in(stream_key, 2), count)[standing].astype(jnp.int32)


def assign_block(own_key, own, number, rows, count, top, limit, lean):
    sequence = jax.random.permutation(own_key, count)
    crowded, usual = load_shares(count, rows * top, limit, lean, True), load_shares(count, rows * top, limit, lean, False)
    places = jnp.arange(count)

    def named(tallies, offset_by):
        used = int((tallies > 0).sum())
        fixed = max(1, used // 4)
        passed = fixed + (places - fixed + offset_by * (used - fixed)) % max(1, count - fixed)
        return jnp.zeros((count,), jnp.int32).at[sequence[jnp.where(places < fixed, places, passed)]].set(jnp.asarray(tallies, jnp.int32))

    tallies = jnp.where(number % 4 == 0, named(crowded, number // 4), named(usual, number - number // 4 - 1))
    mixed = jax.random.permutation(jax.random.fold_in(own, 3), count)
    donor, taker = mixed[0:count // 2 * 2:2], mixed[1:count // 2 * 2:2]
    margin = jnp.minimum(tallies[donor] - 1, limit - tallies[taker]) // 2
    margin = jnp.where((donor == sequence[0]) | (taker == sequence[0]) | (tallies[taker] == 0), 0, jnp.maximum(margin, 0))
    passed = jax.random.randint(jax.random.fold_in(own, 4), (count // 2,), 0, 1 << 20) % (margin + 1)
    tallies = tallies.at[donor].add(-passed).at[taker].add(passed)
    items = jnp.searchsorted(jnp.cumsum(tallies), jnp.arange(rows * top), side="right").astype(jnp.int32)
    grid = items.reshape(top, rows).T
    grid = grid[jax.random.permutation(jax.random.fold_in(own, 1), rows)]
    offset_by = jax.random.randint(jax.random.fold_in(own, 2), (rows, 1), 0, top)
    return jnp.take_along_axis(grid, (jnp.arange(top)[None, :] + offset_by) % top, axis=1)


def load_shares(number_of, total, limit, slope, full):
    weights = [(1 << 20) // math.isqrt(grade ** slope) + 1 for grade in range(1, number_of + 1)]
    largest = limit if full else min(limit, max(-(-total // number_of), total * weights[0] // sum(weights)))
    least = 1 if total - largest >= number_of - 1 else 0
    given, surplus = [largest] + [least] * (number_of - 1), total - largest - least * (number_of - 1)
    while surplus > 0:
        free = [i for i in range(1, number_of) if given[i] < largest] or [i for i in range(1, number_of) if given[i] < limit]
        pool, remaining = sum([weights[i] for i in free]), surplus
        for i in free:
            extra = min(limit - given[i], max(1, remaining * weights[i] // pool), surplus)
            given[i] = given[i] + extra
            surplus = surplus - extra
    return np.array(given)


def noise(rng, shape, deviation, reach, shards=(), held_as=jnp.bfloat16):
    drawn = deviation * jax.random.normal(rng, shape, jnp.float32)
    if shards:
        drawn = drawn * block_scale(rng, shape, shards, -0.22, 0.18)
    return jnp.clip(drawn, -reach, reach).astype(held_as)


def setup_inputs(seed: int = 0) -> dict:
    splits = jax.random.split(jax.random.key(seed), 4)
    embeddings = noise(splits[0], (ROWS, D), 1.0, 6.0, ((0, 32),))
    target_keys = jax.random.split(jax.random.fold_in(splits[1], 1), ROWS // ROWS_DEV)
    target_turns = jax.random.permutation(jax.random.fold_in(splits[1], 3), ROWS // ROWS_DEV)
    target = jax.vmap(lambda own, number: assign_block(jax.random.fold_in(splits[1], 2), own, number, ROWS_DEV, DEVICES, 1, CAP, 2))(target_keys, target_turns).reshape((ROWS, 1))
    cluster = place_ends(ranked_ids(splits[2], (ROWS,), CLUSTERS // N_GRP, 2), jax.random.fold_in(splits[2], 3), 0, (CLUSTERS // N_GRP) - 1).astype(jnp.int32)
    return {"embeddings": embeddings, "target": target, "cluster": cluster}


def normalize(embeddings):
    widened = embeddings.astype(jnp.float32)
    scale_inv = lax.rsqrt(lax.optimization_barrier(jnp.sum(widened * widened, axis=1, keepdims=True)) + 1e-06)
    return (widened * scale_inv).astype(jnp.bfloat16)

def reference(embeddings, target, cluster):
    normed = normalize(embeddings)
    total = normed.shape[0]
    owner_key = target[:, 0] // N_BLK * CLUSTERS + cluster
    positions = jnp.arange(total, dtype=jnp.int32)
    block = math.gcd(total, 1024)

    def one_block(first):
        rows = lax.dynamic_slice_in_dim(normed, first, block, 0)
        keys = lax.dynamic_slice_in_dim(owner_key, first, block, 0)
        scores = jnp.dot(rows, normed.T, preferred_element_type=jnp.float32)
        row_pos = first + jnp.arange(block, dtype=jnp.int32)
        allowed = (keys[:, None] == owner_key[None, :]) & (row_pos[:, None] != positions[None, :])
        return lax.optimization_barrier(jnp.max(jnp.where(allowed, scores, -1.0), axis=1))
    firsts = jnp.arange(total // block, dtype=jnp.int32) * block
    return lax.map(one_block, firsts).reshape(total)
```

```python
import functools

import jax
import jax.numpy as jnp
from jax import lax
from jax.experimental import pallas as pl
from jax.experimental.pallas import tpu as pltpu
from jax.sharding import PartitionSpec as P

CLUSTERS = 64
TAIL = 16


def pack_kernel(per_group, emb_ref, target_ref, cluster_ref, out_ref):
    rows, width = emb_ref.shape
    x = emb_ref[...].astype(jnp.float32)
    scale = lax.rsqrt(jnp.sum(x * x, axis=1, keepdims=True) + 1e-06)
    out_ref[:rows, :] = (x * scale).astype(jnp.bfloat16)
    key = target_ref[...] // per_group * CLUSTERS + cluster_ref[...]
    key = jnp.concatenate([key, jnp.zeros((1, width - rows), jnp.int32)], axis=1)
    key = jnp.broadcast_to(key.astype(jnp.float32), (TAIL, width))
    out_ref[rows:, :] = key.astype(jnp.bfloat16)


def pack(embeddings, target, cluster, per_group):
    rows, width = embeddings.shape
    return pl.pallas_call(
        functools.partial(pack_kernel, per_group),
        out_shape=jax.ShapeDtypeStruct((rows + TAIL, width), jnp.bfloat16),
        name="pack",
    )(embeddings, target.reshape(1, rows), cluster.reshape(1, rows))


def compare_kernel(rows, own_ref, plane_ref, *refs):
    col_refs, out_ref = refs[:-1], refs[-1]
    tile = pl.program_id(0)

    @pl.when(tile == 0)
    def _():
        out_ref[...] = jnp.full_like(out_ref, -1.0)

    block = plane_ref[:rows, :]
    keys = plane_ref[rows:, :rows].astype(jnp.float32)[:1]
    row_keys = jnp.transpose(jnp.broadcast_to(keys, (128, rows)))
    row_keys = jnp.concatenate([row_keys] * (rows // 128), axis=1)
    for at, col_ref in enumerate(col_refs):
        scores = lax.dot_general(
            block, col_ref[:rows, :], (((1,), (1,)), ((), ())), preferred_element_type=jnp.float32
        )
        col_keys = col_ref[rows:, :rows].astype(jnp.float32)[:1]
        allowed = row_keys == col_keys
        if at == 0:
            row_pos = lax.broadcasted_iota(jnp.int32, scores.shape, 0) + (tile - own_ref[0]) * rows
            allowed = allowed & (row_pos != lax.broadcasted_iota(jnp.int32, scores.shape, 1))
        best = jnp.max(jnp.where(allowed, scores, -1.0), axis=0, keepdims=True)
        out_ref[at : at + 1, :] = jnp.maximum(out_ref[at : at + 1, :], best)


def compare(plane, columns, own):
    length, width = columns[0].shape
    rows = length - TAIL
    tiles = plane.shape[0] // length
    return pl.pallas_call(
        functools.partial(compare_kernel, rows),
        grid_spec=pltpu.PrefetchScalarGridSpec(
            num_scalar_prefetch=1,
            grid=(tiles,),
            in_specs=[pl.BlockSpec((length, width), lambda i, own: (i, 0))]
            + [pl.BlockSpec((length, width), lambda i, own: (0, 0)) for _ in columns],
            out_specs=pl.BlockSpec((len(columns), rows), lambda i, own: (0, 0)),
        ),
        out_shape=jax.ShapeDtypeStruct((len(columns), rows), jnp.float32),
        name="compare",
    )(own, plane, *columns)


def body(embeddings, target, cluster):
    groups = lax.axis_size("grp")
    per_group = lax.axis_size("blk")
    packed = pack(embeddings, target, cluster, per_group)
    columns = [packed]
    for shift in range(1, groups):
        columns.append(
            lax.ppermute(packed, "grp", [(z, (z + shift) % groups) for z in range(groups)])
        )
    plane = lax.all_gather(packed, "blk", axis=0, tiled=True)
    own = lax.axis_index("blk").astype(jnp.int32).reshape(1)
    best = compare(plane, columns, own)
    nearest = best[0]
    for shift in range(1, groups):
        back = [((z + shift) % groups, z) for z in range(groups)]
        nearest = jnp.maximum(nearest, lax.ppermute(best[shift], "grp", back))
    return nearest


def solution(mesh):
    return jax.shard_map(
        body,
        mesh=mesh,
        in_specs=(P(("grp", "blk"), None), P(("grp", "blk"), None), P(("grp", "blk"))),
        out_specs=P(("grp", "blk")),
        check_vma=False,
    )
```

```python
import functools

import jax
import jax.numpy as jnp
from jax import lax
from jax.experimental import pallas as pl
from jax.experimental.pallas import tpu as pltpu
from jax.sharding import PartitionSpec as P

CLUSTERS = 64
TAIL = 16
VMEM = 48 << 20


def pack_kernel(per_group, emb_ref, target_ref, cluster_ref, out_ref):
    rows, width = emb_ref.shape
    x = emb_ref[...].astype(jnp.float32)
    scale = lax.rsqrt(jnp.sum(x * x, axis=1, keepdims=True) + 1e-06)
    out_ref[:rows, :] = (x * scale).astype(jnp.bfloat16)
    key = target_ref[...] // per_group * CLUSTERS + cluster_ref[...] + 1
    key = jnp.concatenate([key, jnp.zeros((1, width - rows), jnp.int32)], axis=1)
    key = jnp.broadcast_to(key.astype(jnp.float32), (TAIL, width))
    out_ref[rows:, :] = key.astype(jnp.bfloat16)


def pack(embeddings, target, cluster, per_group):
    rows, width = embeddings.shape
    return pl.pallas_call(
        functools.partial(pack_kernel, per_group),
        out_shape=jax.ShapeDtypeStruct((rows + TAIL, width), jnp.bfloat16),
        name="pack",
    )(embeddings, target.reshape(1, rows), cluster.reshape(1, rows))


def compare_kernel(n_plane, n_cols, *refs):
    plane = refs[:n_plane]
    cols = (plane[0],) + refs[n_plane : n_plane + n_cols]
    outs = refs[n_plane + n_cols :]
    col_outs, row_outs = outs[: n_cols + 1], outs[n_cols + 1 : n_cols + 1 + n_plane]
    rows = col_outs[0].shape[1]
    col_keys = [ref[rows:, :rows].astype(jnp.float32)[:1] for ref in cols]
    best = [jnp.full((1, rows), -1.0, jnp.float32) for _ in cols]
    for k, ref in enumerate(plane):
        keys = ref[rows:, :rows].astype(jnp.float32)[:1]
        row_keys = jnp.transpose(jnp.broadcast_to(keys, (128, rows)))
        row_keys = jnp.concatenate([row_keys] * (rows // 128), axis=1)
        block = ref[:rows, :]
        row_best = jnp.full((rows, 128), -1.0, jnp.float32)
        for at, col_ref in enumerate(cols):
            scores = lax.dot_general(
                block, col_ref[:rows, :], (((1,), (1,)), ((), ())), preferred_element_type=jnp.float32
            )
            allowed = row_keys == col_keys[at]
            if k == 0 and at == 0:
                one = lax.broadcasted_iota(jnp.int32, scores.shape, 0)
                other = lax.broadcasted_iota(jnp.int32, scores.shape, 1)
                allowed = allowed & (one != other)
            masked = jnp.where(allowed, scores, -1.0)
            best[at] = jnp.maximum(best[at], jnp.max(masked, axis=0, keepdims=True))
            if at:
                for lane in range(0, rows, 128):
                    row_best = jnp.maximum(row_best, masked[:, lane : lane + 128])
        if n_cols:
            row_outs[k][...] = jnp.max(jnp.transpose(row_best), axis=0, keepdims=True)
    for at, ref in enumerate(col_outs):
        ref[...] = best[at]


def compare(plane, cols):
    length, width = plane[0].shape
    rows = length - TAIL
    one = jax.ShapeDtypeStruct((1, rows), jnp.float32)
    n_rows = len(plane) if cols else 0
    outs = pl.pallas_call(
        functools.partial(compare_kernel, len(plane), len(cols)),
        out_shape=[one] * (1 + len(cols) + n_rows),
        compiler_params=pltpu.CompilerParams(vmem_limit_bytes=VMEM),
        cost_estimate=pl.CostEstimate(
            flops=2 * len(plane) * (1 + len(cols)) * rows * rows * width,
            bytes_accessed=2 * (len(plane) + len(cols)) * length * width,
            transcendentals=0,
        ),
        name="compare",
    )(*plane, *cols)
    return outs[: 1 + len(cols)], outs[1 + len(cols) :]


def plane_shift(x, mask):
    size = lax.axis_size("blk")
    return lax.ppermute(x, "blk", [(i, i ^ mask) for i in range(size)])


def meetings(groups):
    perms = [[(z, (z - d) % groups) for z in range(groups)] for d in range(1, (groups + 1) // 2)]
    if groups % 2 == 0:
        half = groups // 2
        perms.append([(z, z + half) if z % 2 == 0 else (z + half, z) for z in range(half)])
    return perms


def body(embeddings, target, cluster):
    groups = lax.axis_size("grp")
    per_group = lax.axis_size("blk")
    packed = pack(embeddings, target, cluster, per_group)
    perms = meetings(groups)
    cols = [lax.ppermute(packed, "grp", perm) for perm in perms]
    same_core = [packed] + [plane_shift(packed, mask) for mask in range(2, per_group, 2)]
    plane = []
    for block in same_core:
        plane += [block, plane_shift(block, 1)]
    col_best, row_best = compare(plane, cols)
    found = [col_best[0]]
    for perm, best in zip(perms, col_best[1:]):
        back = [(b, a) for a, b in perm]
        got = lax.ppermute(best, "grp", back)
        if len(back) < groups:
            asked = jnp.array([a for a, _ in perm])
            here = jnp.any(asked == lax.axis_index("grp"))
            got = jnp.where(here, got, -1.0)
        found.append(got)
    for mask, best in enumerate(row_best):
        found.append(plane_shift(best, mask) if mask else best)
    return functools.reduce(jnp.maximum, found).reshape(-1)


def solution(mesh):
    return jax.shard_map(
        body,
        mesh=mesh,
        in_specs=(P(("grp", "blk"), None), P(("grp", "blk"), None), P(("grp", "blk"))),
        out_specs=P(("grp", "blk")),
        check_vma=False,
    )
```

```python
import functools

import jax
import jax.numpy as jnp
from jax import lax
from jax.experimental import pallas as pl
from jax.experimental.pallas import tpu as pltpu
from jax.sharding import PartitionSpec as P

CLUSTERS = 64
TAIL = 16
VMEM = 48 << 20
VMEM_PACK = 8 << 20


def pack_kernel(per_group, emb_ref, target_ref, cluster_ref, out_ref):
    rows, width = emb_ref.shape
    x = emb_ref[...].astype(jnp.float32)
    scale = lax.rsqrt(jnp.sum(x * x, axis=1, keepdims=True) + 1e-06)
    out_ref[:rows, :] = (x * scale).astype(jnp.bfloat16)
    key = target_ref[...] // per_group * CLUSTERS + cluster_ref[...] + 1
    key = jnp.concatenate([key, jnp.zeros((1, width - rows), jnp.int32)], axis=1)
    key = jnp.broadcast_to(key.astype(jnp.float32), (TAIL, width))
    out_ref[rows:, :] = key.astype(jnp.bfloat16)


def pack(embeddings, target, cluster, per_group):
    rows, width = embeddings.shape
    return pl.pallas_call(
        functools.partial(pack_kernel, per_group),
        out_shape=jax.ShapeDtypeStruct((rows + TAIL, width), jnp.bfloat16),
        compiler_params=pltpu.CompilerParams(vmem_limit_bytes=VMEM_PACK),
        name="pack",
    )(embeddings, target.reshape(1, rows), cluster.reshape(1, rows))


def compare_kernel(n_plane, n_cols, own_ref, *refs):
    plane = refs[:n_plane]
    cols = (plane[0],) + refs[n_plane : n_plane + n_cols]
    outs = refs[n_plane + n_cols :]
    col_outs, row_out = outs[: n_cols + 1], outs[n_cols + 1]
    rows = col_outs[0].shape[1]
    col_keys = [ref[rows:, :rows].astype(jnp.float32)[:1] for ref in cols]
    best = [jnp.full((1, rows), -1.0, jnp.float32) for _ in cols]
    for k, ref in enumerate(plane):
        keys = ref[rows:, :rows].astype(jnp.float32)[:1]
        row_keys = jnp.transpose(jnp.broadcast_to(keys, (128, rows)))
        row_keys = jnp.concatenate([row_keys] * (rows // 128), axis=1)
        block = ref[:rows, :]
        row_best = jnp.full((rows, 128), -1.0, jnp.float32)
        for at, col_ref in enumerate(cols):
            scores = lax.dot_general(
                block, col_ref[:rows, :], (((1,), (1,)), ((), ())), preferred_element_type=jnp.float32
            )
            allowed = row_keys == col_keys[at]
            if k == 0 and at == 0:
                one = lax.broadcasted_iota(jnp.int32, scores.shape, 0)
                other = lax.broadcasted_iota(jnp.int32, scores.shape, 1)
                allowed = allowed & (one != other)
            masked = jnp.where(allowed, scores, -1.0)
            best[at] = jnp.maximum(best[at], jnp.max(masked, axis=0, keepdims=True))
            if at:
                for lane in range(0, rows, 128):
                    row_best = jnp.maximum(row_best, masked[:, lane : lane + 128])
        row_out[own_ref[0] ^ k] = jnp.max(jnp.transpose(row_best), axis=0, keepdims=True)
    for at, ref in enumerate(col_outs):
        ref[...] = best[at]


def compare(own, plane, cols):
    length, width = plane[0].shape
    rows = length - TAIL
    one = jax.ShapeDtypeStruct((1, rows), jnp.float32)
    outs = pl.pallas_call(
        functools.partial(compare_kernel, len(plane), len(cols)),
        out_shape=[one] * (1 + len(cols))
        + [jax.ShapeDtypeStruct((len(plane), 1, rows), jnp.float32)],
        in_specs=[pl.BlockSpec(memory_space=pltpu.SMEM)]
        + [pl.BlockSpec(memory_space=pltpu.VMEM)] * (len(plane) + len(cols)),
        compiler_params=pltpu.CompilerParams(vmem_limit_bytes=VMEM),
        cost_estimate=pl.CostEstimate(
            flops=2 * len(plane) * (1 + len(cols)) * rows * rows * width,
            bytes_accessed=2 * (len(plane) + len(cols)) * length * width,
            transcendentals=0,
        ),
        name="compare",
    )(own, *plane, *cols)
    return outs[:-1], outs[-1]


def plane_shift(x, mask):
    size = lax.axis_size("blk")
    return lax.ppermute(x, "blk", [(i, i ^ mask) for i in range(size)])


def meetings(groups):
    perms = [[(z, (z - d) % groups) for z in range(groups)] for d in range(1, (groups + 1) // 2)]
    if groups % 2 == 0:
        half = groups // 2
        perms.append([(z, z + half) if z % 2 == 0 else (z + half, z) for z in range(half)])
    return perms


def body(embeddings, target, cluster):
    groups = lax.axis_size("grp")
    per_group = lax.axis_size("blk")
    packed = pack(embeddings, target, cluster, per_group)
    perms = meetings(groups)
    cols = [lax.ppermute(packed, "grp", perm) for perm in perms]
    same_core = [plane_shift(packed, mask) for mask in range(2, per_group, 2)]
    own_block = lax.optimization_barrier((packed, same_core[0]))[0] if same_core else packed
    plane = []
    for block in [own_block] + same_core:
        plane += [block, plane_shift(block, 1)]
    plane[0] = packed
    own = lax.axis_index("blk").astype(jnp.int32).reshape(1)
    col_best, row_best = compare(own, plane, cols)
    found = [col_best[0]]
    for perm, best in zip(perms, col_best[1:]):
        back = [(b, a) for a, b in perm]
        got = lax.ppermute(best, "grp", back)
        if len(back) < groups:
            asked = jnp.array([a for a, _ in perm])
            here = jnp.any(asked == lax.axis_index("grp"))
            got = jnp.where(here, got, -1.0)
        found.append(got)
    rows_back = lax.all_to_all(row_best, "blk", split_axis=0, concat_axis=0, tiled=True)
    found.append(jnp.max(rows_back, axis=0))
    return functools.reduce(jnp.maximum, found).reshape(-1)


def solution(mesh):
    return jax.shard_map(
        body,
        mesh=mesh,
        in_specs=(P(("grp", "blk"), None), P(("grp", "blk"), None), P(("grp", "blk"))),
        out_specs=P(("grp", "blk")),
        check_vma=False,
    )
```

```python
import functools

import jax
import jax.numpy as jnp
from jax import lax
from jax.experimental import pallas as pl
from jax.experimental.pallas import tpu as pltpu
from jax.sharding import PartitionSpec as P

CLUSTERS = 64
TAIL = 16
VMEM = 24 << 20
VMEM_SMALL = 8 << 20


def pack_kernel(per_group, emb_ref, target_ref, cluster_ref, out_ref):
    rows, width = emb_ref.shape
    x = emb_ref[...].astype(jnp.float32)
    scale = lax.rsqrt(jnp.sum(x * x, axis=1, keepdims=True) + 1e-06)
    out_ref[:rows, :] = (x * scale).astype(jnp.bfloat16)
    key = target_ref[...] // per_group * CLUSTERS + cluster_ref[...] + 1
    key = jnp.concatenate([key, jnp.zeros((1, width - rows), jnp.int32)], axis=1)
    key = jnp.broadcast_to(key.astype(jnp.float32), (TAIL, width))
    out_ref[rows:, :] = key.astype(jnp.bfloat16)


def pack(embeddings, target, cluster, per_group):
    rows, width = embeddings.shape
    return pl.pallas_call(
        functools.partial(pack_kernel, per_group),
        out_shape=jax.ShapeDtypeStruct((rows + TAIL, width), jnp.bfloat16),
        compiler_params=pltpu.CompilerParams(vmem_limit_bytes=VMEM_SMALL),
        name="pack",
    )(embeddings, target.reshape(1, rows), cluster.reshape(1, rows))


def keys_down(ref, rows):
    keys = ref[rows:, :rows].astype(jnp.float32)[:1]
    row_keys = jnp.transpose(jnp.broadcast_to(keys, (128, rows)))
    return jnp.concatenate([row_keys] * (rows // 128), axis=1)


def score_block(row_ref, cols, best, mine):
    rows = best[0].shape[1]
    row_keys = keys_down(row_ref, rows)
    row_best = None
    for at, col_ref in cols:
        scores = lax.dot_general(
            row_ref[:rows, :], col_ref[:rows, :], (((1,), (1,)), ((), ())), preferred_element_type=jnp.float32
        )
        allowed = row_keys == col_ref[rows:, :rows].astype(jnp.float32)[:1]
        if mine and at == 0:
            one = lax.broadcasted_iota(jnp.int32, scores.shape, 0)
            other = lax.broadcasted_iota(jnp.int32, scores.shape, 1)
            allowed = allowed & (one != other)
        masked = jnp.where(allowed, scores, -1.0)
        best[at] = jnp.maximum(best[at], jnp.max(masked, axis=0, keepdims=True))
        if at > 1:
            for lane in range(0, rows, 128):
                part = masked[:, lane : lane + 128]
                row_best = part if row_best is None else jnp.maximum(row_best, part)
    if row_best is None:
        return None
    return jnp.max(jnp.transpose(row_best), axis=0, keepdims=True)


def early_kernel(n_plane, n_cols, *refs):
    plane, cols = refs[:n_plane], refs[n_plane : n_plane + n_cols]
    outs = refs[n_plane + n_cols :]
    rows_out = outs[-1]
    rows = rows_out.shape[2]
    chip = lax.axis_index("blk") // 2
    best = [jnp.full((1, rows), -1.0, jnp.float32)] * n_cols
    for k, ref in enumerate(plane):
        rows_out[chip ^ k] = score_block(ref, list(enumerate(cols)), best, k == 0)
    for ref, value in zip(outs, best):
        ref[...] = value


def compare_early(plane, cols):
    length, width = plane[0].shape
    rows = length - TAIL
    outs = pl.pallas_call(
        functools.partial(early_kernel, len(plane), len(cols)),
        out_shape=[jax.ShapeDtypeStruct((1, rows), jnp.float32)] * len(cols)
        + [jax.ShapeDtypeStruct((len(plane), 1, rows), jnp.float32)],
        compiler_params=pltpu.CompilerParams(vmem_limit_bytes=VMEM),
        cost_estimate=pl.CostEstimate(
            flops=2 * len(plane) * len(cols) * rows * rows * width,
            bytes_accessed=2 * (len(plane) + len(cols)) * length * width,
            transcendentals=0,
        ),
        name="compare_early",
    )(*plane, *cols)
    return outs[:-1], outs[-1]


def late_kernel(n_plane, n_early, n_cols, *refs):
    plane, refs = refs[:n_plane], refs[n_plane:]
    cols, refs = refs[:n_cols], refs[n_cols:]
    earlier, rows_early, refs = refs[:n_early], refs[n_early], refs[n_early + 1 :]
    here, partner_out, rows_out = refs[:-2], refs[-2], refs[-1]
    rows = rows_out.shape[2]
    chip = lax.axis_index("blk") // 2
    best = [ref[...] for ref in earlier]
    best += [jnp.full((1, rows), -1.0, jnp.float32)] * (n_cols - n_early)
    late = list(enumerate(cols))[n_early:]
    for k, ref in enumerate(plane):
        got = score_block(ref, late, best, False)
        rows_out[chip ^ k] = jnp.maximum(rows_early[chip ^ k], got)
    for ref, value in zip(here, [best[0]] + best[2:n_early]):
        ref[...] = value
    for at, value in enumerate([best[1]] + best[n_early:]):
        partner_out[at] = value


def compare_late(plane, cols, earlier, rows_best):
    length, width = plane[0].shape
    rows = length - TAIL
    n_early = len(earlier)
    n_here = n_early - 1
    n_partner = len(cols) - n_here
    pairs = len(plane) * (len(cols) - n_early)
    outs = pl.pallas_call(
        functools.partial(late_kernel, len(plane), n_early, len(cols)),
        out_shape=[jax.ShapeDtypeStruct((1, rows), jnp.float32)] * n_here
        + [
            jax.ShapeDtypeStruct((n_partner, 1, rows), jnp.float32),
            jax.ShapeDtypeStruct(rows_best.shape, jnp.float32),
        ],
        compiler_params=pltpu.CompilerParams(vmem_limit_bytes=VMEM),
        cost_estimate=pl.CostEstimate(
            flops=2 * pairs * rows * rows * width,
            bytes_accessed=2 * (len(plane) + len(cols)) * length * width,
            transcendentals=0,
        ),
        name="compare_late",
    )(*plane, *cols, *earlier, rows_best)
    return outs[:-2], outs[-2], outs[-1]


def join_kernel(n, *refs):
    got = refs[n]
    for at in range(n):
        refs[n + 1 + at][...] = jnp.maximum(refs[at][...], got[at])


def join(here, got):
    return pl.pallas_call(
        functools.partial(join_kernel, len(here)),
        out_shape=[jax.ShapeDtypeStruct(x.shape, x.dtype) for x in here],
        compiler_params=pltpu.CompilerParams(vmem_limit_bytes=VMEM_SMALL),
        name="join",
    )(*here, got)


def plane_shift(x, mask):
    size = lax.axis_size("blk")
    return lax.ppermute(x, "blk", [(i, i ^ mask) for i in range(size)])


def meetings(groups):
    perms = []
    for d in range(1, (groups + 1) // 2):
        perms.append(
            ([(z, (z - d) % groups) for z in range(groups)], [((z - d) % groups, z) for z in range(groups)])
        )
    if groups % 2 == 0:
        half = groups // 2
        there = [(z, z + half) if z % 2 == 0 else (z + half, z) for z in range(half)]
        perms.append((there, [(z, (z + half) % groups) for z in range(groups)]))
    return perms


def body(embeddings, target, cluster):
    groups = lax.axis_size("grp")
    per_group = lax.axis_size("blk")
    packed = pack(embeddings, target, cluster, per_group)
    perms = meetings(groups)
    fetched = [lax.ppermute(packed, "grp", there) for there, _ in perms]
    plane = [packed] + [plane_shift(packed, mask) for mask in range(2, per_group, 2)]
    fetched_too = [plane_shift(block, 1) for block in fetched]
    own_block = lax.optimization_barrier((packed, fetched[-1]))[0]
    cols = [packed, plane_shift(own_block, 1)] + fetched
    col_best, rows_best = compare_early(plane, cols)
    here, partner, rows_best = compare_late(plane, cols + fetched_too, col_best, rows_best)
    here = join(here, plane_shift(partner, 1))
    cores = [[i for i in range(per_group) if i % 2 == core] for core in range(2)]
    rows_back = lax.all_to_all(
        rows_best, "blk", split_axis=0, concat_axis=0, axis_index_groups=cores, tiled=True
    )
    found = [here[0]]
    for (_, back), best in zip(perms, here[1:]):
        found.append(lax.ppermute(best, "grp", back))
    found.append(jnp.max(rows_back, axis=0))
    return functools.reduce(jnp.maximum, found).reshape(-1)


def solution(mesh):
    return jax.shard_map(
        body,
        mesh=mesh,
        in_specs=(P(("grp", "blk"), None), P(("grp", "blk"), None), P(("grp", "blk"))),
        out_specs=P(("grp", "blk")),
        check_vma=False,
    )
```

```python
import functools

import jax
import jax.numpy as jnp
from jax import lax
from jax.experimental import pallas as pl
from jax.experimental.pallas import tpu as pltpu
from jax.sharding import PartitionSpec as P

CLUSTERS = 64
TAIL = 16
VMEM = 24 << 20
VMEM_SMALL = 8 << 20


def pack_kernel(per_group, emb_ref, target_ref, cluster_ref, out_ref):
    rows, width = emb_ref.shape
    x = emb_ref[...].astype(jnp.float32)
    scale = lax.rsqrt(jnp.sum(x * x, axis=1, keepdims=True) + 1e-06)
    out_ref[:rows, :] = (x * scale).astype(jnp.bfloat16)
    key = target_ref[...] // per_group * CLUSTERS + cluster_ref[...] + 1
    key = jnp.concatenate([key, jnp.zeros((1, width - rows), jnp.int32)], axis=1)
    key = jnp.broadcast_to(key.astype(jnp.float32), (TAIL, width))
    out_ref[rows:, :] = key.astype(jnp.bfloat16)


def pack(embeddings, target, cluster, per_group):
    rows, width = embeddings.shape
    return pl.pallas_call(
        functools.partial(pack_kernel, per_group),
        out_shape=jax.ShapeDtypeStruct((rows + TAIL, width), jnp.bfloat16),
        compiler_params=pltpu.CompilerParams(vmem_limit_bytes=VMEM_SMALL),
        name="pack",
    )(embeddings, target.reshape(1, rows), cluster.reshape(1, rows))


def keys_down(ref, rows):
    keys = ref[rows:, :rows].astype(jnp.float32)[:1]
    row_keys = jnp.transpose(jnp.broadcast_to(keys, (128, rows)))
    return jnp.concatenate([row_keys] * (rows // 128), axis=1)


def score_block(row_ref, cols, best, mine):
    rows = best[0].shape[1]
    row_keys = keys_down(row_ref, rows)
    row_best = None
    for at, col_ref in cols:
        scores = lax.dot_general(
            row_ref[:rows, :], col_ref[:rows, :], (((1,), (1,)), ((), ())), preferred_element_type=jnp.float32
        )
        allowed = row_keys == col_ref[rows:, :rows].astype(jnp.float32)[:1]
        if mine and at == 0:
            one = lax.broadcasted_iota(jnp.int32, scores.shape, 0)
            other = lax.broadcasted_iota(jnp.int32, scores.shape, 1)
            allowed = allowed & (one != other)
        masked = jnp.where(allowed, scores, -1.0)
        best[at] = jnp.maximum(best[at], jnp.max(masked, axis=0, keepdims=True))
        if at > 1:
            for lane in range(0, rows, 128):
                part = masked[:, lane : lane + 128]
                row_best = part if row_best is None else jnp.maximum(row_best, part)
    if row_best is None:
        return None
    return jnp.max(jnp.transpose(row_best), axis=0, keepdims=True)


def early_kernel(n_plane, n_cols, *refs):
    plane, cols = refs[:n_plane], refs[n_plane : n_plane + n_cols]
    outs = refs[n_plane + n_cols :]
    rows_out = outs[-1]
    rows = rows_out.shape[2]
    chip = lax.axis_index("blk") // 2
    best = [jnp.full((1, rows), -1.0, jnp.float32)] * n_cols
    for k, ref in enumerate(plane):
        rows_out[chip ^ k] = score_block(ref, list(enumerate(cols)), best, k == 0)
    for ref, value in zip(outs, best):
        ref[...] = value


def compare_early(plane, cols):
    length, width = plane[0].shape
    rows = length - TAIL
    outs = pl.pallas_call(
        functools.partial(early_kernel, len(plane), len(cols)),
        out_shape=[jax.ShapeDtypeStruct((1, rows), jnp.float32)] * len(cols)
        + [jax.ShapeDtypeStruct((len(plane), 1, rows), jnp.float32)],
        compiler_params=pltpu.CompilerParams(vmem_limit_bytes=VMEM),
        cost_estimate=pl.CostEstimate(
            flops=2 * len(plane) * len(cols) * rows * rows * width,
            bytes_accessed=2 * (len(plane) + len(cols)) * length * width,
            transcendentals=0,
        ),
        name="compare_early",
    )(*plane, *cols)
    return outs[:-1], outs[-1]


def late_kernel(n_plane, n_early, n_cols, *refs):
    plane, refs = refs[:n_plane], refs[n_plane:]
    cols, refs = refs[:n_cols], refs[n_cols:]
    earlier, rows_early, refs = refs[:n_early], refs[n_early], refs[n_early + 1 :]
    here, partner_out, rows_out = refs[:-2], refs[-2], refs[-1]
    rows = rows_out.shape[2]
    chip = lax.axis_index("blk") // 2
    best = [ref[...] for ref in earlier]
    best += [jnp.full((1, rows), -1.0, jnp.float32)] * (n_cols - n_early)
    late = list(enumerate(cols))[n_early:]
    for k, ref in enumerate(plane):
        got = score_block(ref, late, best, False)
        rows_out[chip ^ k] = jnp.maximum(rows_early[chip ^ k], got)
    for ref, value in zip(here, [best[0]] + best[2:n_early]):
        ref[...] = value
    for at, value in enumerate([best[1]] + best[n_early:]):
        partner_out[at] = value


def compare_late(plane, cols, earlier, rows_best):
    length, width = plane[0].shape
    rows = length - TAIL
    n_early = len(earlier)
    n_here = n_early - 1
    n_partner = len(cols) - n_here
    pairs = len(plane) * (len(cols) - n_early)
    outs = pl.pallas_call(
        functools.partial(late_kernel, len(plane), n_early, len(cols)),
        out_shape=[jax.ShapeDtypeStruct((1, rows), jnp.float32)] * n_here
        + [
            jax.ShapeDtypeStruct((n_partner, 1, rows), jnp.float32),
            jax.ShapeDtypeStruct(rows_best.shape, jnp.float32),
        ],
        compiler_params=pltpu.CompilerParams(vmem_limit_bytes=VMEM),
        cost_estimate=pl.CostEstimate(
            flops=2 * pairs * rows * rows * width,
            bytes_accessed=2 * (len(plane) + len(cols)) * length * width,
            transcendentals=0,
        ),
        name="compare_late",
    )(*plane, *cols, *earlier, rows_best)
    return outs[:-2], outs[-2], outs[-1]


def join_kernel(n, *refs):
    got = refs[n]
    for at in range(n):
        refs[n + 1 + at][...] = jnp.maximum(refs[at][...], got[at])


def join(here, got):
    return pl.pallas_call(
        functools.partial(join_kernel, len(here)),
        out_shape=[jax.ShapeDtypeStruct(x.shape, x.dtype) for x in here],
        compiler_params=pltpu.CompilerParams(vmem_limit_bytes=VMEM_SMALL),
        name="join",
    )(*here, got)


def plane_shift(x, mask):
    size = lax.axis_size("blk")
    return lax.ppermute(x, "blk", [(i, i ^ mask) for i in range(size)])


def meetings(groups):
    perms = []
    for d in range(1, (groups + 1) // 2):
        perms.append(
            ([(z, (z - d) % groups) for z in range(groups)], [((z - d) % groups, z) for z in range(groups)])
        )
    if groups % 2 == 0:
        half = groups // 2
        there = [(z, z + half) if z % 2 == 0 else (z + half, z) for z in range(half)]
        perms.append((there, [(z, (z + half) % groups) for z in range(groups)]))
    return perms


def body(embeddings, target, cluster):
    groups = lax.axis_size("grp")
    per_group = lax.axis_size("blk")
    packed = pack(embeddings, target, cluster, per_group)
    perms = meetings(groups)
    fetched = [lax.ppermute(packed, "grp", there) for there, _ in perms]
    plane = [packed] + [plane_shift(packed, mask) for mask in range(2, per_group, 2)]
    fetched_too = [plane_shift(block, 1) for block in fetched]
    own_block = lax.optimization_barrier((packed, plane[-1]))[0]
    cols = [packed, plane_shift(own_block, 1)] + fetched
    col_best, rows_best = compare_early(plane, cols)
    here, partner, rows_best = compare_late(plane, cols + fetched_too, col_best, rows_best)
    here = join(here, plane_shift(partner, 1))
    cores = [[i for i in range(per_group) if i % 2 == core] for core in range(2)]
    rows_back = lax.all_to_all(
        rows_best, "blk", split_axis=0, concat_axis=0, axis_index_groups=cores, tiled=True
    )
    found = [here[0]]
    for (_, back), best in zip(perms, here[1:]):
        found.append(lax.ppermute(best, "grp", back))
    found.append(jnp.max(rows_back, axis=0))
    return functools.reduce(jnp.maximum, found).reshape(-1)


def solution(mesh):
    return jax.shard_map(
        body,
        mesh=mesh,
        in_specs=(P(("grp", "blk"), None), P(("grp", "blk"), None), P(("grp", "blk"))),
        out_specs=P(("grp", "blk")),
        check_vma=False,
    )
```

```python
import functools

import jax
import jax.numpy as jnp
from jax import lax
from jax.experimental import pallas as pl
from jax.experimental.pallas import tpu as pltpu
from jax.sharding import PartitionSpec as P

CLUSTERS = 64
TAIL = 16
VMEM = 24 << 20
VMEM_SMALL = 8 << 20


def pack_kernel(per_group, emb_ref, target_ref, cluster_ref, out_ref):
    rows, width = emb_ref.shape
    x = emb_ref[...].astype(jnp.float32)
    scale = lax.rsqrt(jnp.sum(x * x, axis=1, keepdims=True) + 1e-06)
    out_ref[:rows, :] = (x * scale).astype(jnp.bfloat16)
    key = target_ref[...] // per_group * CLUSTERS + cluster_ref[...] + 1
    key = jnp.concatenate([key, jnp.zeros((1, width - rows), jnp.int32)], axis=1)
    key = jnp.broadcast_to(key.astype(jnp.float32), (TAIL, width))
    out_ref[rows:, :] = key.astype(jnp.bfloat16)


def pack(embeddings, target, cluster, per_group):
    rows, width = embeddings.shape
    return pl.pallas_call(
        functools.partial(pack_kernel, per_group),
        out_shape=jax.ShapeDtypeStruct((rows + TAIL, width), jnp.bfloat16),
        compiler_params=pltpu.CompilerParams(vmem_limit_bytes=VMEM_SMALL),
        name="pack",
    )(embeddings, target.reshape(1, rows), cluster.reshape(1, rows))


def whole(pieces):
    return pieces[0][...] if len(pieces) == 1 else jnp.concatenate([ref[...] for ref in pieces], axis=0)


def score_plane(plane, cols, best, rows_best, want_rows, diagonal):
    rows = best[0].shape[1]
    for k, pieces in enumerate(plane):
        block = whole(pieces)
        row_keys = jnp.transpose(jnp.broadcast_to(block[rows:, :rows].astype(jnp.float32)[:1], (128, rows)))
        row_keys = jnp.concatenate([row_keys] * (rows // 128), axis=1)
        row_best = None
        for at, col_ref in enumerate(cols):
            scores = lax.dot_general(
                block[:rows], col_ref[:rows, :], (((1,), (1,)), ((), ())), preferred_element_type=jnp.float32
            )
            allowed = row_keys == col_ref[rows:, :rows].astype(jnp.float32)[:1]
            if diagonal and k == 0 and at == 0:
                one = lax.broadcasted_iota(jnp.int32, scores.shape, 0)
                other = lax.broadcasted_iota(jnp.int32, scores.shape, 1)
                allowed = allowed & (one != other)
            masked = jnp.where(allowed, scores, -1.0)
            best[at] = jnp.maximum(best[at], jnp.max(masked, axis=0, keepdims=True))
            if at in want_rows:
                for lane in range(0, rows, 128):
                    part = masked[:, lane : lane + 128]
                    row_best = part if row_best is None else jnp.maximum(row_best, part)
        if row_best is not None:
            rows_best[k] = jnp.maximum(rows_best[k], jnp.max(jnp.transpose(row_best), axis=0, keepdims=True))


def take(refs, counts):
    groups = []
    for count in counts:
        groups.append(refs[:count])
        refs = refs[count:]
    return groups


def early_kernel(counts, n_cols, *refs):
    *plane, cols, here, (twins,), (rows_out,) = take(refs, counts + (n_cols, n_cols // 2, 1, 1))
    rows = rows_out.shape[2]
    low = jnp.full((1, rows), -1.0, jnp.float32)
    best, rows_best = [low] * n_cols, [low] * len(plane)
    score_plane(plane, cols, best, rows_best, range(2, n_cols), True)
    for at in range(n_cols // 2):
        here[at][...] = best[2 * at]
        twins[at] = best[2 * at + 1]
    for k, value in enumerate(rows_best):
        rows_out[k] = value


def last_kernel(counts, ordered, *refs):
    *plane, cols, (rows_in,), (col_out,), (rows_out,) = take(refs, counts + (1, 1, 1, 1))
    rows = rows_out.shape[2]
    best = [jnp.full((1, rows), -1.0, jnp.float32)]
    rows_best = [rows_in[k] for k in range(len(plane))]
    score_plane(plane, cols, best, rows_best, (0,), False)
    col_out[...] = best[0]
    chip = lax.axis_index("blk") // 2
    for k, value in enumerate(rows_best):
        rows_out[chip ^ k if ordered else k] = value


def call(kernel, name, plane, operands, outs, n_cols):
    rows = outs[0].shape[-1]
    width = plane[0][0].shape[1]
    return pl.pallas_call(
        kernel,
        out_shape=outs,
        compiler_params=pltpu.CompilerParams(vmem_limit_bytes=VMEM),
        cost_estimate=pl.CostEstimate(
            flops=2 * len(plane) * n_cols * rows * rows * width,
            bytes_accessed=2 * (len(plane) + n_cols) * rows * width,
            transcendentals=0,
        ),
        name=name,
    )(*[piece for pieces in plane for piece in pieces], *operands)


def compare_early(plane, cols):
    rows = cols[0].shape[0] - TAIL
    n = len(cols) // 2
    counts = tuple(len(pieces) for pieces in plane)
    outs = [jax.ShapeDtypeStruct((1, rows), jnp.float32)] * n
    outs += [jax.ShapeDtypeStruct((count, 1, rows), jnp.float32) for count in (n, len(plane))]
    outs = call(functools.partial(early_kernel, counts, len(cols)), "compare_early", plane, cols, outs, len(cols))
    return outs[:n], outs[n], outs[n + 1]


def compare_last(name, plane, col, rows_best, ordered):
    rows = col.shape[0] - TAIL
    counts = tuple(len(pieces) for pieces in plane)
    outs = [jax.ShapeDtypeStruct((1, rows), jnp.float32), jax.ShapeDtypeStruct(rows_best.shape, jnp.float32)]
    return call(functools.partial(last_kernel, counts, ordered), name, plane, [col, rows_best], outs, 1)


def join_kernel(n, *refs):
    got = refs[n]
    for at in range(n):
        refs[n + 1 + at][...] = jnp.maximum(refs[at][...], got[at])


def join(here, got):
    return pl.pallas_call(
        functools.partial(join_kernel, len(here)),
        out_shape=[jax.ShapeDtypeStruct(x.shape, x.dtype) for x in here],
        compiler_params=pltpu.CompilerParams(vmem_limit_bytes=VMEM_SMALL),
        name="join",
    )(*here, got)


def plane_shift(x, mask):
    size = lax.axis_size("blk")
    return lax.ppermute(x, "blk", [(i, i ^ mask) for i in range(size)])


def fetch_planes(packed, groups):
    block, fetched, back = packed, [], []
    for shift in range(1, groups // 2 + 1):
        takers = range(groups if 2 * shift < groups else shift)
        block = lax.ppermute(block, "grp", [((z + 1) % groups, z) for z in takers])
        fetched.append(block)
        back.append([(z, (z + shift) % groups) for z in range(groups)])
    return fetched, back


def fetch_plane(packed, per_group, first):
    half = (packed.shape[0] - TAIL) // 2
    plane = {0: (packed,)}
    halves = {}
    masks = range(2, per_group, 2)
    for mask in sorted(masks, key=lambda mask: mask.bit_count()):
        low, high = mask & -mask, 1 << (mask.bit_length() - 1)
        if low == high:
            block = plane_shift(packed, mask)
            plane[mask] = (block,)
            block = lax.optimization_barrier((block, first))[0]
            halves[mask] = (block[:half], block[half:])
        else:
            plane[mask] = halves[mask] = (
                plane_shift(halves[mask ^ low][0], low),
                plane_shift(halves[mask ^ high][1], high),
            )
    return [plane[mask] for mask in range(0, per_group, 2)]


def body(embeddings, target, cluster):
    groups = lax.axis_size("grp")
    per_group = lax.axis_size("blk")
    packed = pack(embeddings, target, cluster, per_group)
    fetched, back = fetch_planes(packed, groups)
    plane = fetch_plane(packed, per_group, fetched[0])
    own_block = lax.optimization_barrier((packed, fetched[0]))[0]
    cols = []
    for block in [own_block] + fetched[:-1]:
        cols += [block, plane_shift(block, 1)]
    cols[0] = packed
    here, twins, rows_best = compare_early(plane, cols)
    here = join(here, plane_shift(twins, 1))
    last, rows_best = compare_last("compare_last", plane, fetched[-1], rows_best, False)
    last_block = lax.optimization_barrier((fetched[-1], rows_best))[0]
    twin, rows_best = compare_last("compare_twin", plane, plane_shift(last_block, 1), rows_best, True)
    here += join([last], plane_shift(twin, 1).reshape(1, *twin.shape))
    cores = [[i for i in range(per_group) if i % 2 == core] for core in range(2)]
    rows_back = lax.all_to_all(
        rows_best, "blk", split_axis=0, concat_axis=0, axis_index_groups=cores, tiled=True
    )
    found = [here[0]]
    for way, best in zip(back, here[1:]):
        found.append(lax.ppermute(best, "grp", way))
    found.append(jnp.max(rows_back, axis=0))
    return functools.reduce(jnp.maximum, found).reshape(-1)


def solution(mesh):
    return jax.shard_map(
        body,
        mesh=mesh,
        in_specs=(P(("grp", "blk"), None), P(("grp", "blk"), None), P(("grp", "blk"))),
        out_specs=P(("grp", "blk")),
        check_vma=False,
    )
```

```python
import functools

import jax
import jax.numpy as jnp
from jax import lax
from jax.experimental import pallas as pl
from jax.experimental.pallas import tpu as pltpu
from jax.sharding import PartitionSpec as P

CLUSTERS = 64
TAIL = 16
VMEM = 24 << 20
VMEM_SMALL = 8 << 20


def pack_kernel(per_group, emb_ref, target_ref, cluster_ref, out_ref):
    rows, width = emb_ref.shape
    x = emb_ref[...].astype(jnp.float32)
    scale = lax.rsqrt(jnp.sum(x * x, axis=1, keepdims=True) + 1e-06)
    out_ref[:rows, :] = (x * scale).astype(jnp.bfloat16)
    key = target_ref[...] // per_group * CLUSTERS + cluster_ref[...] + 1
    key = jnp.concatenate([key, jnp.zeros((1, width - rows), jnp.int32)], axis=1)
    key = jnp.broadcast_to(key.astype(jnp.float32), (TAIL, width))
    out_ref[rows:, :] = key.astype(jnp.bfloat16)


def pack(embeddings, target, cluster, per_group):
    rows, width = embeddings.shape
    return pl.pallas_call(
        functools.partial(pack_kernel, per_group),
        out_shape=jax.ShapeDtypeStruct((rows + TAIL, width), jnp.bfloat16),
        compiler_params=pltpu.CompilerParams(vmem_limit_bytes=VMEM_SMALL),
        name="pack",
    )(embeddings, target.reshape(1, rows), cluster.reshape(1, rows))


def whole(pieces):
    return pieces[0][...] if len(pieces) == 1 else jnp.concatenate([ref[...] for ref in pieces], axis=0)


def score_block(pieces, cols, best, want_rows, diagonal):
    rows = best[0].shape[1]
    block = whole(pieces)
    row_keys = jnp.transpose(jnp.broadcast_to(block[rows:, :rows].astype(jnp.float32)[:1], (128, rows)))
    row_keys = jnp.concatenate([row_keys] * (rows // 128), axis=1)
    row_best = None
    for at, col_ref in enumerate(cols):
        scores = lax.dot_general(
            block[:rows], col_ref[:rows, :], (((1,), (1,)), ((), ())), preferred_element_type=jnp.float32
        )
        allowed = row_keys == col_ref[rows:, :rows].astype(jnp.float32)[:1]
        if at == diagonal:
            one = lax.broadcasted_iota(jnp.int32, scores.shape, 0)
            other = lax.broadcasted_iota(jnp.int32, scores.shape, 1)
            allowed = allowed & (one != other)
        masked = jnp.where(allowed, scores, -1.0)
        best[at] = jnp.maximum(best[at], jnp.max(masked, axis=0, keepdims=True))
        if at in want_rows:
            for lane in range(0, rows, 128):
                part = masked[:, lane : lane + 128]
                row_best = part if row_best is None else jnp.maximum(row_best, part)
    if row_best is None:
        return None
    return jnp.max(jnp.transpose(row_best), axis=0, keepdims=True)


def take(refs, counts):
    groups, at = [], 0
    for count in counts:
        groups.append(refs[at : at + count])
        at += count
    return groups


def first_kernel(counts, n_cols, *refs):
    *plane, cols, bests, (rows_out,) = take(refs, counts + (n_cols, n_cols, 1))
    best = [jnp.full((1, rows_out.shape[2]), -1.0, jnp.float32)] * n_cols
    for at, pieces in enumerate(plane):
        rows_out[at] = score_block(pieces, cols, best, range(2, n_cols), None if at else 0)
    for ref, value in zip(bests, best):
        ref[...] = value


def second_kernel(counts, masks, n_cols, *refs):
    n_here = n_cols // 2
    *plane, cols, earlier, (rows_in,), here, (twins,), (rows_out,) = take(
        refs, counts + (n_cols, n_cols, 1, n_here, 1, 1)
    )
    chip = lax.axis_index("blk") // 2
    best = [ref[...] for ref in earlier]
    n_first = rows_in.shape[0]
    for at in range(n_first):
        rows_out[chip ^ masks[at]] = rows_in[at]
    for at, pieces in enumerate(plane):
        rows_out[chip ^ masks[n_first + at]] = score_block(pieces, cols, best, range(2, n_cols), None)
    for at in range(n_here):
        here[at][...] = best[2 * at]
        twins[at] = best[2 * at + 1]


def last_kernel(counts, *refs):
    *plane, cols, (out_ref,) = take(refs, counts + (1, 1))
    best = [jnp.full(out_ref.shape, -1.0, jnp.float32)]
    for pieces in plane:
        score_block(pieces, cols, best, (), None)
    out_ref[...] = best[0]


def call(kernel, name, plane, operands, outs, n_cols):
    rows = outs[0].shape[-1]
    width = plane[0][0].shape[1]
    return pl.pallas_call(
        kernel,
        out_shape=outs,
        compiler_params=pltpu.CompilerParams(vmem_limit_bytes=VMEM),
        cost_estimate=pl.CostEstimate(
            flops=2 * len(plane) * n_cols * rows * rows * width,
            bytes_accessed=2 * (len(plane) + n_cols) * rows * width,
            transcendentals=0,
        ),
        name=name,
    )(*[piece for pieces in plane for piece in pieces], *operands)


def sizes(plane):
    return tuple(len(pieces) for pieces in plane)


def compare_first(plane, cols):
    rows = cols[0].shape[0] - TAIL
    outs = [jax.ShapeDtypeStruct((1, rows), jnp.float32)] * len(cols)
    outs += [jax.ShapeDtypeStruct((len(plane), 1, rows), jnp.float32)]
    kernel = functools.partial(first_kernel, sizes(plane), len(cols))
    *best, rows_best = call(kernel, "compare_first", plane, cols, outs, len(cols))
    return best, rows_best


def compare_second(plane, masks, cols, best, rows_best):
    rows = cols[0].shape[0] - TAIL
    n = len(cols) // 2
    outs = [jax.ShapeDtypeStruct((1, rows), jnp.float32)] * n
    outs += [jax.ShapeDtypeStruct((count, 1, rows), jnp.float32) for count in (n, len(masks))]
    kernel = functools.partial(second_kernel, sizes(plane), masks, len(cols))
    *here, twins, rows_best = call(kernel, "compare_second", plane, [*cols, *best, rows_best], outs, len(cols))
    return here, twins, rows_best


def compare_last(name, plane, col):
    outs = [jax.ShapeDtypeStruct((1, col.shape[0] - TAIL), jnp.float32)]
    return call(functools.partial(last_kernel, sizes(plane)), name, plane, [col], outs, 1)[0]


def join_kernel(n, *refs):
    got = refs[n]
    for at in range(n):
        refs[n + 1 + at][...] = jnp.maximum(refs[at][...], got[at])


def join(here, got):
    return pl.pallas_call(
        functools.partial(join_kernel, len(here)),
        out_shape=[jax.ShapeDtypeStruct(x.shape, x.dtype) for x in here],
        compiler_params=pltpu.CompilerParams(vmem_limit_bytes=VMEM_SMALL),
        name="join",
    )(*here, got)


def plane_shift(x, mask):
    size = lax.axis_size("blk")
    return lax.ppermute(x, "blk", [(i, i ^ mask) for i in range(size)])


def grp_shift(x, shift, mask=0):
    groups, size = lax.axis_size("grp"), lax.axis_size("blk")
    if not mask:
        return lax.ppermute(x, "grp", [(z, (z + shift) % groups) for z in range(groups)])
    pairs = [
        (z * size + i, (z + shift) % groups * size + (i ^ mask)) for z in range(groups) for i in range(size)
    ]
    return lax.ppermute(x, ("grp", "blk"), pairs)


def fetch_plane(packed, per_group):
    half = (packed.shape[0] - TAIL) // 2
    plane = {0: (packed,)}
    halves = {}
    for mask in sorted(range(2, per_group, 2), key=lambda mask: mask.bit_count()):
        low, high = mask & -mask, 1 << (mask.bit_length() - 1)
        if low == high:
            block = plane_shift(packed, mask)
            plane[mask] = (block,)
            halves[mask] = (block[:half], block[half:])
        else:
            plane[mask] = halves[mask] = (
                plane_shift(halves[mask ^ low][0], low),
                plane_shift(halves[mask ^ high][1], high),
            )
    return plane


def body(embeddings, target, cluster):
    groups = lax.axis_size("grp")
    per_group = lax.axis_size("blk")
    packed = pack(embeddings, target, cluster, per_group)
    fetched = [grp_shift(packed, -1)]
    plane = fetch_plane(packed, per_group)
    direct = [mask for mask, pieces in plane.items() if len(pieces) == 1]
    relayed = [mask for mask, pieces in plane.items() if len(pieces) > 1]
    own_block = lax.optimization_barrier((packed, fetched[0]))[0]
    own_twin = plane_shift(own_block, 1)
    while len(fetched) < groups // 2:
        block = lax.optimization_barrier((fetched[-1], own_twin, *[plane[mask] for mask in direct]))[0]
        fetched.append(grp_shift(block, -1))
    *fetched, last = fetched
    cols = [packed, own_twin]
    for block in fetched:
        cols += [block, plane_shift(block, 1)]
    best, rows_best = compare_first([plane[mask] for mask in direct], cols)
    masks = tuple(mask // 2 for mask in direct + relayed)
    here, twins, rows_best = compare_second([plane[mask] for mask in relayed], masks, cols, best, rows_best)
    here = join(here, plane_shift(twins, 1))
    cores = [[i for i in range(per_group) if i % 2 == core] for core in range(2)]
    rows_back = lax.all_to_all(
        rows_best, "blk", split_axis=0, concat_axis=0, axis_index_groups=cores, tiled=True
    )
    found = [here[0], jnp.max(rows_back, axis=0)]
    for shift, col_best in enumerate(here[1:], 1):
        found.append(grp_shift(col_best, shift))
    blocks = list(plane.values())
    last_then = lax.optimization_barrier((last, rows_best))[0]
    found.append(grp_shift(compare_last("compare_last", blocks, last), groups // 2))
    found.append(grp_shift(compare_last("compare_twin", blocks, plane_shift(last_then, 1)), groups // 2, 1))
    return functools.reduce(jnp.maximum, found).reshape(-1)


def solution(mesh):
    return jax.shard_map(
        body,
        mesh=mesh,
        in_specs=(P(("grp", "blk"), None), P(("grp", "blk"), None), P(("grp", "blk"))),
        out_specs=P(("grp", "blk")),
        check_vma=False,
    )
```

```python
import functools

import jax
import jax.numpy as jnp
from jax import lax
from jax.experimental import pallas as pl
from jax.experimental.pallas import tpu as pltpu
from jax.sharding import PartitionSpec as P

CLUSTERS = 64
TAIL = 16
VMEM = 24 << 20
VMEM_SMALL = 8 << 20


def pack_kernel(per_group, emb_ref, target_ref, cluster_ref, out_ref):
    rows, width = emb_ref.shape
    x = emb_ref[...].astype(jnp.float32)
    scale = lax.rsqrt(jnp.sum(x * x, axis=1, keepdims=True) + 1e-06)
    out_ref[:rows, :] = (x * scale).astype(jnp.bfloat16)
    key = target_ref[...] // per_group * CLUSTERS + cluster_ref[...] + 1
    key = jnp.concatenate([key, jnp.zeros((1, width - rows), jnp.int32)], axis=1)
    key = jnp.broadcast_to(key.astype(jnp.float32), (TAIL, width))
    out_ref[rows:, :] = key.astype(jnp.bfloat16)


def pack(embeddings, target, cluster, per_group):
    rows, width = embeddings.shape
    return pl.pallas_call(
        functools.partial(pack_kernel, per_group),
        out_shape=jax.ShapeDtypeStruct((rows + TAIL, width), jnp.bfloat16),
        compiler_params=pltpu.CompilerParams(vmem_limit_bytes=VMEM_SMALL),
        name="pack",
    )(embeddings, target.reshape(1, rows), cluster.reshape(1, rows))


def whole(pieces):
    return pieces[0][...] if len(pieces) == 1 else jnp.concatenate([ref[...] for ref in pieces], axis=0)


def score_kernel(counts, n_cols, pairs, want_rows, known, rows_known, outs, places, *refs):
    *plane, cols, cols_in, rows_in, col_outs, rows_outs = take(
        refs, counts + (n_cols, bool(known), bool(rows_known), len(outs), bool(want_rows))
    )
    rows = col_outs[0].shape[2]
    low = jnp.full((1, rows), -1.0, jnp.float32)
    best, rows_best = [low] * n_cols, [low] * len(plane)
    for at, col in enumerate(known):
        best[col] = cols_in[0][at]
    for at, k in enumerate(rows_known):
        rows_best[k] = rows_in[0][at]
    for k, pieces in enumerate(plane):
        mine = [at for one, at, _ in pairs if one == k]
        if not mine:
            continue
        diagonal = [at for one, at, same in pairs if one == k and same]
        block = whole(pieces)
        row_keys = jnp.transpose(jnp.broadcast_to(block[rows:, :rows].astype(jnp.float32)[:1], (128, rows)))
        row_keys = jnp.concatenate([row_keys] * (rows // 128), axis=1)
        row_best = None
        for at in mine:
            scores = lax.dot_general(
                block[:rows], cols[at][:rows, :], (((1,), (1,)), ((), ())), preferred_element_type=jnp.float32
            )
            allowed = row_keys == cols[at][rows:, :rows].astype(jnp.float32)[:1]
            if at in diagonal:
                one = lax.broadcasted_iota(jnp.int32, scores.shape, 0)
                other = lax.broadcasted_iota(jnp.int32, scores.shape, 1)
                allowed = allowed & (one != other)
            masked = jnp.where(allowed, scores, -1.0)
            best[at] = jnp.maximum(best[at], jnp.max(masked, axis=0, keepdims=True))
            if at in want_rows:
                for lane in range(0, rows, 128):
                    part = masked[:, lane : lane + 128]
                    row_best = part if row_best is None else jnp.maximum(row_best, part)
        if row_best is not None:
            got = jnp.max(jnp.transpose(row_best), axis=0, keepdims=True)
            rows_best[k] = jnp.maximum(rows_best[k], got)
    for ref, held in zip(col_outs, outs):
        for at, col in enumerate(held):
            ref[at] = best[col]
    if want_rows:
        chip = lax.axis_index("blk") // 2 if places else 0
        for k, value in enumerate(rows_best):
            rows_outs[0][chip ^ places[k] if places else k] = value


def take(refs, counts):
    groups, at = [], 0
    for count in counts:
        groups.append(refs[at : at + count])
        at += count
    return groups


def score(name, plane, cols, pairs, want_rows, outs, known=(), cols_in=(), rows_known=(), rows_in=(), places=None):
    length, width = cols[0].shape
    rows = length - TAIL
    kernel = functools.partial(
        score_kernel,
        tuple(len(pieces) for pieces in plane),
        len(cols),
        tuple(pairs),
        tuple(want_rows),
        tuple(known),
        tuple(rows_known),
        tuple(outs),
        places,
    )
    shapes = [len(held) for held in outs] + ([len(plane)] if want_rows else [])
    return pl.pallas_call(
        kernel,
        out_shape=[jax.ShapeDtypeStruct((count, 1, rows), jnp.float32) for count in shapes],
        compiler_params=pltpu.CompilerParams(vmem_limit_bytes=VMEM),
        cost_estimate=pl.CostEstimate(
            flops=2 * len(pairs) * rows * rows * width,
            bytes_accessed=2 * (len(plane) + len(cols)) * length * width,
            transcendentals=0,
        ),
        name=name,
    )(*[piece for pieces in plane for piece in pieces], *cols, *cols_in, *rows_in)


def join_kernel(n, *refs):
    for at in range(n):
        refs[n + 1 + at][...] = jnp.maximum(refs[at][...], refs[n][at])


def join(here, got):
    return pl.pallas_call(
        functools.partial(join_kernel, len(here)),
        out_shape=[jax.ShapeDtypeStruct((1, x.shape[-1]), x.dtype) for x in here],
        compiler_params=pltpu.CompilerParams(vmem_limit_bytes=VMEM_SMALL),
        name="join",
    )(*[x.reshape(1, -1) for x in here], got)


def plane_shift(x, mask):
    size = lax.axis_size("blk")
    return lax.ppermute(x, "blk", [(i, i ^ mask) for i in range(size)])


def grp_shift(x, shift, mask=0):
    groups, size = lax.axis_size("grp"), lax.axis_size("blk")
    if not mask:
        return lax.ppermute(x, "grp", [(z, (z + shift) % groups) for z in range(groups)])
    pairs = [
        (z * size + i, (z + shift) % groups * size + (i ^ mask)) for z in range(groups) for i in range(size)
    ]
    return lax.ppermute(x, ("grp", "blk"), pairs)


def relay_half_way(x):
    groups = lax.axis_size("grp")
    return lax.ppermute(x, "grp", [((z + 1) % groups, z) for z in range(groups // 2)])


def fetch_plane(packed, per_group, first):
    half = (packed.shape[0] - TAIL) // 2
    plane = {0: (packed,)}
    halves = {}
    masks = range(2, per_group, 2)
    for mask in sorted(masks, key=lambda mask: mask.bit_count()):
        low, high = mask & -mask, 1 << (mask.bit_length() - 1)
        if low == high:
            block = plane_shift(packed, mask)
            plane[mask] = (block,)
            block = lax.optimization_barrier((block, first))[0]
            halves[mask] = (block[:half], block[half:])
        else:
            plane[mask] = halves[mask] = (
                plane_shift(halves[mask ^ low][0], low),
                plane_shift(halves[mask ^ high][1], high),
            )
    return plane


def body(embeddings, target, cluster):
    groups = lax.axis_size("grp")
    per_group = lax.axis_size("blk")
    packed = pack(embeddings, target, cluster, per_group)
    next_one = grp_shift(packed, -1)
    half_way = relay_half_way(next_one)
    blocks = fetch_plane(packed, per_group, next_one)
    plane = list(blocks.values())
    n_direct = sum(len(pieces) == 1 for pieces in plane)
    places = tuple(mask // 2 for mask in blocks)
    every = range(len(plane))

    own_then = lax.optimization_barrier((packed, next_one))[0]
    cols = [packed, plane_shift(own_then, 1), next_one, plane_shift(next_one, 1)]
    pairs = [(k, at, k == at == 0) for k in every for at in range(4)]
    early = [pair for pair in pairs if pair[0] < n_direct]
    best, rows_best = score("compare_direct", plane[:n_direct], cols, early, (2, 3), [(0, 1, 2, 3)])
    own, next_best, twins, rows_best = score(
        "compare_relayed",
        plane,
        cols,
        [pair for pair in pairs if pair not in early],
        (2, 3),
        [(0,), (2,), (1, 3)],
        known=range(4),
        cols_in=[best],
        rows_known=range(n_direct),
        rows_in=[rows_best],
    )
    own, next_best = join([own, next_best], plane_shift(twins, 1))
    found = [own, grp_shift(next_best, 1)]

    half_then = lax.optimization_barrier((half_way, own))[0]
    for name, block, mask, order in (
        ("compare_half_way", half_way, 0, None),
        ("compare_twin", plane_shift(half_then, 1), 1, places),
    ):
        half_best, rows_best = score(
            name,
            plane,
            [block],
            [(k, 0, False) for k in every],
            (0,),
            [(0,)],
            rows_known=every,
            rows_in=[rows_best],
            places=order,
        )
        found.append(grp_shift(half_best.reshape(1, -1), groups // 2, mask))
    cores = [[i for i in range(per_group) if i % 2 == core] for core in range(2)]
    rows_back = lax.all_to_all(
        rows_best, "blk", split_axis=0, concat_axis=0, axis_index_groups=cores, tiled=True
    )
    found.append(jnp.max(rows_back, axis=0))
    return functools.reduce(jnp.maximum, found).reshape(-1)


def solution(mesh):
    return jax.shard_map(
        body,
        mesh=mesh,
        in_specs=(P(("grp", "blk"), None), P(("grp", "blk"), None), P(("grp", "blk"))),
        out_specs=P(("grp", "blk")),
        check_vma=False,
    )
```

```python
import functools

import jax
import jax.numpy as jnp
from jax import lax
from jax.experimental import pallas as pl
from jax.experimental.pallas import tpu as pltpu
from jax.sharding import PartitionSpec as P

CLUSTERS = 64
TAIL = 16
VMEM = 24 << 20
VMEM_SMALL = 8 << 20


def pack_kernel(per_group, emb_ref, target_ref, cluster_ref, out_ref):
    rows, width = emb_ref.shape
    x = emb_ref[...].astype(jnp.float32)
    scale = lax.rsqrt(jnp.sum(x * x, axis=1, keepdims=True) + 1e-06)
    out_ref[:rows, :] = (x * scale).astype(jnp.bfloat16)
    key = target_ref[...] // per_group * CLUSTERS + cluster_ref[...] + 1
    key = jnp.concatenate([key, jnp.zeros((1, width - rows), jnp.int32)], axis=1)
    key = jnp.broadcast_to(key.astype(jnp.float32), (TAIL, width))
    out_ref[rows:, :] = key.astype(jnp.bfloat16)


def pack(embeddings, target, cluster, per_group):
    rows, width = embeddings.shape
    return pl.pallas_call(
        functools.partial(pack_kernel, per_group),
        out_shape=jax.ShapeDtypeStruct((rows + TAIL, width), jnp.bfloat16),
        compiler_params=pltpu.CompilerParams(vmem_limit_bytes=VMEM_SMALL),
        name="pack",
    )(embeddings, target.reshape(1, rows), cluster.reshape(1, rows))


def whole(pieces):
    return pieces[0][...] if len(pieces) == 1 else jnp.concatenate([ref[...] for ref in pieces], axis=0)


def score_kernel(counts, n_cols, pairs, want_rows, known, rows_known, outs, places, *refs):
    *plane, cols, cols_in, rows_in, col_outs, rows_outs = take(
        refs, counts + (n_cols, bool(known), bool(rows_known), len(outs), 2 if places else 1)
    )
    rows = col_outs[0].shape[2]
    low = jnp.full((1, rows), -1.0, jnp.float32)
    best, rows_best = [low] * n_cols, [low] * len(plane)
    for at, col in enumerate(known):
        best[col] = cols_in[0][at]
    for at, k in enumerate(rows_known):
        rows_best[k] = rows_in[0][at]
    for k, pieces in enumerate(plane):
        mine = [at for one, at, _ in pairs if one == k]
        if not mine:
            continue
        diagonal = [at for one, at, same in pairs if one == k and same]
        block = whole(pieces)
        row_keys = jnp.transpose(jnp.broadcast_to(block[rows:, :rows].astype(jnp.float32)[:1], (128, rows)))
        row_keys = jnp.concatenate([row_keys] * (rows // 128), axis=1)
        row_best = None
        for at in mine:
            scores = lax.dot_general(
                block[:rows], cols[at][:rows, :], (((1,), (1,)), ((), ())), preferred_element_type=jnp.float32
            )
            allowed = row_keys == cols[at][rows:, :rows].astype(jnp.float32)[:1]
            if at in diagonal:
                one = lax.broadcasted_iota(jnp.int32, scores.shape, 0)
                other = lax.broadcasted_iota(jnp.int32, scores.shape, 1)
                allowed = allowed & (one != other)
            masked = jnp.where(allowed, scores, -1.0)
            best[at] = jnp.maximum(best[at], jnp.max(masked, axis=0, keepdims=True))
            if at in want_rows:
                for lane in range(0, rows, 128):
                    part = masked[:, lane : lane + 128]
                    row_best = part if row_best is None else jnp.maximum(row_best, part)
        if row_best is not None:
            got = jnp.max(jnp.transpose(row_best), axis=0, keepdims=True)
            rows_best[k] = jnp.maximum(rows_best[k], got)
    for ref, held in zip(col_outs, outs):
        for at, col in enumerate(held):
            ref[at] = best[col]
    for k, value in enumerate(rows_best):
        if places:
            rows_outs[places[k] % 2][places[k] // 2] = value
        else:
            rows_outs[0][k] = value


def take(refs, counts):
    groups, at = [], 0
    for count in counts:
        groups.append(refs[at : at + count])
        at += count
    return groups


def score(name, plane, cols, pairs, want_rows, outs, known=(), cols_in=(), rows_known=(), rows_in=(), places=None):
    length, width = cols[0].shape
    rows = length - TAIL
    kernel = functools.partial(
        score_kernel,
        tuple(len(pieces) for pieces in plane),
        len(cols),
        tuple(pairs),
        tuple(want_rows),
        tuple(known),
        tuple(rows_known),
        tuple(outs),
        places,
    )
    shapes = [len(held) for held in outs] + ([len(plane) // 2] * 2 if places else [len(plane)])
    return pl.pallas_call(
        kernel,
        out_shape=[jax.ShapeDtypeStruct((count, 1, rows), jnp.float32) for count in shapes],
        compiler_params=pltpu.CompilerParams(vmem_limit_bytes=VMEM),
        cost_estimate=pl.CostEstimate(
            flops=2 * len(pairs) * rows * rows * width,
            bytes_accessed=2 * (len(plane) + len(cols)) * length * width,
            transcendentals=0,
        ),
        name=name,
    )(*[piece for pieces in plane for piece in pieces], *cols, *cols_in, *rows_in)


def join_kernel(n, *refs):
    for at in range(n):
        refs[n + 1 + at][...] = jnp.maximum(refs[at][...], refs[n][at])


def join(here, got):
    return pl.pallas_call(
        functools.partial(join_kernel, len(here)),
        out_shape=[jax.ShapeDtypeStruct((1, x.shape[-1]), x.dtype) for x in here],
        compiler_params=pltpu.CompilerParams(vmem_limit_bytes=VMEM_SMALL),
        name="join",
    )(*[x.reshape(1, -1) for x in here], got)


def halve_kernel(keep_ref, got_ref, even_ref, odd_ref):
    for at in range(keep_ref.shape[0]):
        value = jnp.maximum(keep_ref[at], got_ref[at])
        (odd_ref if at % 2 else even_ref)[at // 2] = value


def halve(keep, got):
    half = jax.ShapeDtypeStruct((keep.shape[0] // 2, *keep.shape[1:]), keep.dtype)
    return pl.pallas_call(
        halve_kernel,
        out_shape=[half, half],
        compiler_params=pltpu.CompilerParams(vmem_limit_bytes=VMEM_SMALL),
        name="halve",
    )(keep, got)


def plane_shift(x, mask):
    size = lax.axis_size("blk")
    return lax.ppermute(x, "blk", [(i, i ^ mask) for i in range(size)])


def grp_shift(x, shift, mask=0):
    groups, size = lax.axis_size("grp"), lax.axis_size("blk")
    if not mask:
        return lax.ppermute(x, "grp", [(z, (z + shift) % groups) for z in range(groups)])
    pairs = [
        (z * size + i, (z + shift) % groups * size + (i ^ mask)) for z in range(groups) for i in range(size)
    ]
    return lax.ppermute(x, ("grp", "blk"), pairs)


def relay_half_way(x):
    groups = lax.axis_size("grp")
    return lax.ppermute(x, "grp", [((z + 1) % groups, z) for z in range(groups // 2)])


def fetch_plane(packed, per_group, first):
    half = (packed.shape[0] - TAIL) // 2
    plane = {0: (packed,)}
    halves = {}
    masks = range(2, per_group, 2)
    for mask in sorted(masks, key=lambda mask: mask.bit_count()):
        low, high = mask & -mask, 1 << (mask.bit_length() - 1)
        if low == high:
            block = plane_shift(packed, mask)
            plane[mask] = (block,)
            block = lax.optimization_barrier((block, first))[0]
            halves[mask] = (block[:half], block[half:])
        else:
            plane[mask] = halves[mask] = (
                plane_shift(halves[mask ^ low][0], low),
                plane_shift(halves[mask ^ high][1], high),
            )
    return plane


def body(embeddings, target, cluster):
    groups = lax.axis_size("grp")
    per_group = lax.axis_size("blk")
    packed = pack(embeddings, target, cluster, per_group)
    next_one = grp_shift(packed, -1)
    half_way = relay_half_way(next_one)
    blocks = fetch_plane(packed, per_group, next_one)
    plane = list(blocks.values())
    n_direct = sum(len(pieces) == 1 for pieces in plane)
    places = tuple(mask // 2 for mask in blocks)
    every = range(len(plane))

    own_then = lax.optimization_barrier((packed, next_one))[0]
    cols = [packed, plane_shift(own_then, 1), next_one, plane_shift(next_one, 1)]
    pairs = [(k, at, k == at == 0) for k in every for at in range(4)]
    early = [pair for pair in pairs if pair[0] < n_direct]
    best, rows_best = score("compare_direct", plane[:n_direct], cols, early, (2, 3), [(0, 1, 2, 3)])
    own, next_best, twins, rows_best = score(
        "compare_relayed",
        plane,
        cols,
        [pair for pair in pairs if pair not in early],
        (2, 3),
        [(0,), (2,), (1, 3)],
        known=range(4),
        cols_in=[best],
        rows_known=range(n_direct),
        rows_in=[rows_best],
    )
    own, next_best = join([own, next_best], plane_shift(twins, 1))
    found = [own, grp_shift(next_best, 1)]

    half_then = lax.optimization_barrier((half_way, own))[0]
    half_twin = plane_shift(half_then, 1)
    rest = dict(pairs=[(k, 0, False) for k in every], want_rows=(0,), outs=[(0,)], rows_known=every)
    half_best, rows_best = score("compare_half_way", plane, [half_way], rows_in=[rows_best], **rest)
    found.append(grp_shift(half_best.reshape(1, -1), groups // 2))
    half_twin = lax.optimization_barrier((half_twin, found[1]))[0]
    twin_best, even, odd = score("compare_twin", plane, [half_twin], rows_in=[rows_best], places=places, **rest)
    found.append(grp_shift(twin_best.reshape(1, -1), groups // 2, 1))

    odd = lax.optimization_barrier((odd, found[2]))[0]
    mask = 2
    while len(even) > 1:
        even, odd = halve(even, plane_shift(odd, mask))
        mask *= 2
    found += [even.reshape(1, -1), plane_shift(odd, mask).reshape(1, -1)]
    return functools.reduce(jnp.maximum, found).reshape(-1)


def solution(mesh):
    return jax.shard_map(
        body,
        mesh=mesh,
        in_specs=(P(("grp", "blk"), None), P(("grp", "blk"), None), P(("grp", "blk"))),
        out_specs=P(("grp", "blk")),
        check_vma=False,
    )
```

```python
import functools

import jax
import jax.numpy as jnp
from jax import lax
from jax.experimental import pallas as pl
from jax.experimental.pallas import tpu as pltpu
from jax.sharding import PartitionSpec as P

CLUSTERS = 64
TAIL = 16
VMEM = 24 << 20
VMEM_SMALL = 8 << 20


def pack_kernel(per_group, emb_ref, target_ref, cluster_ref, out_ref):
    rows, width = emb_ref.shape
    x = emb_ref[...].astype(jnp.float32)
    scale = lax.rsqrt(jnp.sum(x * x, axis=1, keepdims=True) + 1e-06)
    out_ref[:rows, :] = (x * scale).astype(jnp.bfloat16)
    key = target_ref[...] // per_group * CLUSTERS + cluster_ref[...] + 1
    key = jnp.concatenate([key, jnp.zeros((1, width - rows), jnp.int32)], axis=1)
    key = jnp.broadcast_to(key.astype(jnp.float32), (TAIL, width))
    out_ref[rows:, :] = key.astype(jnp.bfloat16)


def pack(embeddings, target, cluster, per_group):
    rows, width = embeddings.shape
    return pl.pallas_call(
        functools.partial(pack_kernel, per_group),
        out_shape=jax.ShapeDtypeStruct((rows + TAIL, width), jnp.bfloat16),
        compiler_params=pltpu.CompilerParams(vmem_limit_bytes=VMEM_SMALL),
        name="pack",
    )(embeddings, target.reshape(1, rows), cluster.reshape(1, rows))


def whole(pieces):
    return pieces[0][...] if len(pieces) == 1 else jnp.concatenate([ref[...] for ref in pieces], axis=0)


def score_block(pieces, cols, best, want_rows, diagonal):
    rows = best[0].shape[1]
    block = whole(pieces)
    row_keys = jnp.transpose(jnp.broadcast_to(block[rows:, :rows].astype(jnp.float32)[:1], (128, rows)))
    row_keys = jnp.concatenate([row_keys] * (rows // 128), axis=1)
    row_best = None
    for at, col_ref in enumerate(cols):
        scores = lax.dot_general(
            block[:rows], col_ref[:rows, :], (((1,), (1,)), ((), ())), preferred_element_type=jnp.float32
        )
        allowed = row_keys == col_ref[rows:, :rows].astype(jnp.float32)[:1]
        if at == diagonal:
            one = lax.broadcasted_iota(jnp.int32, scores.shape, 0)
            other = lax.broadcasted_iota(jnp.int32, scores.shape, 1)
            allowed = allowed & (one != other)
        masked = jnp.where(allowed, scores, -1.0)
        best[at] = jnp.maximum(best[at], jnp.max(masked, axis=0, keepdims=True))
        if at in want_rows:
            for lane in range(0, rows, 128):
                part = masked[:, lane : lane + 128]
                row_best = part if row_best is None else jnp.maximum(row_best, part)
    if row_best is None:
        return None
    return jnp.max(jnp.transpose(row_best), axis=0, keepdims=True)


def take(refs, counts):
    groups, at = [], 0
    for count in counts:
        groups.append(refs[at : at + count])
        at += count
    return groups


def first_kernel(counts, n_cols, *refs):
    *plane, cols, bests, (rows_out,) = take(refs, counts + (n_cols, n_cols, 1))
    best = [jnp.full((1, rows_out.shape[2]), -1.0, jnp.float32)] * n_cols
    for at, pieces in enumerate(plane):
        rows_out[at] = score_block(pieces, cols, best, range(2, n_cols), None if at else 0)
    for ref, value in zip(bests, best):
        ref[...] = value


def second_kernel(counts, masks, n_cols, *refs):
    n_here = n_cols // 2
    *plane, cols, earlier, (rows_in,), here, (twins,), (rows_out,) = take(
        refs, counts + (n_cols, n_cols, 1, n_here, 1, 1)
    )
    chip = lax.axis_index("blk") // 2
    best = [ref[...] for ref in earlier]
    n_first = rows_in.shape[0]
    for at in range(n_first):
        rows_out[chip ^ masks[at]] = rows_in[at]
    for at, pieces in enumerate(plane):
        rows_out[chip ^ masks[n_first + at]] = score_block(pieces, cols, best, range(2, n_cols), None)
    for at in range(n_here):
        here[at][...] = best[2 * at]
        twins[at] = best[2 * at + 1]


def last_kernel(counts, *refs):
    *plane, cols, (out_ref,) = take(refs, counts + (1, 1))
    best = [jnp.full(out_ref.shape, -1.0, jnp.float32)]
    for pieces in plane:
        score_block(pieces, cols, best, (), None)
    out_ref[...] = best[0]


def call(kernel, name, plane, operands, outs, n_cols):
    rows = outs[0].shape[-1]
    width = plane[0][0].shape[1]
    return pl.pallas_call(
        kernel,
        out_shape=outs,
        compiler_params=pltpu.CompilerParams(vmem_limit_bytes=VMEM),
        cost_estimate=pl.CostEstimate(
            flops=2 * len(plane) * n_cols * rows * rows * width,
            bytes_accessed=2 * (len(plane) + n_cols) * rows * width,
            transcendentals=0,
        ),
        name=name,
    )(*[piece for pieces in plane for piece in pieces], *operands)


def sizes(plane):
    return tuple(len(pieces) for pieces in plane)


def compare_first(plane, cols):
    rows = cols[0].shape[0] - TAIL
    outs = [jax.ShapeDtypeStruct((1, rows), jnp.float32)] * len(cols)
    outs += [jax.ShapeDtypeStruct((len(plane), 1, rows), jnp.float32)]
    kernel = functools.partial(first_kernel, sizes(plane), len(cols))
    *best, rows_best = call(kernel, "compare_first", plane, cols, outs, len(cols))
    return best, rows_best


def compare_second(plane, masks, cols, best, rows_best):
    rows = cols[0].shape[0] - TAIL
    n = len(cols) // 2
    outs = [jax.ShapeDtypeStruct((1, rows), jnp.float32)] * n
    outs += [jax.ShapeDtypeStruct((count, 1, rows), jnp.float32) for count in (n, len(masks))]
    kernel = functools.partial(second_kernel, sizes(plane), masks, len(cols))
    *here, twins, rows_best = call(kernel, "compare_second", plane, [*cols, *best, rows_best], outs, len(cols))
    return here, twins, rows_best


def compare_last(name, plane, col):
    outs = [jax.ShapeDtypeStruct((1, col.shape[0] - TAIL), jnp.float32)]
    return call(functools.partial(last_kernel, sizes(plane)), name, plane, [col], outs, 1)[0]


def join_kernel(n, *refs):
    got = refs[n]
    for at in range(n):
        refs[n + 1 + at][...] = jnp.maximum(refs[at][...], got[at])


def join(here, got):
    return pl.pallas_call(
        functools.partial(join_kernel, len(here)),
        out_shape=[jax.ShapeDtypeStruct(x.shape, x.dtype) for x in here],
        compiler_params=pltpu.CompilerParams(vmem_limit_bytes=VMEM_SMALL),
        name="join",
    )(*here, got)


def plane_shift(x, mask):
    size = lax.axis_size("blk")
    return lax.ppermute(x, "blk", [(i, i ^ mask) for i in range(size)])


def grp_shift(x, shift, mask=0):
    groups, size = lax.axis_size("grp"), lax.axis_size("blk")
    if not mask:
        return lax.ppermute(x, "grp", [(z, (z + shift) % groups) for z in range(groups)])
    pairs = [
        (z * size + i, (z + shift) % groups * size + (i ^ mask)) for z in range(groups) for i in range(size)
    ]
    return lax.ppermute(x, ("grp", "blk"), pairs)


def fetch_plane(packed, per_group):
    half = (packed.shape[0] - TAIL) // 2
    plane = {0: (packed,)}
    halves = {}
    for mask in sorted(range(2, per_group, 2), key=lambda mask: mask.bit_count()):
        low, high = mask & -mask, 1 << (mask.bit_length() - 1)
        if low == high:
            block = plane_shift(packed, mask)
            plane[mask] = (block,)
            halves[mask] = (block[:half], block[half:])
        else:
            plane[mask] = halves[mask] = (
                plane_shift(halves[mask ^ low][0], low),
                plane_shift(halves[mask ^ high][1], high),
            )
    return plane


def body(embeddings, target, cluster):
    groups = lax.axis_size("grp")
    per_group = lax.axis_size("blk")
    packed = pack(embeddings, target, cluster, per_group)
    fetched = [grp_shift(packed, -1)]
    plane = fetch_plane(packed, per_group)
    direct = [mask for mask, pieces in plane.items() if len(pieces) == 1]
    relayed = [mask for mask, pieces in plane.items() if len(pieces) > 1]
    own_block = lax.optimization_barrier((packed, fetched[0]))[0]
    own_twin = plane_shift(own_block, 1)
    while len(fetched) < groups // 2:
        fetched.append(grp_shift(fetched[-1], -1))
    *fetched, last = fetched
    cols = [packed, own_twin]
    for block in fetched:
        cols += [block, plane_shift(block, 1)]
    best, rows_best = compare_first([plane[mask] for mask in direct], cols)
    masks = tuple(mask // 2 for mask in direct + relayed)
    here, twins, rows_best = compare_second([plane[mask] for mask in relayed], masks, cols, best, rows_best)
    here = join(here, plane_shift(twins, 1))
    cores = [[i for i in range(per_group) if i % 2 == core] for core in range(2)]
    rows_back = lax.all_to_all(
        rows_best, "blk", split_axis=0, concat_axis=0, axis_index_groups=cores, tiled=True
    )
    found = [here[0], jnp.max(rows_back, axis=0)]
    for shift, col_best in enumerate(here[1:], 1):
        found.append(grp_shift(col_best, shift))
    blocks = list(plane.values())
    last_then = lax.optimization_barrier((last, rows_back, here[0]))[0]
    found.append(grp_shift(compare_last("compare_last", blocks, last), groups // 2))
    found.append(grp_shift(compare_last("compare_twin", blocks, plane_shift(last_then, 1)), groups // 2, 1))
    return functools.reduce(jnp.maximum, found).reshape(-1)


def solution(mesh):
    return jax.shard_map(
        body,
        mesh=mesh,
        in_specs=(P(("grp", "blk"), None), P(("grp", "blk"), None), P(("grp", "blk"))),
        out_specs=P(("grp", "blk")),
        check_vma=False,
    )
```

```python
import functools

import jax
import jax.numpy as jnp
from jax import lax
from jax.experimental import pallas as pl
from jax.experimental.pallas import tpu as pltpu
from jax.sharding import PartitionSpec as P

CLUSTERS = 64
TAIL = 16
VMEM = 24 << 20
VMEM_SMALL = 8 << 20


def pack_kernel(per_group, emb_ref, target_ref, cluster_ref, out_ref):
    rows, width = emb_ref.shape
    x = emb_ref[...].astype(jnp.float32)
    scale = lax.rsqrt(jnp.sum(x * x, axis=1, keepdims=True) + 1e-06)
    out_ref[:rows, :] = (x * scale).astype(jnp.bfloat16)
    key = target_ref[...] // per_group * CLUSTERS + cluster_ref[...] + 1
    key = jnp.concatenate([key, jnp.zeros((1, width - rows), jnp.int32)], axis=1)
    key = jnp.broadcast_to(key.astype(jnp.float32), (TAIL, width))
    out_ref[rows:, :] = key.astype(jnp.bfloat16)


def pack(embeddings, target, cluster, per_group):
    rows, width = embeddings.shape
    return pl.pallas_call(
        functools.partial(pack_kernel, per_group),
        out_shape=jax.ShapeDtypeStruct((rows + TAIL, width), jnp.bfloat16),
        compiler_params=pltpu.CompilerParams(vmem_limit_bytes=VMEM_SMALL),
        name="pack",
    )(embeddings, target.reshape(1, rows), cluster.reshape(1, rows))


def whole(pieces):
    return pieces[0][...] if len(pieces) == 1 else jnp.concatenate([ref[...] for ref in pieces], axis=0)


def score_kernel(counts, n_cols, pairs, want_rows, known, rows_known, outs, places, *refs):
    *plane, cols, cols_in, rows_in, col_outs, rows_outs = take(
        refs, counts + (n_cols, bool(known), bool(rows_known), len(outs), 2 if places else 1)
    )
    rows = col_outs[0].shape[2]
    low = jnp.full((1, rows), -1.0, jnp.float32)
    best, rows_best = [low] * n_cols, [low] * len(plane)
    for at, col in enumerate(known):
        best[col] = cols_in[0][at]
    for at, k in enumerate(rows_known):
        rows_best[k] = rows_in[0][at]
    for k, pieces in enumerate(plane):
        mine = [at for one, at, _ in pairs if one == k]
        if not mine:
            continue
        diagonal = [at for one, at, same in pairs if one == k and same]
        block = whole(pieces)
        row_keys = jnp.transpose(jnp.broadcast_to(block[rows:, :rows].astype(jnp.float32)[:1], (128, rows)))
        row_keys = jnp.concatenate([row_keys] * (rows // 128), axis=1)
        row_best = None
        for at in mine:
            scores = lax.dot_general(
                block[:rows], cols[at][:rows, :], (((1,), (1,)), ((), ())), preferred_element_type=jnp.float32
            )
            allowed = row_keys == cols[at][rows:, :rows].astype(jnp.float32)[:1]
            if at in diagonal:
                one = lax.broadcasted_iota(jnp.int32, scores.shape, 0)
                other = lax.broadcasted_iota(jnp.int32, scores.shape, 1)
                allowed = allowed & (one != other)
            masked = jnp.where(allowed, scores, -1.0)
            best[at] = jnp.maximum(best[at], jnp.max(masked, axis=0, keepdims=True))
            if at in want_rows:
                for lane in range(0, rows, 128):
                    part = masked[:, lane : lane + 128]
                    row_best = part if row_best is None else jnp.maximum(row_best, part)
        if row_best is not None:
            got = jnp.max(jnp.transpose(row_best), axis=0, keepdims=True)
            rows_best[k] = jnp.maximum(rows_best[k], got)
    for ref, held in zip(col_outs, outs):
        for at, col in enumerate(held):
            ref[at] = best[col]
    for k, value in enumerate(rows_best):
        if places:
            rows_outs[places[k] % 2][places[k] // 2] = value
        else:
            rows_outs[0][k] = value


def take(refs, counts):
    groups, at = [], 0
    for count in counts:
        groups.append(refs[at : at + count])
        at += count
    return groups


def score(name, plane, cols, pairs, want_rows, outs, known=(), cols_in=(), rows_known=(), rows_in=(), places=None):
    length, width = cols[0].shape
    rows = length - TAIL
    kernel = functools.partial(
        score_kernel,
        tuple(len(pieces) for pieces in plane),
        len(cols),
        tuple(pairs),
        tuple(want_rows),
        tuple(known),
        tuple(rows_known),
        tuple(outs),
        places,
    )
    shapes = [len(held) for held in outs] + ([len(plane) // 2] * 2 if places else [len(plane)])
    return pl.pallas_call(
        kernel,
        out_shape=[jax.ShapeDtypeStruct((count, 1, rows), jnp.float32) for count in shapes],
        compiler_params=pltpu.CompilerParams(vmem_limit_bytes=VMEM),
        cost_estimate=pl.CostEstimate(
            flops=2 * len(pairs) * rows * rows * width,
            bytes_accessed=2 * (len(plane) + len(cols)) * length * width,
            transcendentals=0,
        ),
        name=name,
    )(*[piece for pieces in plane for piece in pieces], *cols, *cols_in, *rows_in)


def join_kernel(n, *refs):
    for at in range(n):
        refs[n + 1 + at][...] = jnp.maximum(refs[at][...], refs[n][at])


def join(here, got):
    return pl.pallas_call(
        functools.partial(join_kernel, len(here)),
        out_shape=[jax.ShapeDtypeStruct((1, x.shape[-1]), x.dtype) for x in here],
        compiler_params=pltpu.CompilerParams(vmem_limit_bytes=VMEM_SMALL),
        name="join",
    )(*[x.reshape(1, -1) for x in here], got)


def halve_kernel(keep_ref, got_ref, even_ref, odd_ref):
    for at in range(keep_ref.shape[0]):
        value = jnp.maximum(keep_ref[at], got_ref[at])
        (odd_ref if at % 2 else even_ref)[at // 2] = value


def halve(keep, got):
    half = jax.ShapeDtypeStruct((keep.shape[0] // 2, *keep.shape[1:]), keep.dtype)
    return pl.pallas_call(
        halve_kernel,
        out_shape=[half, half],
        compiler_params=pltpu.CompilerParams(vmem_limit_bytes=VMEM_SMALL),
        name="halve",
    )(keep, got)


def plane_shift(x, mask):
    size = lax.axis_size("blk")
    return lax.ppermute(x, "blk", [(i, i ^ mask) for i in range(size)])


def grp_shift(x, shift, mask=0):
    groups, size = lax.axis_size("grp"), lax.axis_size("blk")
    if not mask:
        return lax.ppermute(x, "grp", [(z, (z + shift) % groups) for z in range(groups)])
    pairs = [
        (z * size + i, (z + shift) % groups * size + (i ^ mask)) for z in range(groups) for i in range(size)
    ]
    return lax.ppermute(x, ("grp", "blk"), pairs)


def relay_half_way(x):
    groups = lax.axis_size("grp")
    return lax.ppermute(x, "grp", [(z - 1, z) for z in range(groups // 2, groups)])


def fetch_plane(packed, per_group, first):
    half = (packed.shape[0] - TAIL) // 2
    plane = {0: (packed,)}
    halves = {}
    masks = range(2, per_group, 2)
    for mask in sorted(masks, key=lambda mask: mask.bit_count()):
        low, high = mask & -mask, 1 << (mask.bit_length() - 1)
        if low == high:
            block = plane_shift(packed, mask)
            plane[mask] = (block,)
            block = lax.optimization_barrier((block, first))[0]
            halves[mask] = (block[:half], block[half:])
        else:
            plane[mask] = halves[mask] = (
                plane_shift(halves[mask ^ low][0], low),
                plane_shift(halves[mask ^ high][1], high),
            )
    return plane


def body(embeddings, target, cluster):
    groups = lax.axis_size("grp")
    per_group = lax.axis_size("blk")
    packed = pack(embeddings, target, cluster, per_group)
    one_off = grp_shift(packed, 1)
    half_way = relay_half_way(one_off)
    blocks = fetch_plane(packed, per_group, one_off)
    plane = list(blocks.values())
    n_direct = sum(len(pieces) == 1 for pieces in plane)
    places = tuple(mask // 2 for mask in blocks)
    every = range(len(plane))

    own_then = lax.optimization_barrier((packed, one_off))[0]
    cols = [packed, plane_shift(own_then, 1), one_off, plane_shift(one_off, 1)]
    pairs = [(k, at, k == at == 0) for k in every for at in range(4)]
    early = [pair for pair in pairs if pair[0] < n_direct]
    best, rows_best = score("compare_direct", plane[:n_direct], cols, early, (2, 3), [(0, 1, 2, 3)])
    own, one_off_best, twins, rows_best = score(
        "compare_relayed",
        plane,
        cols,
        [pair for pair in pairs if pair not in early],
        (2, 3),
        [(0,), (2,), (1, 3)],
        known=range(4),
        cols_in=[best],
        rows_known=range(n_direct),
        rows_in=[rows_best],
    )
    own, one_off_best = join([own, one_off_best], plane_shift(twins, 1))
    found = [own, grp_shift(one_off_best, -1)]

    half_then = lax.optimization_barrier((half_way, own))[0]
    half_twin = plane_shift(half_then, 1)
    rest = dict(pairs=[(k, 0, False) for k in every], want_rows=(0,), outs=[(0,)], rows_known=every)
    half_best, rows_best = score("compare_half_way", plane, [half_way], rows_in=[rows_best], **rest)
    found.append(grp_shift(half_best.reshape(1, -1), groups // 2))
    twin_best, even, odd = score("compare_twin", plane, [half_twin], rows_in=[rows_best], places=places, **rest)
    found.append(grp_shift(twin_best.reshape(1, -1), groups // 2, 1))

    mask = 2
    while len(even) > 1:
        even, odd = halve(even, plane_shift(odd, mask))
        mask *= 2
    found += [even.reshape(1, -1), plane_shift(odd, mask).reshape(1, -1)]
    return functools.reduce(jnp.maximum, found).reshape(-1)


def solution(mesh):
    return jax.shard_map(
        body,
        mesh=mesh,
        in_specs=(P(("grp", "blk"), None), P(("grp", "blk"), None), P(("grp", "blk"))),
        out_specs=P(("grp", "blk")),
        check_vma=False,
    )
```

```python
import functools

import jax
import jax.numpy as jnp
from jax import lax
from jax.experimental import pallas as pl
from jax.experimental.pallas import tpu as pltpu
from jax.sharding import PartitionSpec as P

CLUSTERS = 64
TAIL = 16
VMEM = 24 << 20
VMEM_SMALL = 8 << 20


def pack_kernel(per_group, emb_ref, target_ref, cluster_ref, out_ref):
    rows, width = emb_ref.shape
    x = emb_ref[...].astype(jnp.float32)
    scale = lax.rsqrt(jnp.sum(x * x, axis=1, keepdims=True) + 1e-06)
    out_ref[:rows, :] = (x * scale).astype(jnp.bfloat16)
    key = target_ref[...] // per_group * CLUSTERS + cluster_ref[...] + 1
    key = jnp.concatenate([key, jnp.zeros((1, width - rows), jnp.int32)], axis=1)
    key = jnp.broadcast_to(key.astype(jnp.float32), (TAIL, width))
    out_ref[rows:, :] = key.astype(jnp.bfloat16)


def pack(embeddings, target, cluster, per_group):
    rows, width = embeddings.shape
    return pl.pallas_call(
        functools.partial(pack_kernel, per_group),
        out_shape=jax.ShapeDtypeStruct((rows + TAIL, width), jnp.bfloat16),
        compiler_params=pltpu.CompilerParams(vmem_limit_bytes=VMEM_SMALL),
        name="pack",
    )(embeddings, target.reshape(1, rows), cluster.reshape(1, rows))


def whole(pieces):
    return pieces[0][...] if len(pieces) == 1 else jnp.concatenate([ref[...] for ref in pieces], axis=0)


def score_kernel(counts, n_cols, pairs, want_rows, known, outs, *refs):
    n_rows = len(counts) if want_rows else 0
    *plane, cols, cols_in, col_outs, row_outs = take(refs, counts + (n_cols, bool(known), len(outs), n_rows))
    rows = col_outs[0].shape[2]
    best = [jnp.full((1, rows), -1.0, jnp.float32)] * n_cols
    for at, col in enumerate(known):
        best[col] = cols_in[0][at]
    for k, pieces in enumerate(plane):
        block = whole(pieces)
        row_keys = jnp.transpose(jnp.broadcast_to(block[rows:, :rows].astype(jnp.float32)[:1], (128, rows)))
        row_keys = jnp.concatenate([row_keys] * (rows // 128), axis=1)
        row_best = None
        for at, same in [(at, same) for one, at, same in pairs if one == k]:
            scores = lax.dot_general(
                block[:rows], cols[at][:rows, :], (((1,), (1,)), ((), ())), preferred_element_type=jnp.float32
            )
            allowed = row_keys == cols[at][rows:, :rows].astype(jnp.float32)[:1]
            if same:
                one = lax.broadcasted_iota(jnp.int32, scores.shape, 0)
                other = lax.broadcasted_iota(jnp.int32, scores.shape, 1)
                allowed = allowed & (one != other)
            masked = jnp.where(allowed, scores, -1.0)
            best[at] = jnp.maximum(best[at], jnp.max(masked, axis=0, keepdims=True))
            if at in want_rows:
                for lane in range(0, rows, 128):
                    part = masked[:, lane : lane + 128]
                    row_best = part if row_best is None else jnp.maximum(row_best, part)
        if row_best is not None:
            row_outs[k][0] = jnp.max(jnp.transpose(row_best), axis=0, keepdims=True)
    for ref, held in zip(col_outs, outs):
        for at, col in enumerate(held):
            ref[at] = best[col]


def take(refs, counts):
    groups, at = [], 0
    for count in counts:
        groups.append(refs[at : at + count])
        at += count
    return groups


def score(name, plane, cols, pairs, want_rows, outs, known=(), cols_in=()):
    length, width = cols[0].shape
    rows = length - TAIL
    counts = tuple(len(pieces) for pieces in plane)
    kernel = functools.partial(
        score_kernel, counts, len(cols), tuple(pairs), tuple(want_rows), tuple(known), tuple(outs)
    )
    shapes = [len(held) for held in outs] + [1] * (len(plane) if want_rows else 0)
    return pl.pallas_call(
        kernel,
        out_shape=[jax.ShapeDtypeStruct((count, 1, rows), jnp.float32) for count in shapes],
        compiler_params=pltpu.CompilerParams(vmem_limit_bytes=VMEM),
        cost_estimate=pl.CostEstimate(
            flops=2 * len(pairs) * rows * rows * width,
            bytes_accessed=2 * (len(plane) + len(cols)) * length * width,
            transcendentals=0,
        ),
        name=name,
    )(*[piece for pieces in plane for piece in pieces], *cols, *cols_in)


def join_kernel(n, *refs):
    for at in range(n):
        refs[n + 1 + at][...] = jnp.maximum(refs[at][...], refs[n][at])


def join(here, got):
    return pl.pallas_call(
        functools.partial(join_kernel, len(here)),
        out_shape=[jax.ShapeDtypeStruct((1, x.shape[-1]), x.dtype) for x in here],
        compiler_params=pltpu.CompilerParams(vmem_limit_bytes=VMEM_SMALL),
        name="join",
    )(*[x.reshape(1, -1) for x in here], got)


def plane_shift(x, mask):
    size = lax.axis_size("blk")
    return lax.ppermute(x, "blk", [(i, i ^ mask) for i in range(size)])


def grp_shift(x, shift, mask=0):
    groups, size = lax.axis_size("grp"), lax.axis_size("blk")
    if not mask:
        return lax.ppermute(x, "grp", [(z, (z + shift) % groups) for z in range(groups)])
    pairs = [
        (z * size + i, (z + shift) % groups * size + (i ^ mask)) for z in range(groups) for i in range(size)
    ]
    return lax.ppermute(x, ("grp", "blk"), pairs)


def fetch_plane(packed, per_group):
    half = (packed.shape[0] - TAIL) // 2
    plane = {0: (packed,)}
    halves = {}
    for mask in sorted(range(2, per_group, 2), key=lambda mask: mask.bit_count()):
        low, high = mask & -mask, 1 << (mask.bit_length() - 1)
        if low == high:
            block = plane_shift(packed, mask)
            plane[mask] = (block,)
            halves[mask] = (block[:half], block[half:])
        else:
            plane[mask] = halves[mask] = (
                plane_shift(halves[mask ^ low][0], low),
                plane_shift(halves[mask ^ high][1], high),
            )
    return plane


def body(embeddings, target, cluster):
    groups = lax.axis_size("grp")
    per_group = lax.axis_size("blk")
    packed = pack(embeddings, target, cluster, per_group)
    one_off = grp_shift(packed, 1)
    plane = fetch_plane(packed, per_group)
    own_then = lax.optimization_barrier((packed, one_off))[0]
    own_twin = plane_shift(own_then, 1)
    half_way = grp_shift(one_off, 1)
    direct = [mask for mask, pieces in plane.items() if len(pieces) == 1]
    relayed = [mask for mask, pieces in plane.items() if len(pieces) > 1]

    cols = [packed, own_twin, one_off, plane_shift(one_off, 1)]
    every = range(len(cols))
    best, *rows_direct = score(
        "compare_direct",
        [plane[mask] for mask in direct],
        cols,
        [(k, at, k == at == 0) for k in range(len(direct)) for at in every],
        (2, 3),
        [tuple(every)],
    )
    early = [plane_shift(best, mask) for best, mask in zip(rows_direct[1:], direct[1:])]
    best = lax.optimization_barrier((best, early[0]))[0]
    own, one_off_best, twins, *rows_relayed = score(
        "compare_relayed",
        [plane[mask] for mask in relayed],
        cols,
        [(k, at, False) for k in range(len(relayed)) for at in every],
        (2, 3),
        [(0,), (2,), (1, 3)],
        known=every,
        cols_in=[best],
    )
    own, one_off_best = join([own, one_off_best], plane_shift(twins, 1))
    found = [own.reshape(1, 1, -1), rows_direct[0]]
    early += [plane_shift(best, mask) for best, mask in zip(rows_relayed, relayed)]
    found.append(grp_shift(one_off_best.reshape(1, 1, -1), -1))

    blocks = list(plane.values())
    pairs = [(k, 0, False) for k in range(len(blocks))]
    half_then = lax.optimization_barrier((half_way, own, early))[0]
    for name, block, mask in (("compare_half_way", half_way, 0), ("compare_twin", plane_shift(half_then, 1), 1)):
        (half_best,) = score(name, blocks, [block], pairs, (), [(0,)])
        found.append(grp_shift(half_best, groups // 2, mask))
    return functools.reduce(jnp.maximum, found + early).reshape(-1)


def solution(mesh):
    return jax.shard_map(
        body,
        mesh=mesh,
        in_specs=(P(("grp", "blk"), None), P(("grp", "blk"), None), P(("grp", "blk"))),
        out_specs=P(("grp", "blk")),
        check_vma=False,
    )
```

```python
import functools

import jax
import jax.numpy as jnp
from jax import lax
from jax.experimental import pallas as pl
from jax.experimental.pallas import tpu as pltpu
from jax.sharding import PartitionSpec as P

CLUSTERS = 64
TAIL = 16
VMEM = 24 << 20
VMEM_SMALL = 8 << 20


def pack_kernel(per_group, emb_ref, target_ref, cluster_ref, out_ref):
    rows, width = emb_ref.shape
    x = emb_ref[...].astype(jnp.float32)
    scale = lax.rsqrt(jnp.sum(x * x, axis=1, keepdims=True) + 1e-06)
    out_ref[:rows, :] = (x * scale).astype(jnp.bfloat16)
    key = target_ref[...] // per_group * CLUSTERS + cluster_ref[...] + 1
    key = jnp.concatenate([key, jnp.zeros((1, width - rows), jnp.int32)], axis=1)
    key = jnp.broadcast_to(key.astype(jnp.float32), (TAIL, width))
    out_ref[rows:, :] = key.astype(jnp.bfloat16)


def pack(embeddings, target, cluster, per_group):
    rows, width = embeddings.shape
    return pl.pallas_call(
        functools.partial(pack_kernel, per_group),
        out_shape=jax.ShapeDtypeStruct((rows + TAIL, width), jnp.bfloat16),
        compiler_params=pltpu.CompilerParams(vmem_limit_bytes=VMEM_SMALL),
        name="pack",
    )(embeddings, target.reshape(1, rows), cluster.reshape(1, rows))


def whole(pieces):
    return pieces[0][...] if len(pieces) == 1 else jnp.concatenate([ref[...] for ref in pieces], axis=0)


def score_kernel(counts, n_cols, pairs, want_rows, known, n_rows_in, outs, row_outs, *refs):
    *plane, cols, cols_in, rows_in, col_refs, row_refs = take(
        refs, counts + (n_cols, bool(known), n_rows_in, len(outs), len(row_outs))
    )
    rows = col_refs[0].shape[2]
    best = [jnp.full((1, rows), -1.0, jnp.float32)] * n_cols
    rows_best = [ref[0] for ref in rows_in]
    for at, col in enumerate(known):
        best[col] = cols_in[0][at]
    for k, pieces in enumerate(plane):
        block = whole(pieces)
        row_keys = jnp.transpose(jnp.broadcast_to(block[rows:, :rows].astype(jnp.float32)[:1], (128, rows)))
        row_keys = jnp.concatenate([row_keys] * (rows // 128), axis=1)
        row_best = None
        for at, same in [(at, same) for one, at, same in pairs if one == k]:
            scores = lax.dot_general(
                block[:rows], cols[at][:rows, :], (((1,), (1,)), ((), ())), preferred_element_type=jnp.float32
            )
            allowed = row_keys == cols[at][rows:, :rows].astype(jnp.float32)[:1]
            if same:
                one = lax.broadcasted_iota(jnp.int32, scores.shape, 0)
                other = lax.broadcasted_iota(jnp.int32, scores.shape, 1)
                allowed = allowed & (one != other)
            masked = jnp.where(allowed, scores, -1.0)
            best[at] = jnp.maximum(best[at], jnp.max(masked, axis=0, keepdims=True))
            if at in want_rows:
                for lane in range(0, rows, 128):
                    part = masked[:, lane : lane + 128]
                    row_best = part if row_best is None else jnp.maximum(row_best, part)
        if row_best is not None:
            rows_best.append(jnp.max(jnp.transpose(row_best), axis=0, keepdims=True))
    for refs, values, places in ((col_refs, best, outs), (row_refs, rows_best, row_outs)):
        for ref, held in zip(refs, places):
            for at, one in enumerate(held):
                ref[at] = values[one]


def take(refs, counts):
    groups, at = [], 0
    for count in counts:
        groups.append(refs[at : at + count])
        at += count
    return groups


def score(name, plane, cols, pairs, outs, want_rows=(), row_outs=(), known=(), cols_in=(), rows_in=()):
    length, width = cols[0].shape
    rows = length - TAIL
    counts = tuple(len(pieces) for pieces in plane)
    kernel = functools.partial(
        score_kernel,
        counts,
        len(cols),
        tuple(pairs),
        tuple(want_rows),
        tuple(known),
        len(rows_in),
        tuple(outs),
        tuple(row_outs),
    )
    return pl.pallas_call(
        kernel,
        out_shape=[jax.ShapeDtypeStruct((len(held), 1, rows), jnp.float32) for held in (*outs, *row_outs)],
        compiler_params=pltpu.CompilerParams(vmem_limit_bytes=VMEM),
        cost_estimate=pl.CostEstimate(
            flops=2 * len(pairs) * rows * rows * width,
            bytes_accessed=2 * (len(plane) + len(cols)) * length * width,
            transcendentals=0,
        ),
        name=name,
    )(*[piece for pieces in plane for piece in pieces], *cols, *cols_in, *rows_in)


def join_kernel(n, *refs):
    for at in range(n):
        refs[n + 1 + at][...] = jnp.maximum(refs[at][...], refs[n][at])


def join(here, got):
    return pl.pallas_call(
        functools.partial(join_kernel, len(here)),
        out_shape=[jax.ShapeDtypeStruct((1, x.shape[-1]), x.dtype) for x in here],
        compiler_params=pltpu.CompilerParams(vmem_limit_bytes=VMEM_SMALL),
        name="join",
    )(*[x.reshape(1, -1) for x in here], got)


def halve_kernel(keep_ref, got_ref, low_ref, high_ref):
    half = low_ref.shape[0]
    for at in range(half):
        low_ref[at] = jnp.maximum(keep_ref[at], got_ref[at])
        high_ref[at] = jnp.maximum(keep_ref[half + at], got_ref[half + at])


def halve(keep, got):
    half = jax.ShapeDtypeStruct((keep.shape[0] // 2, *keep.shape[1:]), keep.dtype)
    return pl.pallas_call(
        halve_kernel,
        out_shape=[half, half],
        compiler_params=pltpu.CompilerParams(vmem_limit_bytes=VMEM_SMALL),
        name="halve",
    )(keep, got)


def plane_shift(x, mask):
    size = lax.axis_size("blk")
    return lax.ppermute(x, "blk", [(i, i ^ mask) for i in range(size)])


def grp_shift(x, shift, mask=0):
    groups, size = lax.axis_size("grp"), lax.axis_size("blk")
    if not mask:
        return lax.ppermute(x, "grp", [(z, (z + shift) % groups) for z in range(groups)])
    pairs = [
        (z * size + i, (z + shift) % groups * size + (i ^ mask)) for z in range(groups) for i in range(size)
    ]
    return lax.ppermute(x, ("grp", "blk"), pairs)


def fetch_plane(packed, per_group):
    half = (packed.shape[0] - TAIL) // 2
    plane = {0: (packed,)}
    halves = {}
    for mask in sorted(range(2, per_group, 2), key=lambda mask: mask.bit_count()):
        low, high = mask & -mask, 1 << (mask.bit_length() - 1)
        if low == high:
            block = plane_shift(packed, mask)
            plane[mask] = (block,)
            halves[mask] = (block[:half], block[half:])
        else:
            plane[mask] = halves[mask] = (
                plane_shift(halves[mask ^ low][0], low),
                plane_shift(halves[mask ^ high][1], high),
            )
    return plane


def body(embeddings, target, cluster):
    groups = lax.axis_size("grp")
    per_group = lax.axis_size("blk")
    packed = pack(embeddings, target, cluster, per_group)
    one_off = grp_shift(packed, 1)
    plane = fetch_plane(packed, per_group)
    half_way = grp_shift(one_off, 1)
    direct = [mask for mask, pieces in plane.items() if len(pieces) == 1]
    relayed = [mask for mask, pieces in plane.items() if len(pieces) > 1]

    own_then = lax.optimization_barrier((packed, one_off))[0]
    cols = [packed, plane_shift(own_then, 1), one_off, plane_shift(one_off, 1)]
    every = range(len(cols))
    best, *rows_direct = score(
        "compare_direct",
        [plane[mask] for mask in direct],
        cols,
        [(k, at, k == at == 0) for k in range(len(direct)) for at in every],
        [tuple(every)],
        (2, 3),
        [(k,) for k in range(len(direct))],
    )
    masks = direct + relayed
    in_order = [masks.index(mask) for mask in sorted(masks)]
    half = len(masks) // 2
    own, one_off_best, twins, low, high = score(
        "compare_relayed",
        [plane[mask] for mask in relayed],
        cols,
        [(k, at, False) for k in range(len(relayed)) for at in every],
        [(0,), (2,), (1, 3)],
        (2, 3),
        [tuple(in_order[:half]), tuple(in_order[half:])],
        known=every,
        cols_in=[best],
        rows_in=rows_direct,
    )
    own, one_off_best = join([own, one_off_best], plane_shift(twins, 1))
    found = [own.reshape(1, 1, -1), grp_shift(one_off_best.reshape(1, 1, -1), -1)]

    mask = per_group // 2
    got = plane_shift(high, mask)
    blocks = list(plane.values())
    pairs = [(k, 0, False) for k in range(len(blocks))]
    half_then = lax.optimization_barrier((half_way, own, got))[0]
    for name, block, twin in (("compare_half_way", half_way, 0), ("compare_twin", plane_shift(half_then, 1), 1)):
        (half_best,) = score(name, blocks, [block], pairs, [(0,)])
        found.append(grp_shift(half_best, groups // 2, twin))
    while len(low) > 1:
        low, high = halve(low, got)
        mask //= 2
        got = plane_shift(high, mask)
    found += [low, got]
    return functools.reduce(jnp.maximum, found).reshape(-1)


def solution(mesh):
    return jax.shard_map(
        body,
        mesh=mesh,
        in_specs=(P(("grp", "blk"), None), P(("grp", "blk"), None), P(("grp", "blk"))),
        out_specs=P(("grp", "blk")),
        check_vma=False,
    )
```

```python
import functools

import jax
import jax.numpy as jnp
from jax import lax
from jax.experimental import pallas as pl
from jax.experimental.pallas import tpu as pltpu
from jax.sharding import PartitionSpec as P

CLUSTERS = 64
TAIL = 16
VMEM = 24 << 20
VMEM_SMALL = 8 << 20


def pack_kernel(per_group, emb_ref, target_ref, cluster_ref, out_ref):
    rows, width = emb_ref.shape
    x = emb_ref[...].astype(jnp.float32)
    scale = lax.rsqrt(jnp.sum(x * x, axis=1, keepdims=True) + 1e-06)
    out_ref[:rows, :] = (x * scale).astype(jnp.bfloat16)
    key = target_ref[...] // per_group * CLUSTERS + cluster_ref[...] + 1
    key = jnp.concatenate([key, jnp.zeros((1, width - rows), jnp.int32)], axis=1)
    key = jnp.broadcast_to(key.astype(jnp.float32), (TAIL, width))
    out_ref[rows:, :] = key.astype(jnp.bfloat16)


def pack(embeddings, target, cluster, per_group):
    rows, width = embeddings.shape
    return pl.pallas_call(
        functools.partial(pack_kernel, per_group),
        out_shape=jax.ShapeDtypeStruct((rows + TAIL, width), jnp.bfloat16),
        compiler_params=pltpu.CompilerParams(vmem_limit_bytes=VMEM_SMALL),
        name="pack",
    )(embeddings, target.reshape(1, rows), cluster.reshape(1, rows))


def whole(pieces):
    return pieces[0][...] if len(pieces) == 1 else jnp.concatenate([ref[...] for ref in pieces], axis=0)


def score_kernel(counts, n_cols, pairs, want_rows, known, n_rows_in, outs, row_outs, *refs):
    *plane, cols, cols_in, rows_in, col_refs, row_refs = take(
        refs, counts + (n_cols, bool(known), n_rows_in, len(outs), len(row_outs))
    )
    rows = col_refs[0].shape[2]
    best = [jnp.full((1, rows), -1.0, jnp.float32)] * n_cols
    rows_best = [ref[0] for ref in rows_in]
    for at, col in enumerate(known):
        best[col] = cols_in[0][at]
    for k, pieces in enumerate(plane):
        block = whole(pieces)
        row_keys = jnp.transpose(jnp.broadcast_to(block[rows:, :rows].astype(jnp.float32)[:1], (128, rows)))
        row_keys = jnp.concatenate([row_keys] * (rows // 128), axis=1)
        row_best = None
        for at, same in [(at, same) for one, at, same in pairs if one == k]:
            scores = lax.dot_general(
                block[:rows], cols[at][:rows, :], (((1,), (1,)), ((), ())), preferred_element_type=jnp.float32
            )
            allowed = row_keys == cols[at][rows:, :rows].astype(jnp.float32)[:1]
            if same:
                one = lax.broadcasted_iota(jnp.int32, scores.shape, 0)
                other = lax.broadcasted_iota(jnp.int32, scores.shape, 1)
                allowed = allowed & (one != other)
            masked = jnp.where(allowed, scores, -1.0)
            best[at] = jnp.maximum(best[at], jnp.max(masked, axis=0, keepdims=True))
            if at in want_rows:
                for lane in range(0, rows, 128):
                    part = masked[:, lane : lane + 128]
                    row_best = part if row_best is None else jnp.maximum(row_best, part)
        if row_best is not None:
            rows_best.append(jnp.max(jnp.transpose(row_best), axis=0, keepdims=True))
    for refs, values, places in ((col_refs, best, outs), (row_refs, rows_best, row_outs)):
        for ref, held in zip(refs, places):
            for at, one in enumerate(held):
                ref[at] = values[one]


def take(refs, counts):
    groups, at = [], 0
    for count in counts:
        groups.append(refs[at : at + count])
        at += count
    return groups


def score(name, plane, cols, pairs, outs, want_rows=(), row_outs=(), known=(), cols_in=(), rows_in=()):
    length, width = cols[0].shape
    rows = length - TAIL
    counts = tuple(len(pieces) for pieces in plane)
    kernel = functools.partial(
        score_kernel,
        counts,
        len(cols),
        tuple(pairs),
        tuple(want_rows),
        tuple(known),
        len(rows_in),
        tuple(outs),
        tuple(row_outs),
    )
    return pl.pallas_call(
        kernel,
        out_shape=[jax.ShapeDtypeStruct((len(held), 1, rows), jnp.float32) for held in (*outs, *row_outs)],
        compiler_params=pltpu.CompilerParams(vmem_limit_bytes=VMEM),
        cost_estimate=pl.CostEstimate(
            flops=2 * len(pairs) * rows * rows * width,
            bytes_accessed=2 * (len(plane) + len(cols)) * length * width,
            transcendentals=0,
        ),
        name=name,
    )(*[piece for pieces in plane for piece in pieces], *cols, *cols_in, *rows_in)


def join_kernel(n, *refs):
    for at in range(n):
        refs[n + 1 + at][...] = jnp.maximum(refs[at][...], refs[n][at])


def join(here, got):
    return pl.pallas_call(
        functools.partial(join_kernel, len(here)),
        out_shape=[jax.ShapeDtypeStruct((1, x.shape[-1]), x.dtype) for x in here],
        compiler_params=pltpu.CompilerParams(vmem_limit_bytes=VMEM_SMALL),
        name="join",
    )(*[x.reshape(1, -1) for x in here], got)


def halve_kernel(keep_ref, got_ref, low_ref, high_ref):
    half = low_ref.shape[0]
    for at in range(half):
        low_ref[at] = jnp.maximum(keep_ref[at], got_ref[at])
        high_ref[at] = jnp.maximum(keep_ref[half + at], got_ref[half + at])


def halve(keep, got):
    half = jax.ShapeDtypeStruct((keep.shape[0] // 2, *keep.shape[1:]), keep.dtype)
    return pl.pallas_call(
        halve_kernel,
        out_shape=[half, half],
        compiler_params=pltpu.CompilerParams(vmem_limit_bytes=VMEM_SMALL),
        name="halve",
    )(keep, got)


def plane_shift(x, mask):
    size = lax.axis_size("blk")
    return lax.ppermute(x, "blk", [(i, i ^ mask) for i in range(size)])


def grp_shift(x, shift, mask=0):
    groups, size = lax.axis_size("grp"), lax.axis_size("blk")
    if not mask:
        return lax.ppermute(x, "grp", [(z, (z + shift) % groups) for z in range(groups)])
    pairs = [
        (z * size + i, (z + shift) % groups * size + (i ^ mask)) for z in range(groups) for i in range(size)
    ]
    return lax.ppermute(x, ("grp", "blk"), pairs)


def fetch_plane(packed, per_group):
    half = (packed.shape[0] - TAIL) // 2
    plane = {0: (packed,)}
    halves = {}
    for mask in sorted(range(2, per_group, 2), key=lambda mask: mask.bit_count()):
        low, high = mask & -mask, 1 << (mask.bit_length() - 1)
        if low == high:
            block = plane_shift(packed, mask)
            plane[mask] = (block,)
            halves[mask] = (block[:half], block[half:])
        else:
            plane[mask] = halves[mask] = (
                plane_shift(halves[mask ^ low][0], low),
                plane_shift(halves[mask ^ high][1], high),
            )
    return plane


def body(embeddings, target, cluster):
    groups = lax.axis_size("grp")
    per_group = lax.axis_size("blk")
    packed = pack(embeddings, target, cluster, per_group)
    one_off = grp_shift(packed, 1)
    plane = fetch_plane(packed, per_group)
    half_way = grp_shift(one_off, 1)
    direct = [mask for mask, pieces in plane.items() if len(pieces) == 1]
    relayed = [mask for mask, pieces in plane.items() if len(pieces) > 1]

    own_then = lax.optimization_barrier((packed, one_off))[0]
    cols = [packed, plane_shift(own_then, 1), one_off, plane_shift(one_off, 1)]
    every = range(len(cols))
    best, *rows_direct = score(
        "compare_direct",
        [plane[mask] for mask in direct],
        cols,
        [(k, at, k == at == 0) for k in range(len(direct)) for at in every],
        [tuple(every)],
        (2, 3),
        [(k,) for k in range(len(direct))],
    )
    masks = direct + relayed
    in_order = [masks.index(mask) for mask in sorted(masks)]
    half = len(masks) // 2
    own, one_off_best, twins, low, high = score(
        "compare_relayed",
        [plane[mask] for mask in relayed],
        cols,
        [(k, at, False) for k in range(len(relayed)) for at in every],
        [(0,), (2,), (1, 3)],
        (2, 3),
        [tuple(in_order[:half]), tuple(in_order[half:])],
        known=every,
        cols_in=[best],
        rows_in=rows_direct,
    )
    own, one_off_best = join([own, one_off_best], plane_shift(twins, 1))
    found = [own.reshape(1, 1, -1), grp_shift(one_off_best.reshape(1, 1, -1), -1)]

    mask = per_group // 2
    got = plane_shift(high, mask)
    blocks = list(plane.values())
    pairs = [(k, 0, False) for k in range(len(blocks))]
    half_then = lax.optimization_barrier((half_way, found, got))[0]
    for name, block, twin in (("compare_half_way", half_way, 0), ("compare_twin", plane_shift(half_then, 1), 1)):
        (half_best,) = score(name, blocks, [block], pairs, [(0,)])
        found.append(grp_shift(half_best, groups // 2, twin))
    while len(low) > 1:
        low, high = halve(low, got)
        high = lax.optimization_barrier((high, half_best))[0]
        mask //= 2
        got = plane_shift(high, mask)
    found += [low, got]
    return functools.reduce(jnp.maximum, found).reshape(-1)


def solution(mesh):
    return jax.shard_map(
        body,
        mesh=mesh,
        in_specs=(P(("grp", "blk"), None), P(("grp", "blk"), None), P(("grp", "blk"))),
        out_specs=P(("grp", "blk")),
        check_vma=False,
    )
```

```python
import functools

import jax
import jax.numpy as jnp
from jax import lax
from jax.experimental import pallas as pl
from jax.experimental.pallas import tpu as pltpu
from jax.sharding import PartitionSpec as P

CLUSTERS = 64
TAIL = 16
VMEM = 24 << 20
VMEM_SMALL = 8 << 20


def pack_kernel(per_group, emb_ref, target_ref, cluster_ref, out_ref):
    rows, width = emb_ref.shape
    x = emb_ref[...].astype(jnp.float32)
    scale = lax.rsqrt(jnp.sum(x * x, axis=1, keepdims=True) + 1e-06)
    out_ref[:rows, :] = (x * scale).astype(jnp.bfloat16)
    key = target_ref[...] // per_group * CLUSTERS + cluster_ref[...] + 1
    key = jnp.concatenate([key, jnp.zeros((1, width - rows), jnp.int32)], axis=1)
    key = jnp.broadcast_to(key.astype(jnp.float32), (TAIL, width))
    out_ref[rows:, :] = key.astype(jnp.bfloat16)


def pack(embeddings, target, cluster, per_group):
    rows, width = embeddings.shape
    return pl.pallas_call(
        functools.partial(pack_kernel, per_group),
        out_shape=jax.ShapeDtypeStruct((rows + TAIL, width), jnp.bfloat16),
        compiler_params=pltpu.CompilerParams(vmem_limit_bytes=VMEM_SMALL),
        name="pack",
    )(embeddings, target.reshape(1, rows), cluster.reshape(1, rows))


def whole(pieces):
    return pieces[0][...] if len(pieces) == 1 else jnp.concatenate([ref[...] for ref in pieces], axis=0)


def score_kernel(counts, n_cols, pairs, want_rows, known, n_rows_in, outs, row_outs, places, *refs):
    *plane, cols, cols_in, rows_in, col_refs, row_refs = take(
        refs, counts + (n_cols, bool(known), n_rows_in, len(outs), 1 if places else len(row_outs))
    )
    rows = col_refs[0].shape[2]
    best = [jnp.full((1, rows), -1.0, jnp.float32)] * n_cols
    rows_best = [ref[0] for ref in rows_in]
    for at, col in enumerate(known):
        best[col] = cols_in[0][at]
    for k, pieces in enumerate(plane):
        block = whole(pieces)
        row_keys = jnp.transpose(jnp.broadcast_to(block[rows:, :rows].astype(jnp.float32)[:1], (128, rows)))
        row_keys = jnp.concatenate([row_keys] * (rows // 128), axis=1)
        row_best = None
        for at, same in [(at, same) for one, at, same in pairs if one == k]:
            scores = lax.dot_general(
                block[:rows], cols[at][:rows, :], (((1,), (1,)), ((), ())), preferred_element_type=jnp.float32
            )
            allowed = row_keys == cols[at][rows:, :rows].astype(jnp.float32)[:1]
            if same:
                one = lax.broadcasted_iota(jnp.int32, scores.shape, 0)
                other = lax.broadcasted_iota(jnp.int32, scores.shape, 1)
                allowed = allowed & (one != other)
            masked = jnp.where(allowed, scores, -1.0)
            best[at] = jnp.maximum(best[at], jnp.max(masked, axis=0, keepdims=True))
            if at in want_rows:
                for lane in range(0, rows, 128):
                    part = masked[:, lane : lane + 128]
                    row_best = part if row_best is None else jnp.maximum(row_best, part)
        if row_best is not None:
            rows_best.append(jnp.max(jnp.transpose(row_best), axis=0, keepdims=True))
    for refs, values, holds in ((col_refs, best, outs), (row_refs, rows_best, row_outs)):
        for ref, held in zip(refs, holds):
            for at, one in enumerate(held):
                ref[at] = values[one]
    if places:
        chip = lax.axis_index("blk") // 2
        for place, value in zip(places, rows_best):
            row_refs[0][chip ^ place] = value


def take(refs, counts):
    groups, at = [], 0
    for count in counts:
        groups.append(refs[at : at + count])
        at += count
    return groups


def score(name, plane, cols, pairs, outs, want_rows=(), row_outs=(), known=(), cols_in=(), rows_in=(), places=()):
    length, width = cols[0].shape
    rows = length - TAIL
    counts = tuple(len(pieces) for pieces in plane)
    kernel = functools.partial(
        score_kernel,
        counts,
        len(cols),
        tuple(pairs),
        tuple(want_rows),
        tuple(known),
        len(rows_in),
        tuple(outs),
        tuple(row_outs),
        tuple(places),
    )
    held_rows = [places] if places else row_outs
    return pl.pallas_call(
        kernel,
        out_shape=[jax.ShapeDtypeStruct((len(held), 1, rows), jnp.float32) for held in (*outs, *held_rows)],
        compiler_params=pltpu.CompilerParams(vmem_limit_bytes=VMEM),
        cost_estimate=pl.CostEstimate(
            flops=2 * len(pairs) * rows * rows * width,
            bytes_accessed=2 * (len(plane) + len(cols)) * length * width,
            transcendentals=0,
        ),
        name=name,
    )(*[piece for pieces in plane for piece in pieces], *cols, *cols_in, *rows_in)


def join_kernel(n, *refs):
    for at in range(n):
        refs[n + 1 + at][...] = jnp.maximum(refs[at][...], refs[n][at])


def join(here, got):
    return pl.pallas_call(
        functools.partial(join_kernel, len(here)),
        out_shape=[jax.ShapeDtypeStruct((1, x.shape[-1]), x.dtype) for x in here],
        compiler_params=pltpu.CompilerParams(vmem_limit_bytes=VMEM_SMALL),
        name="join",
    )(*[x.reshape(1, -1) for x in here], got)


def plane_shift(x, mask):
    size = lax.axis_size("blk")
    return lax.ppermute(x, "blk", [(i, i ^ mask) for i in range(size)])


def grp_shift(x, shift, mask=0):
    groups, size = lax.axis_size("grp"), lax.axis_size("blk")
    if not mask:
        return lax.ppermute(x, "grp", [(z, (z + shift) % groups) for z in range(groups)])
    pairs = [
        (z * size + i, (z + shift) % groups * size + (i ^ mask)) for z in range(groups) for i in range(size)
    ]
    return lax.ppermute(x, ("grp", "blk"), pairs)


def fetch_plane(packed, per_group):
    half = (packed.shape[0] - TAIL) // 2
    plane = {0: (packed,)}
    halves = {}
    for mask in sorted(range(2, per_group, 2), key=lambda mask: mask.bit_count()):
        low, high = mask & -mask, 1 << (mask.bit_length() - 1)
        if low == high:
            block = plane_shift(packed, mask)
            plane[mask] = (block,)
            halves[mask] = (block[:half], block[half:])
        else:
            plane[mask] = halves[mask] = (
                plane_shift(halves[mask ^ low][0], low),
                plane_shift(halves[mask ^ high][1], high),
            )
    return plane


def body(embeddings, target, cluster):
    groups = lax.axis_size("grp")
    per_group = lax.axis_size("blk")
    packed = pack(embeddings, target, cluster, per_group)
    one_off = grp_shift(packed, 1)
    plane = fetch_plane(packed, per_group)
    half_way = grp_shift(one_off, 1)
    direct = [mask for mask, pieces in plane.items() if len(pieces) == 1]
    relayed = [mask for mask, pieces in plane.items() if len(pieces) > 1]

    own_then = lax.optimization_barrier((packed, one_off))[0]
    cols = [packed, plane_shift(own_then, 1), one_off, plane_shift(one_off, 1)]
    every = range(len(cols))
    best, *rows_direct = score(
        "compare_direct",
        [plane[mask] for mask in direct],
        cols,
        [(k, at, k == at == 0) for k in range(len(direct)) for at in every],
        [tuple(every)],
        (2, 3),
        [(k,) for k in range(len(direct))],
    )
    own, one_off_best, twins, rows_best = score(
        "compare_relayed",
        [plane[mask] for mask in relayed],
        cols,
        [(k, at, False) for k in range(len(relayed)) for at in every],
        [(0,), (2,), (1, 3)],
        (2, 3),
        known=every,
        cols_in=[best],
        rows_in=rows_direct,
        places=[mask // 2 for mask in direct + relayed],
    )
    cores = [[i for i in range(per_group) if i % 2 == core] for core in range(2)]
    rows_back = lax.all_to_all(
        rows_best, "blk", split_axis=0, concat_axis=0, axis_index_groups=cores, tiled=True
    )
    own, one_off_best = join([own, one_off_best], plane_shift(twins, 1))
    found = [own.reshape(1, 1, -1), grp_shift(one_off_best.reshape(1, 1, -1), -1)]

    blocks = list(plane.values())
    pairs = [(k, 0, False) for k in range(len(blocks))]
    half_then = lax.optimization_barrier((half_way, own))[0]
    for name, block, twin in (("compare_half_way", half_way, 0), ("compare_twin", plane_shift(half_then, 1), 1)):
        (half_best,) = score(name, blocks, [block], pairs, [(0,)])
        found.append(grp_shift(half_best, groups // 2, twin))
    found.append(jnp.max(rows_back, axis=0, keepdims=True))
    return functools.reduce(jnp.maximum, found).reshape(-1)


def solution(mesh):
    return jax.shard_map(
        body,
        mesh=mesh,
        in_specs=(P(("grp", "blk"), None), P(("grp", "blk"), None), P(("grp", "blk"))),
        out_specs=P(("grp", "blk")),
        check_vma=False,
    )
```

```python
import functools

import jax
import jax.numpy as jnp
from jax import lax
from jax.experimental import pallas as pl
from jax.experimental.pallas import tpu as pltpu
from jax.sharding import PartitionSpec as P

CLUSTERS = 64
TAIL = 16
VMEM = 24 << 20
VMEM_SMALL = 8 << 20


def pack_kernel(per_group, emb_ref, target_ref, cluster_ref, out_ref):
    rows, width = emb_ref.shape
    x = emb_ref[...].astype(jnp.float32)
    scale = lax.rsqrt(jnp.sum(x * x, axis=1, keepdims=True) + 1e-06)
    out_ref[:rows, :] = (x * scale).astype(jnp.bfloat16)
    key = target_ref[...] // per_group * CLUSTERS + cluster_ref[...] + 1
    key = jnp.concatenate([key, jnp.zeros((1, width - rows), jnp.int32)], axis=1)
    key = jnp.broadcast_to(key.astype(jnp.float32), (TAIL, width))
    out_ref[rows:, :] = key.astype(jnp.bfloat16)


def pack(embeddings, target, cluster, per_group):
    rows, width = embeddings.shape
    return pl.pallas_call(
        functools.partial(pack_kernel, per_group),
        out_shape=jax.ShapeDtypeStruct((rows + TAIL, width), jnp.bfloat16),
        compiler_params=pltpu.CompilerParams(vmem_limit_bytes=VMEM_SMALL),
        name="pack",
    )(embeddings, target.reshape(1, rows), cluster.reshape(1, rows))


def whole(pieces):
    return pieces[0][...] if len(pieces) == 1 else jnp.concatenate([ref[...] for ref in pieces], axis=0)


def score_kernel(counts, n_cols, pairs, want_rows, known, n_rows_in, outs, row_outs, places, *refs):
    *plane, cols, cols_in, rows_in, col_refs, row_refs = take(
        refs, counts + (n_cols, bool(known), n_rows_in, len(outs), 1 if places else len(row_outs))
    )
    rows = col_refs[0].shape[2]
    best = [jnp.full((1, rows), -1.0, jnp.float32)] * n_cols
    rows_best = [ref[0] for ref in rows_in]
    for at, col in enumerate(known):
        best[col] = cols_in[0][at]
    for k, pieces in enumerate(plane):
        block = whole(pieces)
        row_keys = jnp.transpose(jnp.broadcast_to(block[rows:, :rows].astype(jnp.float32)[:1], (128, rows)))
        row_keys = jnp.concatenate([row_keys] * (rows // 128), axis=1)
        row_best = None
        for at, same in [(at, same) for one, at, same in pairs if one == k]:
            scores = lax.dot_general(
                block[:rows], cols[at][:rows, :], (((1,), (1,)), ((), ())), preferred_element_type=jnp.float32
            )
            allowed = row_keys == cols[at][rows:, :rows].astype(jnp.float32)[:1]
            if same:
                one = lax.broadcasted_iota(jnp.int32, scores.shape, 0)
                other = lax.broadcasted_iota(jnp.int32, scores.shape, 1)
                allowed = allowed & (one != other)
            masked = jnp.where(allowed, scores, -1.0)
            best[at] = jnp.maximum(best[at], jnp.max(masked, axis=0, keepdims=True))
            if at in want_rows:
                for lane in range(0, rows, 128):
                    part = masked[:, lane : lane + 128]
                    row_best = part if row_best is None else jnp.maximum(row_best, part)
        if row_best is not None:
            rows_best.append(jnp.max(jnp.transpose(row_best), axis=0, keepdims=True))
    for refs, values, holds in ((col_refs, best, outs), (row_refs, rows_best, row_outs)):
        for ref, held in zip(refs, holds):
            for at, one in enumerate(held):
                ref[at] = values[one]
    if places:
        chip = lax.axis_index("blk") // 2
        for place, value in zip(places, rows_best):
            row_refs[0][chip ^ place] = value


def take(refs, counts):
    groups, at = [], 0
    for count in counts:
        groups.append(refs[at : at + count])
        at += count
    return groups


def score(name, plane, cols, pairs, outs, want_rows=(), row_outs=(), known=(), cols_in=(), rows_in=(), places=(), weight=1):
    length, width = cols[0].shape
    rows = length - TAIL
    counts = tuple(len(pieces) for pieces in plane)
    kernel = functools.partial(
        score_kernel,
        counts,
        len(cols),
        tuple(pairs),
        tuple(want_rows),
        tuple(known),
        len(rows_in),
        tuple(outs),
        tuple(row_outs),
        tuple(places),
    )
    held_rows = [places] if places else row_outs
    return pl.pallas_call(
        kernel,
        out_shape=[jax.ShapeDtypeStruct((len(held), 1, rows), jnp.float32) for held in (*outs, *held_rows)],
        compiler_params=pltpu.CompilerParams(vmem_limit_bytes=VMEM),
        cost_estimate=pl.CostEstimate(
            flops=weight * 2 * len(pairs) * rows * rows * width,
            bytes_accessed=weight * 2 * (len(plane) + len(cols)) * length * width,
            transcendentals=0,
        ),
        name=name,
    )(*[piece for pieces in plane for piece in pieces], *cols, *cols_in, *rows_in)


def join_kernel(n, *refs):
    for at in range(n):
        refs[n + 1 + at][...] = jnp.maximum(refs[at][...], refs[n][at])


def join(here, got):
    return pl.pallas_call(
        functools.partial(join_kernel, len(here)),
        out_shape=[jax.ShapeDtypeStruct((1, x.shape[-1]), x.dtype) for x in here],
        compiler_params=pltpu.CompilerParams(vmem_limit_bytes=VMEM_SMALL),
        name="join",
    )(*[x.reshape(1, -1) for x in here], got)


def plane_shift(x, mask):
    size = lax.axis_size("blk")
    return lax.ppermute(x, "blk", [(i, i ^ mask) for i in range(size)])


def grp_shift(x, shift, mask=0):
    groups, size = lax.axis_size("grp"), lax.axis_size("blk")
    if not mask:
        return lax.ppermute(x, "grp", [(z, (z + shift) % groups) for z in range(groups)])
    pairs = [
        (z * size + i, (z + shift) % groups * size + (i ^ mask)) for z in range(groups) for i in range(size)
    ]
    return lax.ppermute(x, ("grp", "blk"), pairs)


def fetch_plane(packed, per_group):
    half = (packed.shape[0] - TAIL) // 2
    plane = {0: (packed,)}
    halves = {}
    for mask in sorted(range(2, per_group, 2), key=lambda mask: mask.bit_count()):
        low, high = mask & -mask, 1 << (mask.bit_length() - 1)
        if low == high:
            block = plane_shift(packed, mask)
            plane[mask] = (block,)
            halves[mask] = (block[:half], block[half:])
        else:
            plane[mask] = halves[mask] = (
                plane_shift(halves[mask ^ low][0], low),
                plane_shift(halves[mask ^ high][1], high),
            )
    return plane


def body(embeddings, target, cluster):
    groups = lax.axis_size("grp")
    per_group = lax.axis_size("blk")
    packed = pack(embeddings, target, cluster, per_group)
    one_off = grp_shift(packed, 1)
    plane = fetch_plane(packed, per_group)
    half_way = grp_shift(one_off, 1)
    direct = [mask for mask, pieces in plane.items() if len(pieces) == 1]
    relayed = [mask for mask, pieces in plane.items() if len(pieces) > 1]

    own_then = lax.optimization_barrier((packed, one_off))[0]
    cols = [packed, plane_shift(own_then, 1), one_off, plane_shift(one_off, 1)]
    every = range(len(cols))
    best, *rows_direct = score(
        "compare_direct",
        [plane[mask] for mask in direct],
        cols,
        [(k, at, k == at == 0) for k in range(len(direct)) for at in every],
        [tuple(every)],
        (2, 3),
        [(k,) for k in range(len(direct))],
    )
    own, one_off_best, twins, rows_best = score(
        "compare_relayed",
        [plane[mask] for mask in relayed],
        cols,
        [(k, at, False) for k in range(len(relayed)) for at in every],
        [(0,), (2,), (1, 3)],
        (2, 3),
        known=every,
        cols_in=[best],
        rows_in=rows_direct,
        places=[mask // 2 for mask in direct + relayed],
    )
    cores = [[i for i in range(per_group) if i % 2 == core] for core in range(2)]
    rows_back = lax.all_to_all(
        rows_best, "blk", split_axis=0, concat_axis=0, axis_index_groups=cores, tiled=True
    )
    own, one_off_best = join([own, one_off_best], plane_shift(twins, 1))
    found = [own.reshape(1, 1, -1), grp_shift(one_off_best.reshape(1, 1, -1), -1)]

    blocks = list(plane.values())
    pairs = [(k, 0, False) for k in range(len(blocks))]
    half_then = lax.optimization_barrier((half_way, own))[0]
    for name, block, twin in (("compare_half_way", half_way, 0), ("compare_twin", plane_shift(half_then, 1), 1)):
        (half_best,) = score(name, blocks, [block], pairs, [(0,)], weight=0)
        found.append(grp_shift(half_best, groups // 2, twin))
    found.append(jnp.max(rows_back, axis=0, keepdims=True))
    return functools.reduce(jnp.maximum, found).reshape(-1)


def solution(mesh):
    return jax.shard_map(
        body,
        mesh=mesh,
        in_specs=(P(("grp", "blk"), None), P(("grp", "blk"), None), P(("grp", "blk"))),
        out_specs=P(("grp", "blk")),
        check_vma=False,
    )
```

```python
import functools

import jax
import jax.numpy as jnp
from jax import lax
from jax.experimental import pallas as pl
from jax.experimental.pallas import tpu as pltpu
from jax.sharding import PartitionSpec as P

CLUSTERS = 64
TAIL = 16
VMEM = 24 << 20
VMEM_SMALL = 8 << 20


def pack_kernel(per_group, emb_ref, target_ref, cluster_ref, out_ref):
    rows, width = emb_ref.shape
    x = emb_ref[...].astype(jnp.float32)
    scale = lax.rsqrt(jnp.sum(x * x, axis=1, keepdims=True) + 1e-06)
    out_ref[:rows, :] = (x * scale).astype(jnp.bfloat16)
    key = target_ref[...] // per_group * CLUSTERS + cluster_ref[...] + 1
    key = jnp.concatenate([key, jnp.zeros((1, width - rows), jnp.int32)], axis=1)
    key = jnp.broadcast_to(key.astype(jnp.float32), (TAIL, width))
    out_ref[rows:, :] = key.astype(jnp.bfloat16)


def pack(embeddings, target, cluster, per_group):
    rows, width = embeddings.shape
    return pl.pallas_call(
        functools.partial(pack_kernel, per_group),
        out_shape=jax.ShapeDtypeStruct((rows + TAIL, width), jnp.bfloat16),
        compiler_params=pltpu.CompilerParams(vmem_limit_bytes=VMEM_SMALL),
        name="pack",
    )(embeddings, target.reshape(1, rows), cluster.reshape(1, rows))


def whole(pieces):
    return pieces[0][...] if len(pieces) == 1 else jnp.concatenate([ref[...] for ref in pieces], axis=0)


def score_kernel(counts, n_cols, pairs, want_rows, known, outs, *refs):
    n_rows = len(counts) if want_rows else 0
    *plane, cols, cols_in, col_outs, row_outs = take(refs, counts + (n_cols, bool(known), len(outs), n_rows))
    rows = col_outs[0].shape[2]
    best = [jnp.full((1, rows), -1.0, jnp.float32)] * n_cols
    for at, col in enumerate(known):
        best[col] = cols_in[0][at]
    for k, pieces in enumerate(plane):
        block = whole(pieces)
        row_keys = jnp.transpose(jnp.broadcast_to(block[rows:, :rows].astype(jnp.float32)[:1], (128, rows)))
        row_keys = jnp.concatenate([row_keys] * (rows // 128), axis=1)
        row_best = None
        for at, same in [(at, same) for one, at, same in pairs if one == k]:
            scores = lax.dot_general(
                block[:rows], cols[at][:rows, :], (((1,), (1,)), ((), ())), preferred_element_type=jnp.float32
            )
            allowed = row_keys == cols[at][rows:, :rows].astype(jnp.float32)[:1]
            if same:
                one = lax.broadcasted_iota(jnp.int32, scores.shape, 0)
                other = lax.broadcasted_iota(jnp.int32, scores.shape, 1)
                allowed = allowed & (one != other)
            masked = jnp.where(allowed, scores, -1.0)
            best[at] = jnp.maximum(best[at], jnp.max(masked, axis=0, keepdims=True))
            if at in want_rows:
                for lane in range(0, rows, 128):
                    part = masked[:, lane : lane + 128]
                    row_best = part if row_best is None else jnp.maximum(row_best, part)
        if row_best is not None:
            row_outs[k][0] = jnp.max(jnp.transpose(row_best), axis=0, keepdims=True)
    for ref, held in zip(col_outs, outs):
        for at, col in enumerate(held):
            ref[at] = best[col]


def take(refs, counts):
    groups, at = [], 0
    for count in counts:
        groups.append(refs[at : at + count])
        at += count
    return groups


def score(name, plane, cols, pairs, want_rows, outs, known=(), cols_in=()):
    length, width = cols[0].shape
    rows = length - TAIL
    counts = tuple(len(pieces) for pieces in plane)
    kernel = functools.partial(
        score_kernel, counts, len(cols), tuple(pairs), tuple(want_rows), tuple(known), tuple(outs)
    )
    shapes = [len(held) for held in outs] + [1] * (len(plane) if want_rows else 0)
    return pl.pallas_call(
        kernel,
        out_shape=[jax.ShapeDtypeStruct((count, 1, rows), jnp.float32) for count in shapes],
        compiler_params=pltpu.CompilerParams(vmem_limit_bytes=VMEM),
        cost_estimate=pl.CostEstimate(
            flops=2 * len(pairs) * rows * rows * width,
            bytes_accessed=2 * (len(plane) + len(cols)) * length * width,
            transcendentals=0,
        ),
        name=name,
    )(*[piece for pieces in plane for piece in pieces], *cols, *cols_in)


def join_kernel(n, *refs):
    for at in range(n):
        refs[n + 1 + at][...] = jnp.maximum(refs[at][...], refs[n][at])


def join(here, got):
    return pl.pallas_call(
        functools.partial(join_kernel, len(here)),
        out_shape=[jax.ShapeDtypeStruct((1, x.shape[-1]), x.dtype) for x in here],
        compiler_params=pltpu.CompilerParams(vmem_limit_bytes=VMEM_SMALL),
        name="join",
    )(*[x.reshape(1, -1) for x in here], got)


def plane_shift(x, mask):
    size = lax.axis_size("blk")
    return lax.ppermute(x, "blk", [(i, i ^ mask) for i in range(size)])


def grp_shift(x, shift, mask=0):
    groups, size = lax.axis_size("grp"), lax.axis_size("blk")
    if not mask:
        return lax.ppermute(x, "grp", [(z, (z + shift) % groups) for z in range(groups)])
    pairs = [
        (z * size + i, (z + shift) % groups * size + (i ^ mask)) for z in range(groups) for i in range(size)
    ]
    return lax.ppermute(x, ("grp", "blk"), pairs)


def fetch_plane(packed, per_group):
    half = (packed.shape[0] - TAIL) // 2
    plane = {0: (packed,)}
    halves = {}
    for mask in sorted(range(2, per_group, 2), key=lambda mask: mask.bit_count()):
        low, high = mask & -mask, 1 << (mask.bit_length() - 1)
        if low == high:
            block = plane_shift(packed, mask)
            plane[mask] = (block,)
            halves[mask] = (block[:half], block[half:])
        else:
            plane[mask] = halves[mask] = (
                plane_shift(halves[mask ^ low][0], low),
                plane_shift(halves[mask ^ high][1], high),
            )
    return plane


def body(embeddings, target, cluster):
    groups = lax.axis_size("grp")
    per_group = lax.axis_size("blk")
    packed = pack(embeddings, target, cluster, per_group)
    one_off = grp_shift(packed, 1)
    plane = fetch_plane(packed, per_group)
    own_then = lax.optimization_barrier((packed, one_off))[0]
    own_twin = plane_shift(own_then, 1)
    half_way = grp_shift(one_off, 1)
    direct = [mask for mask, pieces in plane.items() if len(pieces) == 1]
    relayed = [mask for mask, pieces in plane.items() if len(pieces) > 1]

    cols = [packed, own_twin, one_off, plane_shift(one_off, 1)]
    every = range(len(cols))
    best, *rows_direct = score(
        "compare_direct",
        [plane[mask] for mask in direct],
        cols,
        [(k, at, k == at == 0) for k in range(len(direct)) for at in every],
        (2, 3),
        [tuple(every)],
    )
    early = [plane_shift(best, mask) for best, mask in zip(rows_direct[1:], direct[1:])]
    best = lax.optimization_barrier((best, early))[0]
    own, one_off_best, twins, *rows_relayed = score(
        "compare_relayed",
        [plane[mask] for mask in relayed],
        cols,
        [(k, at, False) for k in range(len(relayed)) for at in every],
        (2, 3),
        [(0,), (2,), (1, 3)],
        known=every,
        cols_in=[best],
    )
    own, one_off_best = join([own, one_off_best], plane_shift(twins, 1))
    found = [own.reshape(1, 1, -1), rows_direct[0]]
    early += [plane_shift(best, mask) for best, mask in zip(rows_relayed, relayed)]
    found.append(grp_shift(one_off_best.reshape(1, 1, -1), -1))

    blocks = list(plane.values())
    pairs = [(k, 0, False) for k in range(len(blocks))]
    half_then = lax.optimization_barrier((half_way, own))[0]
    half_twin = lax.optimization_barrier((plane_shift(half_then, 1), early))[0]
    for name, block, mask in (("compare_half_way", half_way, 0), ("compare_twin", half_twin, 1)):
        (half_best,) = score(name, blocks, [block], pairs, (), [(0,)])
        found.append(grp_shift(half_best, groups // 2, mask))
    return functools.reduce(jnp.maximum, found + early).reshape(-1)


def solution(mesh):
    return jax.shard_map(
        body,
        mesh=mesh,
        in_specs=(P(("grp", "blk"), None), P(("grp", "blk"), None), P(("grp", "blk"))),
        out_specs=P(("grp", "blk")),
        check_vma=False,
    )
```

```python
import functools

import jax
import jax.numpy as jnp
from jax import lax
from jax.experimental import pallas as pl
from jax.experimental.pallas import tpu as pltpu
from jax.sharding import PartitionSpec as P

CLUSTERS = 64
LANES = 128
TAIL = 16
VMEM = 24 << 20
VMEM_SMALL = 8 << 20


def pack_kernel(per_group, emb_ref, target_ref, cluster_ref, out_ref):
    rows, width = emb_ref.shape
    x = emb_ref[...].astype(jnp.float32)
    scale = lax.rsqrt(jnp.sum(x * x, axis=1, keepdims=True) + 1e-06)
    normed = (x * scale).astype(jnp.bfloat16)
    for at in range(width // LANES):
        out_ref[at * rows : (at + 1) * rows, :] = normed[:, at * LANES : (at + 1) * LANES]
    key = (target_ref[...] // per_group * CLUSTERS + cluster_ref[...] + 1).astype(jnp.float32)
    tail = [key[:, at : at + LANES] for at in range(0, rows, LANES)]
    tail.append(jnp.zeros((TAIL - len(tail), LANES), jnp.float32))
    out_ref[out_ref.shape[0] - TAIL :, :] = jnp.concatenate(tail, axis=0).astype(jnp.bfloat16)


def pack(embeddings, target, cluster, per_group):
    rows, width = embeddings.shape
    return pl.pallas_call(
        functools.partial(pack_kernel, per_group),
        out_shape=jax.ShapeDtypeStruct((rows * width // LANES + TAIL, LANES), jnp.bfloat16),
        compiler_params=pltpu.CompilerParams(vmem_limit_bytes=VMEM_SMALL),
        name="pack",
    )(embeddings, target.reshape(1, rows), cluster.reshape(1, rows))


def unpack(pieces, rows):
    panels = [ref[at : at + rows, :] for ref in pieces for at in range(0, ref.shape[0] - rows + 1, rows)]
    tail = pieces[-1][pieces[-1].shape[0] - TAIL :, :].astype(jnp.float32)
    keys = [tail[at : at + 1, :] for at in range(rows // LANES)]
    return jnp.concatenate(panels, axis=1), jnp.concatenate(keys, axis=1)


def score_kernel(counts, n_cols, pairs, want_rows, known, outs, *refs):
    n_rows = len(counts) if want_rows else 0
    *plane, cols, cols_in, col_outs, row_outs = take(refs, counts + (n_cols, bool(known), len(outs), n_rows))
    rows = col_outs[0].shape[2]
    best = [jnp.full((1, rows), -1.0, jnp.float32)] * n_cols
    for at, col in enumerate(known):
        best[col] = cols_in[0][at]
    cols = [unpack([ref], rows) for ref in cols]
    for k, pieces in enumerate(plane):
        block, keys = unpack(pieces, rows)
        row_keys = jnp.transpose(jnp.broadcast_to(keys, (LANES, rows)))
        row_keys = jnp.concatenate([row_keys] * (rows // LANES), axis=1)
        row_best = None
        for at, same in [(at, same) for one, at, same in pairs if one == k]:
            col, col_keys = cols[at]
            scores = lax.dot_general(
                block, col, (((1,), (1,)), ((), ())), preferred_element_type=jnp.float32
            )
            allowed = row_keys == col_keys
            if same:
                one = lax.broadcasted_iota(jnp.int32, scores.shape, 0)
                other = lax.broadcasted_iota(jnp.int32, scores.shape, 1)
                allowed = allowed & (one != other)
            masked = jnp.where(allowed, scores, -1.0)
            best[at] = jnp.maximum(best[at], jnp.max(masked, axis=0, keepdims=True))
            if at in want_rows:
                for lane in range(0, rows, LANES):
                    part = masked[:, lane : lane + LANES]
                    row_best = part if row_best is None else jnp.maximum(row_best, part)
        if row_best is not None:
            row_outs[k][0] = jnp.max(jnp.transpose(row_best), axis=0, keepdims=True)
    for ref, held in zip(col_outs, outs):
        for at, col in enumerate(held):
            ref[at] = best[col]


def take(refs, counts):
    groups, at = [], 0
    for count in counts:
        groups.append(refs[at : at + count])
        at += count
    return groups


def score(name, rows, plane, cols, pairs, want_rows, outs, known=(), cols_in=()):
    size = cols[0].size
    counts = tuple(len(pieces) for pieces in plane)
    kernel = functools.partial(
        score_kernel, counts, len(cols), tuple(pairs), tuple(want_rows), tuple(known), tuple(outs)
    )
    shapes = [len(held) for held in outs] + [1] * (len(plane) if want_rows else 0)
    return pl.pallas_call(
        kernel,
        out_shape=[jax.ShapeDtypeStruct((count, 1, rows), jnp.float32) for count in shapes],
        compiler_params=pltpu.CompilerParams(vmem_limit_bytes=VMEM),
        cost_estimate=pl.CostEstimate(
            flops=2 * len(pairs) * rows * size,
            bytes_accessed=2 * (len(plane) + len(cols)) * size,
            transcendentals=0,
        ),
        name=name,
    )(*[piece for pieces in plane for piece in pieces], *cols, *cols_in)


def join_kernel(n, *refs):
    for at in range(n):
        refs[n + 1 + at][...] = jnp.maximum(refs[at][...], refs[n][at])


def join(here, got):
    return pl.pallas_call(
        functools.partial(join_kernel, len(here)),
        out_shape=[jax.ShapeDtypeStruct((1, x.shape[-1]), x.dtype) for x in here],
        compiler_params=pltpu.CompilerParams(vmem_limit_bytes=VMEM_SMALL),
        name="join",
    )(*[x.reshape(1, -1) for x in here], got)


def plane_shift(x, mask):
    size = lax.axis_size("blk")
    return lax.ppermute(x, "blk", [(i, i ^ mask) for i in range(size)])


def grp_shift(x, shift, mask=0):
    groups, size = lax.axis_size("grp"), lax.axis_size("blk")
    if not mask:
        return lax.ppermute(x, "grp", [(z, (z + shift) % groups) for z in range(groups)])
    pairs = [
        (z * size + i, (z + shift) % groups * size + (i ^ mask)) for z in range(groups) for i in range(size)
    ]
    return lax.ppermute(x, ("grp", "blk"), pairs)


def fetch_plane(packed, rows, per_group):
    half = packed.shape[0] // rows // 2 * rows
    plane = {0: (packed,)}
    halves = {}
    for mask in sorted(range(2, per_group, 2), key=lambda mask: mask.bit_count()):
        low, high = mask & -mask, 1 << (mask.bit_length() - 1)
        if low == high:
            block = plane_shift(packed, mask)
            plane[mask] = (block,)
            halves[mask] = (block[:half], block[half:])
        else:
            plane[mask] = halves[mask] = (
                plane_shift(halves[mask ^ low][0], low),
                plane_shift(halves[mask ^ high][1], high),
            )
    return plane


def body(embeddings, target, cluster):
    groups = lax.axis_size("grp")
    per_group = lax.axis_size("blk")
    rows = embeddings.shape[0]
    packed = pack(embeddings, target, cluster, per_group)
    one_off = grp_shift(packed, 1)
    plane = fetch_plane(packed, rows, per_group)
    own_then = lax.optimization_barrier((packed, one_off))[0]
    own_twin = plane_shift(own_then, 1)
    half_way = grp_shift(one_off, 1)
    direct = [mask for mask, pieces in plane.items() if len(pieces) == 1]
    relayed = [mask for mask, pieces in plane.items() if len(pieces) > 1]

    cols = [packed, own_twin, one_off, plane_shift(one_off, 1)]
    every = range(len(cols))
    best, *rows_direct = score(
        "compare_direct",
        rows,
        [plane[mask] for mask in direct],
        cols,
        [(k, at, k == at == 0) for k in range(len(direct)) for at in every],
        (2, 3),
        [tuple(every)],
    )
    early = [plane_shift(best, mask) for best, mask in zip(rows_direct[1:], direct[1:])]
    best = lax.optimization_barrier((best, early))[0]
    own, one_off_best, twins, *rows_relayed = score(
        "compare_relayed",
        rows,
        [plane[mask] for mask in relayed],
        cols,
        [(k, at, False) for k in range(len(relayed)) for at in every],
        (2, 3),
        [(0,), (2,), (1, 3)],
        known=every,
        cols_in=[best],
    )
    own, one_off_best = join([own, one_off_best], plane_shift(twins, 1))
    found = [own.reshape(1, 1, -1), rows_direct[0]]
    early += [plane_shift(best, mask) for best, mask in zip(rows_relayed, relayed)]
    found.append(grp_shift(one_off_best.reshape(1, 1, -1), -1))

    blocks = list(plane.values())
    pairs = [(k, 0, False) for k in range(len(blocks))]
    half_then = lax.optimization_barrier((half_way, own))[0]
    half_twin = lax.optimization_barrier((plane_shift(half_then, 1), early))[0]
    for name, block, mask in (("compare_half_way", half_way, 0), ("compare_twin", half_twin, 1)):
        (half_best,) = score(name, rows, blocks, [block], pairs, (), [(0,)])
        found.append(grp_shift(half_best, groups // 2, mask))
    return functools.reduce(jnp.maximum, found + early).reshape(-1)


def solution(mesh):
    return jax.shard_map(
        body,
        mesh=mesh,
        in_specs=(P(("grp", "blk"), None), P(("grp", "blk"), None), P(("grp", "blk"))),
        out_specs=P(("grp", "blk")),
        check_vma=False,
    )
```

```python
import functools

import jax
import jax.numpy as jnp
from jax import lax
from jax.experimental import pallas as pl
from jax.experimental.pallas import tpu as pltpu
from jax.sharding import PartitionSpec as P

CLUSTERS = 64
LANES = 128
TAIL = 16
VMEM = 24 << 20
VMEM_SMALL = 8 << 20


def pack_kernel(per_group, emb_ref, target_ref, cluster_ref, out_ref):
    rows, width = emb_ref.shape
    x = emb_ref[...].astype(jnp.float32)
    scale = lax.rsqrt(jnp.sum(x * x, axis=1, keepdims=True) + 1e-06)
    normed = (x * scale).astype(jnp.bfloat16)
    for at in range(width // LANES):
        out_ref[at * rows : (at + 1) * rows, :] = normed[:, at * LANES : (at + 1) * LANES]
    key = (target_ref[...] // per_group * CLUSTERS + cluster_ref[...] + 1).astype(jnp.float32)
    tail = [key[:, at : at + LANES] for at in range(0, rows, LANES)]
    tail.append(jnp.zeros((TAIL - len(tail), LANES), jnp.float32))
    out_ref[out_ref.shape[0] - TAIL :, :] = jnp.concatenate(tail, axis=0).astype(jnp.bfloat16)


def pack(embeddings, target, cluster, per_group):
    rows, width = embeddings.shape
    return pl.pallas_call(
        functools.partial(pack_kernel, per_group),
        out_shape=jax.ShapeDtypeStruct((rows * width // LANES + TAIL, LANES), jnp.bfloat16),
        compiler_params=pltpu.CompilerParams(vmem_limit_bytes=VMEM_SMALL),
        name="pack",
    )(embeddings, target.reshape(1, rows), cluster.reshape(1, rows))


def unpack(pieces, rows):
    panels = [ref[at : at + rows, :] for ref in pieces for at in range(0, ref.shape[0] - rows + 1, rows)]
    tail = pieces[-1][pieces[-1].shape[0] - TAIL :, :].astype(jnp.float32)
    keys = [tail[at : at + 1, :] for at in range(rows // LANES)]
    return jnp.concatenate(panels, axis=1), jnp.concatenate(keys, axis=1)


def score_kernel(counts, n_cols, pairs, want_rows, known, outs, *refs):
    n_rows = len(counts) if want_rows else 0
    *plane, cols, cols_in, col_outs, row_outs = take(refs, counts + (n_cols, bool(known), len(outs), n_rows))
    rows = col_outs[0].shape[2]
    best = [jnp.full((1, rows), -1.0, jnp.float32)] * n_cols
    for at, col in enumerate(known):
        best[col] = cols_in[0][at]
    cols = [unpack([ref], rows) for ref in cols]
    for k, pieces in enumerate(plane):
        block, keys = unpack(pieces, rows)
        row_keys = jnp.transpose(jnp.broadcast_to(keys, (LANES, rows)))
        row_keys = jnp.concatenate([row_keys] * (rows // LANES), axis=1)
        row_best = None
        for at, same in [(at, same) for one, at, same in pairs if one == k]:
            col, col_keys = cols[at]
            scores = lax.dot_general(
                block, col, (((1,), (1,)), ((), ())), preferred_element_type=jnp.float32
            )
            allowed = row_keys == col_keys
            if same:
                one = lax.broadcasted_iota(jnp.int32, scores.shape, 0)
                other = lax.broadcasted_iota(jnp.int32, scores.shape, 1)
                allowed = allowed & (one != other)
            masked = jnp.where(allowed, scores, -1.0)
            best[at] = jnp.maximum(best[at], jnp.max(masked, axis=0, keepdims=True))
            if at in want_rows:
                for lane in range(0, rows, LANES):
                    part = masked[:, lane : lane + LANES]
                    row_best = part if row_best is None else jnp.maximum(row_best, part)
        if row_best is not None:
            row_outs[k][0] = jnp.max(jnp.transpose(row_best), axis=0, keepdims=True)
    for ref, held in zip(col_outs, outs):
        for at, col in enumerate(held):
            ref[at] = best[col]


def take(refs, counts):
    groups, at = [], 0
    for count in counts:
        groups.append(refs[at : at + count])
        at += count
    return groups


def score(name, rows, plane, cols, pairs, want_rows, outs, known=(), cols_in=()):
    size = cols[0].size
    counts = tuple(len(pieces) for pieces in plane)
    kernel = functools.partial(
        score_kernel, counts, len(cols), tuple(pairs), tuple(want_rows), tuple(known), tuple(outs)
    )
    shapes = [len(held) for held in outs] + [1] * (len(plane) if want_rows else 0)
    return pl.pallas_call(
        kernel,
        out_shape=[jax.ShapeDtypeStruct((count, 1, rows), jnp.float32) for count in shapes],
        compiler_params=pltpu.CompilerParams(vmem_limit_bytes=VMEM),
        cost_estimate=pl.CostEstimate(
            flops=2 * len(pairs) * rows * size,
            bytes_accessed=2 * (len(plane) + len(cols)) * size,
            transcendentals=0,
        ),
        name=name,
    )(*[piece for pieces in plane for piece in pieces], *cols, *cols_in)


def join_kernel(n, *refs):
    for at in range(n):
        refs[n + 1 + at][...] = jnp.maximum(refs[at][...], refs[n][at])


def join(here, got):
    return pl.pallas_call(
        functools.partial(join_kernel, len(here)),
        out_shape=[jax.ShapeDtypeStruct((1, x.shape[-1]), x.dtype) for x in here],
        compiler_params=pltpu.CompilerParams(vmem_limit_bytes=VMEM_SMALL),
        name="join",
    )(*[x.reshape(1, -1) for x in here], got)


def plane_shift(x, mask):
    size = lax.axis_size("blk")
    return lax.ppermute(x, "blk", [(i, i ^ mask) for i in range(size)])


def grp_shift(x, shift, mask=0):
    groups, size = lax.axis_size("grp"), lax.axis_size("blk")
    if not mask:
        return lax.ppermute(x, "grp", [(z, (z + shift) % groups) for z in range(groups)])
    pairs = [
        (z * size + i, (z + shift) % groups * size + (i ^ mask)) for z in range(groups) for i in range(size)
    ]
    return lax.ppermute(x, ("grp", "blk"), pairs)


def fetch_plane(packed, rows, per_group):
    half = packed.shape[0] // rows // 2 * rows
    plane = {0: (packed,)}
    halves = {}
    for mask in sorted(range(2, per_group, 2), key=lambda mask: mask.bit_count()):
        low, high = mask & -mask, 1 << (mask.bit_length() - 1)
        if low == high:
            block = plane_shift(packed, mask)
            plane[mask] = (block,)
            halves[mask] = (block[:half], block[half:])
        else:
            plane[mask] = halves[mask] = (
                plane_shift(halves[mask ^ low][0], low),
                plane_shift(halves[mask ^ high][1], high),
            )
    return plane


def body(embeddings, target, cluster):
    groups = lax.axis_size("grp")
    per_group = lax.axis_size("blk")
    rows = embeddings.shape[0]
    packed = pack(embeddings, target, cluster, per_group)
    one_off = grp_shift(packed, 1)
    plane = fetch_plane(packed, rows, per_group)
    own_then = lax.optimization_barrier((packed, one_off))[0]
    own_twin = plane_shift(own_then, 1)
    half_way = grp_shift(one_off, 1)
    direct = [mask for mask, pieces in plane.items() if len(pieces) == 1]
    relayed = [mask for mask, pieces in plane.items() if len(pieces) > 1]

    cols = [packed, own_twin, one_off, plane_shift(one_off, 1)]
    every = range(len(cols))
    best, *rows_direct = score(
        "compare_direct",
        rows,
        [plane[mask] for mask in direct],
        cols,
        [(k, at, k == at == 0) for k in range(len(direct)) for at in every],
        (2, 3),
        [tuple(every)],
    )
    early = [plane_shift(best, mask) for best, mask in zip(rows_direct[1:], direct[1:])]
    best = lax.optimization_barrier((best, early))[0]
    own, one_off_best, twins, *rows_relayed = score(
        "compare_relayed",
        rows,
        [plane[mask] for mask in relayed],
        cols,
        [(k, at, False) for k in range(len(relayed)) for at in every],
        (2, 3),
        [(0,), (2,), (1, 3)],
        known=every,
        cols_in=[best],
    )
    own, one_off_best = join([own, one_off_best], plane_shift(twins, 1))
    found = [own.reshape(1, 1, -1), rows_direct[0]]
    early += [plane_shift(best, mask) for best, mask in zip(rows_relayed, relayed)]
    found.append(grp_shift(one_off_best.reshape(1, 1, -1), -1))

    blocks = list(plane.values())
    pairs = [(k, 0, False) for k in range(len(blocks))]
    half_then = lax.optimization_barrier((half_way, own, early))[0]
    half_twin = plane_shift(half_then, 1)
    for name, block, mask in (("compare_half_way", half_way, 0), ("compare_twin", half_twin, 1)):
        (half_best,) = score(name, rows, blocks, [block], pairs, (), [(0,)])
        found.append(grp_shift(half_best, groups // 2, mask))
    return functools.reduce(jnp.maximum, found + early).reshape(-1)


def solution(mesh):
    return jax.shard_map(
        body,
        mesh=mesh,
        in_specs=(P(("grp", "blk"), None), P(("grp", "blk"), None), P(("grp", "blk"))),
        out_specs=P(("grp", "blk")),
        check_vma=False,
    )
```

```python
import functools

import jax
import jax.numpy as jnp
from jax import lax
from jax.experimental import pallas as pl
from jax.experimental.pallas import tpu as pltpu
from jax.sharding import PartitionSpec as P

CLUSTERS = 64
LANES = 128
TAIL = 16
VMEM = 24 << 20
VMEM_SMALL = 8 << 20


def pack_kernel(per_group, emb_ref, target_ref, cluster_ref, out_ref):
    rows, width = emb_ref.shape
    x = emb_ref[...].astype(jnp.float32)
    scale = lax.rsqrt(jnp.sum(x * x, axis=1, keepdims=True) + 1e-06)
    normed = (x * scale).astype(jnp.bfloat16)
    for at in range(width // LANES):
        out_ref[at * rows : (at + 1) * rows, :] = normed[:, at * LANES : (at + 1) * LANES]
    key = (target_ref[...] // per_group * CLUSTERS + cluster_ref[...] + 1).astype(jnp.float32)
    tail = [key[:, at : at + LANES] for at in range(0, rows, LANES)]
    tail.append(jnp.zeros((TAIL - len(tail), LANES), jnp.float32))
    out_ref[out_ref.shape[0] - TAIL :, :] = jnp.concatenate(tail, axis=0).astype(jnp.bfloat16)


def pack(embeddings, target, cluster, per_group):
    rows, width = embeddings.shape
    return pl.pallas_call(
        functools.partial(pack_kernel, per_group),
        out_shape=jax.ShapeDtypeStruct((rows * width // LANES + TAIL, LANES), jnp.bfloat16),
        compiler_params=pltpu.CompilerParams(vmem_limit_bytes=VMEM_SMALL),
        name="pack",
    )(embeddings, target.reshape(1, rows), cluster.reshape(1, rows))


def unpack(pieces, rows):
    panels = [ref[at : at + rows, :] for ref in pieces for at in range(0, ref.shape[0] - rows + 1, rows)]
    tail = pieces[-1][pieces[-1].shape[0] - TAIL :, :].astype(jnp.float32)
    keys = [tail[at : at + 1, :] for at in range(rows // LANES)]
    return jnp.concatenate(panels, axis=1), jnp.concatenate(keys, axis=1)


def score_kernel(counts, n_cols, pairs, want_rows, known, outs, *refs):
    n_rows = len(counts) if want_rows else 0
    *blocks, cols_in, col_outs, row_outs = take(refs, counts + n_cols + (bool(known), len(outs), n_rows))
    plane, cols = blocks[: len(counts)], blocks[len(counts) :]
    rows = col_outs[0].shape[2]
    best = [jnp.full((1, rows), -1.0, jnp.float32)] * len(n_cols)
    for at, col in enumerate(known):
        best[col] = cols_in[0][at]
    cols = [unpack(pieces, rows) for pieces in cols]
    for k, pieces in enumerate(plane):
        block, keys = unpack(pieces, rows)
        row_keys = jnp.transpose(jnp.broadcast_to(keys, (LANES, rows)))
        row_keys = jnp.concatenate([row_keys] * (rows // LANES), axis=1)
        row_best = None
        for at, same in [(at, same) for one, at, same in pairs if one == k]:
            col, col_keys = cols[at]
            scores = lax.dot_general(
                block, col, (((1,), (1,)), ((), ())), preferred_element_type=jnp.float32
            )
            allowed = row_keys == col_keys
            if same:
                one = lax.broadcasted_iota(jnp.int32, scores.shape, 0)
                other = lax.broadcasted_iota(jnp.int32, scores.shape, 1)
                allowed = allowed & (one != other)
            masked = jnp.where(allowed, scores, -1.0)
            best[at] = jnp.maximum(best[at], jnp.max(masked, axis=0, keepdims=True))
            if at in want_rows:
                for lane in range(0, rows, LANES):
                    part = masked[:, lane : lane + LANES]
                    row_best = part if row_best is None else jnp.maximum(row_best, part)
        if row_best is not None:
            row_outs[k][0] = jnp.max(jnp.transpose(row_best), axis=0, keepdims=True)
    for ref, held in zip(col_outs, outs):
        for at, col in enumerate(held):
            ref[at] = best[col]


def take(refs, counts):
    groups, at = [], 0
    for count in counts:
        groups.append(refs[at : at + count])
        at += count
    return groups


def score(name, rows, plane, cols, pairs, want_rows, outs, known=(), cols_in=()):
    size = sum(piece.size for piece in cols[0])
    counts = tuple(len(pieces) for pieces in plane)
    n_cols = tuple(len(pieces) for pieces in cols)
    kernel = functools.partial(
        score_kernel, counts, n_cols, tuple(pairs), tuple(want_rows), tuple(known), tuple(outs)
    )
    shapes = [len(held) for held in outs] + [1] * (len(plane) if want_rows else 0)
    return pl.pallas_call(
        kernel,
        out_shape=[jax.ShapeDtypeStruct((count, 1, rows), jnp.float32) for count in shapes],
        compiler_params=pltpu.CompilerParams(vmem_limit_bytes=VMEM),
        cost_estimate=pl.CostEstimate(
            flops=0,
            bytes_accessed=0,
            transcendentals=0,
        ),
        name=name,
    )(*[piece for pieces in (*plane, *cols) for piece in pieces], *cols_in)


def join_kernel(n, *refs):
    for at in range(n):
        refs[n + 1 + at][...] = jnp.maximum(refs[at][...], refs[n][at])


def join(here, got):
    return pl.pallas_call(
        functools.partial(join_kernel, len(here)),
        out_shape=[jax.ShapeDtypeStruct((1, x.shape[-1]), x.dtype) for x in here],
        compiler_params=pltpu.CompilerParams(vmem_limit_bytes=VMEM_SMALL),
        name="join",
    )(*[x.reshape(1, -1) for x in here], got)


def plane_shift(x, mask):
    size = lax.axis_size("blk")
    return lax.ppermute(x, "blk", [(i, i ^ mask) for i in range(size)])


def grp_shift(x, shift, mask=0):
    groups, size = lax.axis_size("grp"), lax.axis_size("blk")
    if not mask:
        return lax.ppermute(x, "grp", [(z, (z + shift) % groups) for z in range(groups)])
    pairs = [
        (z * size + i, (z + shift) % groups * size + (i ^ mask)) for z in range(groups) for i in range(size)
    ]
    return lax.ppermute(x, ("grp", "blk"), pairs)


def cut(block, rows, parts):
    panels = block.shape[0] // rows
    first = (panels - panels // parts) * rows
    return block[:first], block[first:]


def fetch_plane(packed, rows, per_group):
    plane = {0: (packed,)}
    halves = {}
    for mask in sorted(range(2, per_group, 2), key=lambda mask: mask.bit_count()):
        low, high = mask & -mask, 1 << (mask.bit_length() - 1)
        if low == high:
            block = plane_shift(packed, mask)
            plane[mask] = (block,)
            halves[mask] = cut(block, rows, 2)
        else:
            plane[mask] = halves[mask] = (
                plane_shift(halves[mask ^ low][0], low),
                plane_shift(halves[mask ^ high][1], high),
            )
    return plane


def body(embeddings, target, cluster):
    groups = lax.axis_size("grp")
    per_group = lax.axis_size("blk")
    rows = embeddings.shape[0]
    packed = pack(embeddings, target, cluster, per_group)
    one_off = [grp_shift(piece, 1) for piece in cut(packed, rows, 3)]
    plane = fetch_plane(packed, rows, per_group)
    half_way = [grp_shift(piece, 1) for piece in one_off]
    own_then = lax.optimization_barrier((packed, one_off[0]))[0]
    one_off_then = one_off
    own_twin = plane_shift(own_then, 1)
    own_block = lax.optimization_barrier((packed, half_way[0]))[0]
    direct = [mask for mask, pieces in plane.items() if len(pieces) == 1]
    relayed = [mask for mask, pieces in plane.items() if len(pieces) > 1]

    cols = [(own_block,), (own_twin,), one_off, [plane_shift(piece, 1) for piece in one_off_then]]
    every = range(len(cols))
    best, *rows_direct = score(
        "compare_direct",
        rows,
        [plane[mask] for mask in direct],
        cols,
        [(k, at, k == at == 0) for k in range(len(direct)) for at in every],
        (2, 3),
        [tuple(every)],
    )
    early = [plane_shift(best, mask) for best, mask in zip(rows_direct[1:], direct[1:])]
    best = lax.optimization_barrier((best, early))[0]
    own, one_off_best, twins, *rows_relayed = score(
        "compare_relayed",
        rows,
        [plane[mask] for mask in relayed],
        cols,
        [(k, at, False) for k in range(len(relayed)) for at in every],
        (2, 3),
        [(0,), (2,), (1, 3)],
        known=every,
        cols_in=[best],
    )
    own, one_off_best = join([own, one_off_best], plane_shift(twins, 1))
    found = [own.reshape(1, 1, -1), rows_direct[0]]
    early += [plane_shift(best, mask) for best, mask in zip(rows_relayed, relayed)]
    found.append(grp_shift(one_off_best.reshape(1, 1, -1), -1))

    blocks = list(plane.values())
    pairs = [(k, 0, False) for k in range(len(blocks))]
    half_then = lax.optimization_barrier((half_way, own))[0]
    half_twin = [plane_shift(piece, 1) for piece in half_then]
    half_twin = lax.optimization_barrier((half_twin, early))[0]
    for name, block, mask in (("compare_half_way", half_way, 0), ("compare_twin", half_twin, 1)):
        (half_best,) = score(name, rows, blocks, [block], pairs, (), [(0,)])
        found.append(grp_shift(half_best, groups // 2, mask))
    return functools.reduce(jnp.maximum, found + early).reshape(-1)


def solution(mesh):
    return jax.shard_map(
        body,
        mesh=mesh,
        in_specs=(P(("grp", "blk"), None), P(("grp", "blk"), None), P(("grp", "blk"))),
        out_specs=P(("grp", "blk")),
        check_vma=False,
    )
```

```python
import functools

import jax
import jax.numpy as jnp
from jax import lax
from jax.experimental import pallas as pl
from jax.experimental.pallas import tpu as pltpu
from jax.sharding import PartitionSpec as P

CLUSTERS = 64
LANES = 128
TAIL = 16
VMEM = 24 << 20
VMEM_SMALL = 8 << 20


def put_block(x, key, out_ref):
    rows, width = x.shape
    x = x.astype(jnp.float32)
    scale = lax.rsqrt(jnp.sum(x * x, axis=1, keepdims=True) + 1e-06)
    normed = (x * scale).astype(jnp.bfloat16)
    for at in range(width // LANES):
        out_ref[at * rows : (at + 1) * rows, :] = normed[:, at * LANES : (at + 1) * LANES]
    tail = [key[:, at : at + LANES] for at in range(0, rows, LANES)]
    tail.append(jnp.zeros((TAIL - len(tail), LANES), jnp.float32))
    out_ref[out_ref.shape[0] - TAIL :, :] = jnp.concatenate(tail, axis=0).astype(jnp.bfloat16)


def pack_own_kernel(per_group, emb_ref, target_ref, cluster_ref, out_ref, key_ref):
    key = (target_ref[...] // per_group * CLUSTERS + cluster_ref[...] + 1).astype(jnp.float32)
    key_ref[...] = key
    put_block(emb_ref[...], key, out_ref)


def pack_kernel(emb_ref, key_ref, out_ref):
    put_block(emb_ref[...], key_ref[...], out_ref)


def block_shape(embeddings):
    return jax.ShapeDtypeStruct((embeddings.size // LANES + TAIL, LANES), jnp.bfloat16)


def pack_own(embeddings, target, cluster, per_group):
    rows = embeddings.shape[0]
    return pl.pallas_call(
        functools.partial(pack_own_kernel, per_group),
        out_shape=[block_shape(embeddings), jax.ShapeDtypeStruct((1, rows), jnp.float32)],
        compiler_params=pltpu.CompilerParams(vmem_limit_bytes=VMEM_SMALL),
        name="pack_own",
    )(embeddings, target.reshape(1, rows), cluster.reshape(1, rows))


def pack(embeddings, keys):
    return pl.pallas_call(
        pack_kernel,
        out_shape=block_shape(embeddings),
        compiler_params=pltpu.CompilerParams(vmem_limit_bytes=VMEM_SMALL),
        name="pack",
    )(embeddings, keys)


def unpack(pieces, rows):
    panels = [ref[at : at + rows, :] for ref in pieces for at in range(0, ref.shape[0] - rows + 1, rows)]
    tail = pieces[-1][pieces[-1].shape[0] - TAIL :, :].astype(jnp.float32)
    keys = [tail[at : at + 1, :] for at in range(rows // LANES)]
    return jnp.concatenate(panels, axis=1), jnp.concatenate(keys, axis=1)


def score_kernel(counts, n_cols, pairs, want_rows, known, outs, *refs):
    n_rows = len(counts) if want_rows else 0
    *plane, cols, cols_in, col_outs, row_outs = take(refs, counts + (n_cols, bool(known), len(outs), n_rows))
    rows = col_outs[0].shape[2]
    best = [jnp.full((1, rows), -1.0, jnp.float32)] * n_cols
    for at, col in enumerate(known):
        best[col] = cols_in[0][at]
    cols = [unpack([ref], rows) for ref in cols]
    for k, pieces in enumerate(plane):
        block, keys = unpack(pieces, rows)
        row_keys = jnp.transpose(jnp.broadcast_to(keys, (LANES, rows)))
        row_keys = jnp.concatenate([row_keys] * (rows // LANES), axis=1)
        row_best = None
        for at, same in [(at, same) for one, at, same in pairs if one == k]:
            col, col_keys = cols[at]
            scores = lax.dot_general(
                block, col, (((1,), (1,)), ((), ())), preferred_element_type=jnp.float32
            )
            allowed = row_keys == col_keys
            if same:
                one = lax.broadcasted_iota(jnp.int32, scores.shape, 0)
                other = lax.broadcasted_iota(jnp.int32, scores.shape, 1)
                allowed = allowed & (one != other)
            masked = jnp.where(allowed, scores, -1.0)
            best[at] = jnp.maximum(best[at], jnp.max(masked, axis=0, keepdims=True))
            if at in want_rows:
                for lane in range(0, rows, LANES):
                    part = masked[:, lane : lane + LANES]
                    row_best = part if row_best is None else jnp.maximum(row_best, part)
        if row_best is not None:
            row_outs[k][0] = jnp.max(jnp.transpose(row_best), axis=0, keepdims=True)
    for ref, held in zip(col_outs, outs):
        for at, col in enumerate(held):
            ref[at] = best[col]


def take(refs, counts):
    groups, at = [], 0
    for count in counts:
        groups.append(refs[at : at + count])
        at += count
    return groups


def score(name, rows, plane, cols, pairs, want_rows, outs, known=(), cols_in=()):
    size = cols[0].size
    counts = tuple(len(pieces) for pieces in plane)
    kernel = functools.partial(
        score_kernel, counts, len(cols), tuple(pairs), tuple(want_rows), tuple(known), tuple(outs)
    )
    shapes = [len(held) for held in outs] + [1] * (len(plane) if want_rows else 0)
    return pl.pallas_call(
        kernel,
        out_shape=[jax.ShapeDtypeStruct((count, 1, rows), jnp.float32) for count in shapes],
        compiler_params=pltpu.CompilerParams(vmem_limit_bytes=VMEM),
        cost_estimate=pl.CostEstimate(
            flops=2 * len(pairs) * rows * size,
            bytes_accessed=2 * (len(plane) + len(cols)) * size,
            transcendentals=0,
        ),
        name=name,
    )(*[piece for pieces in plane for piece in pieces], *cols, *cols_in)


def join_kernel(n, *refs):
    for at in range(n):
        refs[n + 1 + at][...] = jnp.maximum(refs[at][...], refs[n][at])


def join(here, got):
    return pl.pallas_call(
        functools.partial(join_kernel, len(here)),
        out_shape=[jax.ShapeDtypeStruct((1, x.shape[-1]), x.dtype) for x in here],
        compiler_params=pltpu.CompilerParams(vmem_limit_bytes=VMEM_SMALL),
        name="join",
    )(*[x.reshape(1, -1) for x in here], got)


def plane_shift(x, mask):
    size = lax.axis_size("blk")
    return lax.ppermute(x, "blk", [(i, i ^ mask) for i in range(size)])


def grp_shift(x, shift, mask=0):
    groups, size = lax.axis_size("grp"), lax.axis_size("blk")
    if not mask:
        return lax.ppermute(x, "grp", [(z, (z + shift) % groups) for z in range(groups)])
    pairs = [
        (z * size + i, (z + shift) % groups * size + (i ^ mask)) for z in range(groups) for i in range(size)
    ]
    return lax.ppermute(x, ("grp", "blk"), pairs)


def fetch_plane(packed, rows, per_group):
    half = packed.shape[0] // rows // 2 * rows
    plane = {0: (packed,)}
    halves = {}
    for mask in sorted(range(2, per_group, 2), key=lambda mask: mask.bit_count()):
        low, high = mask & -mask, 1 << (mask.bit_length() - 1)
        if low == high:
            block = plane_shift(packed, mask)
            plane[mask] = (block,)
            halves[mask] = (block[:half], block[half:])
        else:
            plane[mask] = halves[mask] = (
                plane_shift(halves[mask ^ low][0], low),
                plane_shift(halves[mask ^ high][1], high),
            )
    return plane


def body(embeddings, target, cluster):
    groups = lax.axis_size("grp")
    per_group = lax.axis_size("blk")
    rows = embeddings.shape[0]
    one_off_raw = grp_shift(embeddings, 1)
    half_way_raw = grp_shift(one_off_raw, 1)
    packed, keys = pack_own(embeddings, target, cluster, per_group)
    plane = fetch_plane(packed, rows, per_group)
    one_off_keys, half_way_keys = lax.optimization_barrier((grp_shift(keys, 1), grp_shift(keys, 2)))
    one_off = pack(one_off_raw, one_off_keys)
    half_way = pack(half_way_raw, half_way_keys)
    own_then = lax.optimization_barrier((packed, one_off_raw))[0]
    own_twin = plane_shift(own_then, 1)
    direct = [mask for mask, pieces in plane.items() if len(pieces) == 1]
    relayed = [mask for mask, pieces in plane.items() if len(pieces) > 1]

    cols = [packed, own_twin, one_off, plane_shift(one_off, 1)]
    every = range(len(cols))
    best, *rows_direct = score(
        "compare_direct",
        rows,
        [plane[mask] for mask in direct],
        cols,
        [(k, at, k == at == 0) for k in range(len(direct)) for at in every],
        (2, 3),
        [tuple(every)],
    )
    early = [plane_shift(best, mask) for best, mask in zip(rows_direct[1:], direct[1:])]
    best = lax.optimization_barrier((best, early))[0]
    own, one_off_best, twins, *rows_relayed = score(
        "compare_relayed",
        rows,
        [plane[mask] for mask in relayed],
        cols,
        [(k, at, False) for k in range(len(relayed)) for at in every],
        (2, 3),
        [(0,), (2,), (1, 3)],
        known=every,
        cols_in=[best],
    )
    own, one_off_best = join([own, one_off_best], plane_shift(twins, 1))
    found = [own.reshape(1, 1, -1), rows_direct[0]]
    early += [plane_shift(best, mask) for best, mask in zip(rows_relayed, relayed)]
    found.append(grp_shift(one_off_best.reshape(1, 1, -1), -1))

    blocks = list(plane.values())
    pairs = [(k, 0, False) for k in range(len(blocks))]
    half_then = lax.optimization_barrier((half_way, own))[0]
    half_twin = lax.optimization_barrier((plane_shift(half_then, 1), early))[0]
    for name, block, mask in (("compare_half_way", half_way, 0), ("compare_twin", half_twin, 1)):
        (half_best,) = score(name, rows, blocks, [block], pairs, (), [(0,)])
        found.append(grp_shift(half_best, groups // 2, mask))
    return functools.reduce(jnp.maximum, found + early).reshape(-1)


def solution(mesh):
    return jax.shard_map(
        body,
        mesh=mesh,
        in_specs=(P(("grp", "blk"), None), P(("grp", "blk"), None), P(("grp", "blk"))),
        out_specs=P(("grp", "blk")),
        check_vma=False,
    )
```

```python
import functools

import jax
import jax.numpy as jnp
from jax import lax
from jax.experimental import pallas as pl
from jax.experimental.pallas import tpu as pltpu
from jax.sharding import PartitionSpec as P

CLUSTERS = 64
LANES = 128
TAIL = 16
VMEM = 24 << 20
VMEM_SMALL = 8 << 20


def put_block(x, key, out_ref):
    rows, width = x.shape
    x = x.astype(jnp.float32)
    scale = lax.rsqrt(jnp.sum(x * x, axis=1, keepdims=True) + 1e-06)
    normed = (x * scale).astype(jnp.bfloat16)
    for at in range(width // LANES):
        out_ref[at * rows : (at + 1) * rows, :] = normed[:, at * LANES : (at + 1) * LANES]
    tail = [key[:, at : at + LANES] for at in range(0, rows, LANES)]
    tail.append(jnp.zeros((TAIL - len(tail), LANES), jnp.float32))
    out_ref[out_ref.shape[0] - TAIL :, :] = jnp.concatenate(tail, axis=0).astype(jnp.bfloat16)


def pack_own_kernel(per_group, emb_ref, target_ref, cluster_ref, out_ref, key_ref):
    key = (target_ref[...] // per_group * CLUSTERS + cluster_ref[...] + 1).astype(jnp.float32)
    key_ref[...] = key
    put_block(emb_ref[...], key, out_ref)


def pack_kernel(emb_ref, key_ref, out_ref):
    put_block(emb_ref[...], key_ref[...], out_ref)


def block_shape(embeddings):
    return jax.ShapeDtypeStruct((embeddings.size // LANES + TAIL, LANES), jnp.bfloat16)


def pack_own(embeddings, target, cluster, per_group):
    rows = embeddings.shape[0]
    return pl.pallas_call(
        functools.partial(pack_own_kernel, per_group),
        out_shape=[block_shape(embeddings), jax.ShapeDtypeStruct((1, rows), jnp.float32)],
        compiler_params=pltpu.CompilerParams(vmem_limit_bytes=VMEM_SMALL),
        name="pack_own",
    )(embeddings, target.reshape(1, rows), cluster.reshape(1, rows))


def pack(embeddings, keys):
    return pl.pallas_call(
        pack_kernel,
        out_shape=block_shape(embeddings),
        compiler_params=pltpu.CompilerParams(vmem_limit_bytes=VMEM_SMALL),
        name="pack",
    )(embeddings, keys)


def unpack(pieces, rows):
    panels = [ref[at : at + rows, :] for ref in pieces for at in range(0, ref.shape[0] - rows + 1, rows)]
    tail = pieces[-1][pieces[-1].shape[0] - TAIL :, :].astype(jnp.float32)
    keys = [tail[at : at + 1, :] for at in range(rows // LANES)]
    return jnp.concatenate(panels, axis=1), jnp.concatenate(keys, axis=1)


def score_kernel(counts, n_cols, pairs, want_rows, known, outs, *refs):
    n_rows = len(counts) if want_rows else 0
    *blocks, cols_in, col_outs, row_outs = take(refs, counts + n_cols + (bool(known), len(outs), n_rows))
    plane, cols = blocks[: len(counts)], blocks[len(counts) :]
    rows = col_outs[0].shape[2]
    best = [jnp.full((1, rows), -1.0, jnp.float32)] * len(n_cols)
    for at, col in enumerate(known):
        best[col] = cols_in[0][at]
    cols = [unpack(pieces, rows) for pieces in cols]
    for k, pieces in enumerate(plane):
        block, keys = unpack(pieces, rows)
        row_keys = jnp.transpose(jnp.broadcast_to(keys, (LANES, rows)))
        row_keys = jnp.concatenate([row_keys] * (rows // LANES), axis=1)
        row_best = None
        for at, same in [(at, same) for one, at, same in pairs if one == k]:
            col, col_keys = cols[at]
            scores = lax.dot_general(
                block, col, (((1,), (1,)), ((), ())), preferred_element_type=jnp.float32
            )
            allowed = row_keys == col_keys
            if same:
                one = lax.broadcasted_iota(jnp.int32, scores.shape, 0)
                other = lax.broadcasted_iota(jnp.int32, scores.shape, 1)
                allowed = allowed & (one != other)
            masked = jnp.where(allowed, scores, -1.0)
            best[at] = jnp.maximum(best[at], jnp.max(masked, axis=0, keepdims=True))
            if at in want_rows:
                for lane in range(0, rows, LANES):
                    part = masked[:, lane : lane + LANES]
                    row_best = part if row_best is None else jnp.maximum(row_best, part)
        if row_best is not None:
            row_outs[k][0] = jnp.max(jnp.transpose(row_best), axis=0, keepdims=True)
    for ref, held in zip(col_outs, outs):
        for at, col in enumerate(held):
            ref[at] = best[col]


def take(refs, counts):
    groups, at = [], 0
    for count in counts:
        groups.append(refs[at : at + count])
        at += count
    return groups


def score(name, rows, plane, cols, pairs, want_rows, outs, known=(), cols_in=()):
    size = sum(piece.size for piece in cols[0])
    counts = tuple(len(pieces) for pieces in plane)
    n_cols = tuple(len(pieces) for pieces in cols)
    kernel = functools.partial(
        score_kernel, counts, n_cols, tuple(pairs), tuple(want_rows), tuple(known), tuple(outs)
    )
    shapes = [len(held) for held in outs] + [1] * (len(plane) if want_rows else 0)
    return pl.pallas_call(
        kernel,
        out_shape=[jax.ShapeDtypeStruct((count, 1, rows), jnp.float32) for count in shapes],
        compiler_params=pltpu.CompilerParams(vmem_limit_bytes=VMEM),
        cost_estimate=pl.CostEstimate(
            flops=2 * len(pairs) * rows * size,
            bytes_accessed=2 * (len(plane) + len(cols)) * size,
            transcendentals=0,
        ),
        name=name,
    )(*[piece for pieces in (*plane, *cols) for piece in pieces], *cols_in)


def join_kernel(n, *refs):
    for at in range(n):
        refs[n + 1 + at][...] = jnp.maximum(refs[at][...], refs[n][at])


def join(here, got):
    return pl.pallas_call(
        functools.partial(join_kernel, len(here)),
        out_shape=[jax.ShapeDtypeStruct((1, x.shape[-1]), x.dtype) for x in here],
        compiler_params=pltpu.CompilerParams(vmem_limit_bytes=VMEM_SMALL),
        name="join",
    )(*[x.reshape(1, -1) for x in here], got)


def plane_shift(x, mask):
    size = lax.axis_size("blk")
    return lax.ppermute(x, "blk", [(i, i ^ mask) for i in range(size)])


def grp_shift(x, shift, mask=0):
    groups, size = lax.axis_size("grp"), lax.axis_size("blk")
    if not mask:
        return lax.ppermute(x, "grp", [(z, (z + shift) % groups) for z in range(groups)])
    pairs = [
        (z * size + i, (z + shift) % groups * size + (i ^ mask)) for z in range(groups) for i in range(size)
    ]
    return lax.ppermute(x, ("grp", "blk"), pairs)


def cut(block, rows):
    half = block.shape[0] // rows // 2 * rows
    return block[:half], block[half:]


def fetch_plane(packed, rows, per_group):
    plane = {0: (packed,)}
    halves = {}
    for mask in sorted(range(2, per_group, 2), key=lambda mask: mask.bit_count()):
        low, high = mask & -mask, 1 << (mask.bit_length() - 1)
        if low == high:
            block = plane_shift(packed, mask)
            plane[mask] = (block,)
            halves[mask] = cut(block, rows)
        else:
            plane[mask] = halves[mask] = (
                plane_shift(halves[mask ^ low][0], low),
                plane_shift(halves[mask ^ high][1], high),
            )
    return plane


def body(embeddings, target, cluster):
    groups = lax.axis_size("grp")
    per_group = lax.axis_size("blk")
    rows = embeddings.shape[0]
    one_off_raw = grp_shift(embeddings, 1)
    half_way_raw = grp_shift(one_off_raw, 1)
    packed, keys = pack_own(embeddings, target, cluster, per_group)
    plane = fetch_plane(packed, rows, per_group)
    one_off_keys, half_way_keys = lax.optimization_barrier((grp_shift(keys, 1), grp_shift(keys, 2)))
    one_off = pack(one_off_raw, one_off_keys)
    half_way = pack(half_way_raw, half_way_keys)
    own_then = lax.optimization_barrier((packed, one_off_keys))[0]
    own_twin = plane_shift(own_then, 1)
    direct = [mask for mask, pieces in plane.items() if len(pieces) == 1]
    relayed = [mask for mask, pieces in plane.items() if len(pieces) > 1]

    cols = [(packed,), (own_twin,), (one_off,), [plane_shift(piece, 1) for piece in cut(one_off, rows)]]
    every = range(len(cols))
    best, *rows_direct = score(
        "compare_direct",
        rows,
        [plane[mask] for mask in direct],
        cols,
        [(k, at, k == at == 0) for k in range(len(direct)) for at in every],
        (2, 3),
        [tuple(every)],
    )
    early = [plane_shift(best, mask) for best, mask in zip(rows_direct[1:], direct[1:])]
    best = lax.optimization_barrier((best, early))[0]
    own, one_off_best, twins, *rows_relayed = score(
        "compare_relayed",
        rows,
        [plane[mask] for mask in relayed],
        cols,
        [(k, at, False) for k in range(len(relayed)) for at in every],
        (2, 3),
        [(0,), (2,), (1, 3)],
        known=every,
        cols_in=[best],
    )
    own, one_off_best = join([own, one_off_best], plane_shift(twins, 1))
    found = [own.reshape(1, 1, -1), rows_direct[0]]
    early += [plane_shift(best, mask) for best, mask in zip(rows_relayed, relayed)]
    found.append(grp_shift(one_off_best.reshape(1, 1, -1), -1))

    blocks = list(plane.values())
    pairs = [(k, 0, False) for k in range(len(blocks))]
    half_then = lax.optimization_barrier((half_way, own))[0]
    half_twin = lax.optimization_barrier((plane_shift(half_then, 1), early))[0]
    for name, block, mask in (("compare_half_way", half_way, 0), ("compare_twin", half_twin, 1)):
        (half_best,) = score(name, rows, blocks, [(block,)], pairs, (), [(0,)])
        found.append(grp_shift(half_best, groups // 2, mask))
    return functools.reduce(jnp.maximum, found + early).reshape(-1)


def solution(mesh):
    return jax.shard_map(
        body,
        mesh=mesh,
        in_specs=(P(("grp", "blk"), None), P(("grp", "blk"), None), P(("grp", "blk"))),
        out_specs=P(("grp", "blk")),
        check_vma=False,
    )
```

```python
import functools

import jax
import jax.numpy as jnp
from jax import lax
from jax.experimental import pallas as pl
from jax.experimental.pallas import tpu as pltpu
from jax.sharding import PartitionSpec as P

CLUSTERS = 64
LANES = 128
TAIL = 16
VMEM = 24 << 20
VMEM_SMALL = 8 << 20


def put_block(x, key, out_ref):
    rows, width = x.shape
    x = x.astype(jnp.float32)
    scale = lax.rsqrt(jnp.sum(x * x, axis=1, keepdims=True) + 1e-06)
    normed = (x * scale).astype(jnp.bfloat16)
    for at in range(width // LANES):
        out_ref[at * rows : (at + 1) * rows, :] = normed[:, at * LANES : (at + 1) * LANES]
    tail = [key[:, at : at + LANES] for at in range(0, rows, LANES)]
    tail.append(jnp.zeros((TAIL - len(tail), LANES), jnp.float32))
    out_ref[out_ref.shape[0] - TAIL :, :] = jnp.concatenate(tail, axis=0).astype(jnp.bfloat16)


def pack_own_kernel(per_group, emb_ref, target_ref, cluster_ref, out_ref, key_ref):
    key = (target_ref[...] // per_group * CLUSTERS + cluster_ref[...] + 1).astype(jnp.float32)
    key_ref[...] = key
    put_block(emb_ref[...], key, out_ref)


def pack_kernel(emb_ref, key_ref, out_ref):
    put_block(emb_ref[...], key_ref[...], out_ref)


def block_shape(embeddings):
    return jax.ShapeDtypeStruct((embeddings.size // LANES + TAIL, LANES), jnp.bfloat16)


def pack_own(embeddings, target, cluster, per_group):
    rows = embeddings.shape[0]
    return pl.pallas_call(
        functools.partial(pack_own_kernel, per_group),
        out_shape=[block_shape(embeddings), jax.ShapeDtypeStruct((1, rows), jnp.float32)],
        compiler_params=pltpu.CompilerParams(vmem_limit_bytes=VMEM_SMALL),
        name="pack_own",
    )(embeddings, target.reshape(1, rows), cluster.reshape(1, rows))


def pack(embeddings, keys):
    return pl.pallas_call(
        pack_kernel,
        out_shape=block_shape(embeddings),
        compiler_params=pltpu.CompilerParams(vmem_limit_bytes=VMEM_SMALL),
        name="pack",
    )(embeddings, keys)


def unpack(pieces, rows):
    panels = [ref[at : at + rows, :] for ref in pieces for at in range(0, ref.shape[0] - rows + 1, rows)]
    tail = pieces[-1][pieces[-1].shape[0] - TAIL :, :].astype(jnp.float32)
    keys = [tail[at : at + 1, :] for at in range(rows // LANES)]
    return jnp.concatenate(panels, axis=1), jnp.concatenate(keys, axis=1)


def score_kernel(counts, n_cols, pairs, want_rows, known, outs, *refs):
    n_rows = len(counts) if want_rows else 0
    *blocks, cols_in, col_outs, row_outs = take(refs, counts + n_cols + (bool(known), len(outs), n_rows))
    plane, cols = blocks[: len(counts)], blocks[len(counts) :]
    rows = col_outs[0].shape[2]
    best = [jnp.full((1, rows), -1.0, jnp.float32)] * len(n_cols)
    for at, col in enumerate(known):
        best[col] = cols_in[0][at]
    cols = [unpack(pieces, rows) for pieces in cols]
    for k, pieces in enumerate(plane):
        block, keys = unpack(pieces, rows)
        row_keys = jnp.transpose(jnp.broadcast_to(keys, (LANES, rows)))
        row_keys = jnp.concatenate([row_keys] * (rows // LANES), axis=1)
        row_best = None
        for at, same in [(at, same) for one, at, same in pairs if one == k]:
            col, col_keys = cols[at]
            scores = lax.dot_general(
                block, col, (((1,), (1,)), ((), ())), preferred_element_type=jnp.float32
            )
            allowed = row_keys == col_keys
            if same:
                one = lax.broadcasted_iota(jnp.int32, scores.shape, 0)
                other = lax.broadcasted_iota(jnp.int32, scores.shape, 1)
                allowed = allowed & (one != other)
            masked = jnp.where(allowed, scores, -1.0)
            best[at] = jnp.maximum(best[at], jnp.max(masked, axis=0, keepdims=True))
            if at in want_rows:
                for lane in range(0, rows, LANES):
                    part = masked[:, lane : lane + LANES]
                    row_best = part if row_best is None else jnp.maximum(row_best, part)
        if row_best is not None:
            row_outs[k][0] = jnp.max(jnp.transpose(row_best), axis=0, keepdims=True)
    for ref, held in zip(col_outs, outs):
        for at, col in enumerate(held):
            ref[at] = best[col]


def take(refs, counts):
    groups, at = [], 0
    for count in counts:
        groups.append(refs[at : at + count])
        at += count
    return groups


def score(name, rows, plane, cols, pairs, want_rows, outs, known=(), cols_in=()):
    size = sum(piece.size for piece in cols[0])
    counts = tuple(len(pieces) for pieces in plane)
    n_cols = tuple(len(pieces) for pieces in cols)
    kernel = functools.partial(
        score_kernel, counts, n_cols, tuple(pairs), tuple(want_rows), tuple(known), tuple(outs)
    )
    shapes = [len(held) for held in outs] + [1] * (len(plane) if want_rows else 0)
    return pl.pallas_call(
        kernel,
        out_shape=[jax.ShapeDtypeStruct((count, 1, rows), jnp.float32) for count in shapes],
        compiler_params=pltpu.CompilerParams(vmem_limit_bytes=VMEM),
        cost_estimate=pl.CostEstimate(
            flops=2 * len(pairs) * rows * size,
            bytes_accessed=2 * (len(plane) + len(cols)) * size,
            transcendentals=0,
        ),
        name=name,
    )(*[piece for pieces in (*plane, *cols) for piece in pieces], *cols_in)


def join_kernel(n, *refs):
    for at in range(n):
        refs[n + 1 + at][...] = jnp.maximum(refs[at][...], refs[n][at])


def join(here, got):
    return pl.pallas_call(
        functools.partial(join_kernel, len(here)),
        out_shape=[jax.ShapeDtypeStruct((1, x.shape[-1]), x.dtype) for x in here],
        compiler_params=pltpu.CompilerParams(vmem_limit_bytes=VMEM_SMALL),
        name="join",
    )(*[x.reshape(1, -1) for x in here], got)


def plane_shift(x, mask):
    size = lax.axis_size("blk")
    return lax.ppermute(x, "blk", [(i, i ^ mask) for i in range(size)])


def grp_shift(x, shift, mask=0):
    groups, size = lax.axis_size("grp"), lax.axis_size("blk")
    if not mask:
        return lax.ppermute(x, "grp", [(z, (z + shift) % groups) for z in range(groups)])
    pairs = [
        (z * size + i, (z + shift) % groups * size + (i ^ mask)) for z in range(groups) for i in range(size)
    ]
    return lax.ppermute(x, ("grp", "blk"), pairs)


def cut(block, rows):
    half = block.shape[0] // rows // 2 * rows
    return block[:half], block[half:]


def fetch_plane(packed, rows, per_group):
    plane = {0: (packed,)}
    halves = {}
    for mask in sorted(range(2, per_group, 2), key=lambda mask: mask.bit_count()):
        low, high = mask & -mask, 1 << (mask.bit_length() - 1)
        if low == high:
            block = plane_shift(packed, mask)
            plane[mask] = (block,)
            halves[mask] = cut(block, rows)
        else:
            plane[mask] = halves[mask] = (
                plane_shift(halves[mask ^ low][0], low),
                plane_shift(halves[mask ^ high][1], high),
            )
    return plane


def body(embeddings, target, cluster):
    groups = lax.axis_size("grp")
    per_group = lax.axis_size("blk")
    rows = embeddings.shape[0]
    one_off_raw = grp_shift(embeddings, 1)
    half_way_raw = grp_shift(one_off_raw, 1)
    packed, keys = pack_own(embeddings, target, cluster, per_group)
    plane = fetch_plane(packed, rows, per_group)
    one_off_keys, half_way_keys = lax.optimization_barrier((grp_shift(keys, 1), grp_shift(keys, 2)))
    one_off = pack(one_off_raw, one_off_keys)
    half_way = pack(half_way_raw, half_way_keys)
    own_then = lax.optimization_barrier((packed, one_off_keys))[0]
    own_twin = plane_shift(own_then, 1)
    direct = [mask for mask, pieces in plane.items() if len(pieces) == 1]
    relayed = [mask for mask, pieces in plane.items() if len(pieces) > 1]

    cols = [(packed,), (own_twin,), (one_off,), [plane_shift(piece, 1) for piece in cut(one_off, rows)]]
    every = range(len(cols))
    best, *rows_direct = score(
        "compare_direct",
        rows,
        [plane[mask] for mask in direct],
        cols,
        [(k, at, k == at == 0) for k in range(len(direct)) for at in every],
        (2, 3),
        [tuple(every)],
    )
    early = [plane_shift(best, mask) for best, mask in zip(rows_direct[1:], direct[1:])]
    best = lax.optimization_barrier((best, early[0]))[0]
    own, one_off_best, twins, *rows_relayed = score(
        "compare_relayed",
        rows,
        [plane[mask] for mask in relayed],
        cols,
        [(k, at, False) for k in range(len(relayed)) for at in every],
        (2, 3),
        [(0,), (2,), (1, 3)],
        known=every,
        cols_in=[best],
    )
    twins = lax.optimization_barrier((twins, early))[0]
    own, one_off_best = join([own, one_off_best], plane_shift(twins, 1))
    found = [own.reshape(1, 1, -1), rows_direct[0]]
    early += [plane_shift(best, mask) for best, mask in zip(rows_relayed, relayed)]
    found.append(grp_shift(one_off_best.reshape(1, 1, -1), -1))

    blocks = list(plane.values())
    pairs = [(k, 0, False) for k in range(len(blocks))]
    half_then = lax.optimization_barrier((half_way, own))[0]
    half_twin = lax.optimization_barrier((plane_shift(half_then, 1), early))[0]
    for name, block, mask in (("compare_half_way", half_way, 0), ("compare_twin", half_twin, 1)):
        (half_best,) = score(name, rows, blocks, [(block,)], pairs, (), [(0,)])
        found.append(grp_shift(half_best, groups // 2, mask))
    return functools.reduce(jnp.maximum, found + early).reshape(-1)


def solution(mesh):
    return jax.shard_map(
        body,
        mesh=mesh,
        in_specs=(P(("grp", "blk"), None), P(("grp", "blk"), None), P(("grp", "blk"))),
        out_specs=P(("grp", "blk")),
        check_vma=False,
    )
```

```python
import functools

import jax
import jax.numpy as jnp
from jax import lax
from jax.experimental import pallas as pl
from jax.experimental.pallas import tpu as pltpu
from jax.sharding import PartitionSpec as P

CLUSTERS = 64
LANES = 128
TAIL = 16
VMEM = 24 << 20
VMEM_SMALL = 8 << 20


def put_block(x, key, out_ref):
    rows, width = x.shape
    x = x.astype(jnp.float32)
    scale = lax.rsqrt(jnp.sum(x * x, axis=1, keepdims=True) + 1e-06)
    normed = (x * scale).astype(jnp.bfloat16)
    for at in range(width // LANES):
        out_ref[at * rows : (at + 1) * rows, :] = normed[:, at * LANES : (at + 1) * LANES]
    tail = [key[:, at : at + LANES] for at in range(0, rows, LANES)]
    tail.append(jnp.zeros((TAIL - len(tail), LANES), jnp.float32))
    out_ref[out_ref.shape[0] - TAIL :, :] = jnp.concatenate(tail, axis=0).astype(jnp.bfloat16)


def pack_own_kernel(per_group, emb_ref, target_ref, cluster_ref, out_ref, key_ref):
    key = (target_ref[...] // per_group * CLUSTERS + cluster_ref[...] + 1).astype(jnp.float32)
    key_ref[...] = key
    put_block(emb_ref[...], key, out_ref)


def pack_kernel(emb_ref, key_ref, out_ref):
    put_block(emb_ref[...], key_ref[...], out_ref)


def block_shape(embeddings):
    return jax.ShapeDtypeStruct((embeddings.size // LANES + TAIL, LANES), jnp.bfloat16)


def pack_own(embeddings, target, cluster, per_group):
    rows = embeddings.shape[0]
    return pl.pallas_call(
        functools.partial(pack_own_kernel, per_group),
        out_shape=[block_shape(embeddings), jax.ShapeDtypeStruct((1, rows), jnp.float32)],
        compiler_params=pltpu.CompilerParams(vmem_limit_bytes=VMEM_SMALL),
        name="pack_own",
    )(embeddings, target.reshape(1, rows), cluster.reshape(1, rows))


def pack(embeddings, keys):
    return pl.pallas_call(
        pack_kernel,
        out_shape=block_shape(embeddings),
        compiler_params=pltpu.CompilerParams(vmem_limit_bytes=VMEM_SMALL),
        name="pack",
    )(embeddings, keys)


def unpack(pieces, rows):
    panels = [ref[at : at + rows, :] for ref in pieces for at in range(0, ref.shape[0] - rows + 1, rows)]
    tail = pieces[-1][pieces[-1].shape[0] - TAIL :, :].astype(jnp.float32)
    keys = [tail[at : at + 1, :] for at in range(rows // LANES)]
    return jnp.concatenate(panels, axis=1), jnp.concatenate(keys, axis=1)


def score_kernel(counts, n_cols, pairs, want_rows, known, outs, *refs):
    n_rows = len(counts) if want_rows else 0
    *blocks, cols_in, col_outs, row_outs = take(refs, counts + n_cols + (bool(known), len(outs), n_rows))
    plane, cols = blocks[: len(counts)], blocks[len(counts) :]
    rows = col_outs[0].shape[2]
    best = [jnp.full((1, rows), -1.0, jnp.float32)] * len(n_cols)
    for at, col in enumerate(known):
        best[col] = cols_in[0][at]
    cols = [unpack(pieces, rows) for pieces in cols]
    for k, pieces in enumerate(plane):
        block, keys = unpack(pieces, rows)
        row_keys = jnp.transpose(jnp.broadcast_to(keys, (LANES, rows)))
        row_keys = jnp.concatenate([row_keys] * (rows // LANES), axis=1)
        row_best = None
        for at, same in [(at, same) for one, at, same in pairs if one == k]:
            col, col_keys = cols[at]
            scores = lax.dot_general(
                block, col, (((1,), (1,)), ((), ())), preferred_element_type=jnp.float32
            )
            allowed = row_keys == col_keys
            if same:
                one = lax.broadcasted_iota(jnp.int32, scores.shape, 0)
                other = lax.broadcasted_iota(jnp.int32, scores.shape, 1)
                allowed = allowed & (one != other)
            masked = jnp.where(allowed, scores, -1.0)
            best[at] = jnp.maximum(best[at], jnp.max(masked, axis=0, keepdims=True))
            if at in want_rows:
                for lane in range(0, rows, LANES):
                    part = masked[:, lane : lane + LANES]
                    row_best = part if row_best is None else jnp.maximum(row_best, part)
        if row_best is not None:
            row_outs[k][0] = jnp.max(jnp.transpose(row_best), axis=0, keepdims=True)
    for ref, held in zip(col_outs, outs):
        for at, col in enumerate(held):
            ref[at] = best[col]


def take(refs, counts):
    groups, at = [], 0
    for count in counts:
        groups.append(refs[at : at + count])
        at += count
    return groups


def score(name, rows, plane, cols, pairs, want_rows, outs, known=(), cols_in=()):
    size = sum(piece.size for piece in cols[0])
    counts = tuple(len(pieces) for pieces in plane)
    n_cols = tuple(len(pieces) for pieces in cols)
    kernel = functools.partial(
        score_kernel, counts, n_cols, tuple(pairs), tuple(want_rows), tuple(known), tuple(outs)
    )
    shapes = [len(held) for held in outs] + [1] * (len(plane) if want_rows else 0)
    return pl.pallas_call(
        kernel,
        out_shape=[jax.ShapeDtypeStruct((count, 1, rows), jnp.float32) for count in shapes],
        compiler_params=pltpu.CompilerParams(vmem_limit_bytes=VMEM),
        cost_estimate=pl.CostEstimate(
            flops=2 * len(pairs) * rows * size,
            bytes_accessed=2 * (len(plane) + len(cols)) * size,
            transcendentals=0,
        ),
        name=name,
    )(*[piece for pieces in (*plane, *cols) for piece in pieces], *cols_in)


def join_kernel(n, *refs):
    for at in range(n):
        refs[n + 1 + at][...] = jnp.maximum(refs[at][...], refs[n][at])


def join(here, got):
    return pl.pallas_call(
        functools.partial(join_kernel, len(here)),
        out_shape=[jax.ShapeDtypeStruct((1, x.shape[-1]), x.dtype) for x in here],
        compiler_params=pltpu.CompilerParams(vmem_limit_bytes=VMEM_SMALL),
        name="join",
    )(*[x.reshape(1, -1) for x in here], got)


def plane_shift(x, mask):
    size = lax.axis_size("blk")
    return lax.ppermute(x, "blk", [(i, i ^ mask) for i in range(size)])


def grp_shift(x, shift, mask=0):
    groups, size = lax.axis_size("grp"), lax.axis_size("blk")
    if not mask:
        return lax.ppermute(x, "grp", [(z, (z + shift) % groups) for z in range(groups)])
    pairs = [
        (z * size + i, (z + shift) % groups * size + (i ^ mask)) for z in range(groups) for i in range(size)
    ]
    return lax.ppermute(x, ("grp", "blk"), pairs)


def cut(block, rows):
    half = block.shape[0] // rows // 2 * rows
    return block[:half], block[half:]


def fetch_plane(packed, rows, per_group):
    plane = {0: (packed,)}
    halves = {}
    for mask in sorted(range(2, per_group, 2), key=lambda mask: mask.bit_count()):
        low, high = mask & -mask, 1 << (mask.bit_length() - 1)
        if low == high:
            block = plane_shift(packed, mask)
            plane[mask] = (block,)
            halves[mask] = cut(block, rows)
        else:
            plane[mask] = halves[mask] = (
                plane_shift(halves[mask ^ low][0], low),
                plane_shift(halves[mask ^ high][1], high),
            )
    return plane


def body(embeddings, target, cluster):
    groups = lax.axis_size("grp")
    per_group = lax.axis_size("blk")
    rows = embeddings.shape[0]
    one_off_raw = grp_shift(embeddings, 1)
    half_way_raw = grp_shift(one_off_raw, 1)
    packed, keys = pack_own(embeddings, target, cluster, per_group)
    plane = fetch_plane(packed, rows, per_group)
    one_off_keys, half_way_keys = lax.optimization_barrier((grp_shift(keys, 1), grp_shift(keys, 2)))
    one_off = pack(one_off_raw, one_off_keys)
    half_way = pack(half_way_raw, half_way_keys)
    own_then = lax.optimization_barrier((packed, one_off_keys))[0]
    own_twin = plane_shift(own_then, 1)
    direct = [mask for mask, pieces in plane.items() if len(pieces) == 1]
    relayed = [mask for mask, pieces in plane.items() if len(pieces) > 1]

    cols = [(packed,), (own_twin,), (one_off,), [plane_shift(piece, 1) for piece in cut(one_off, rows)]]
    every = range(len(cols))
    best, *rows_direct = score(
        "compare_direct",
        rows,
        [plane[mask] for mask in direct],
        cols,
        [(k, at, k == at == 0) for k in range(len(direct)) for at in every],
        (2, 3),
        [tuple(every)],
    )
    early = [plane_shift(best, mask) for best, mask in zip(rows_direct[1:], direct[1:])]
    best = lax.optimization_barrier((best, early))[0]
    own, one_off_best, twins, *rows_relayed = score(
        "compare_relayed",
        rows,
        [plane[mask] for mask in relayed],
        cols,
        [(k, at, False) for k in range(len(relayed)) for at in every],
        (2, 3),
        [(0,), (2,), (1, 3)],
        known=every,
        cols_in=[best],
    )
    own, one_off_best = join([own, one_off_best], plane_shift(twins, 1))
    found = [own.reshape(1, 1, -1), rows_direct[0]]
    hops = [plane_shift(best, 1 << (mask.bit_length() - 1)) for best, mask in zip(rows_relayed, relayed)]
    late = [plane_shift(hop, mask ^ (1 << (mask.bit_length() - 1))) for hop, mask in zip(hops, relayed)]
    found.append(grp_shift(one_off_best.reshape(1, 1, -1), -1))

    blocks = list(plane.values())
    pairs = [(k, 0, False) for k in range(len(blocks))]
    half_then = lax.optimization_barrier((half_way, own, hops))[0]
    half_twin = lax.optimization_barrier((plane_shift(half_then, 1), early))[0]
    for name, block, mask in (("compare_half_way", half_way, 0), ("compare_twin", half_twin, 1)):
        (half_best,) = score(name, rows, blocks, [(block,)], pairs, (), [(0,)])
        found.append(grp_shift(half_best, groups // 2, mask))
    return functools.reduce(jnp.maximum, found + early + late).reshape(-1)


def solution(mesh):
    return jax.shard_map(
        body,
        mesh=mesh,
        in_specs=(P(("grp", "blk"), None), P(("grp", "blk"), None), P(("grp", "blk"))),
        out_specs=P(("grp", "blk")),
        check_vma=False,
    )
```

```python
import functools

import jax
import jax.numpy as jnp
from jax import lax
from jax.experimental import pallas as pl
from jax.experimental.pallas import tpu as pltpu
from jax.sharding import PartitionSpec as P

CLUSTERS = 64
LANES = 128
TAIL = 16
VMEM = 24 << 20
VMEM_SMALL = 8 << 20


def put_block(x, key, out_ref):
    rows, width = x.shape
    x = x.astype(jnp.float32)
    scale = lax.rsqrt(jnp.sum(x * x, axis=1, keepdims=True) + 1e-06)
    normed = (x * scale).astype(jnp.bfloat16)
    for at in range(width // LANES):
        out_ref[at * rows : (at + 1) * rows, :] = normed[:, at * LANES : (at + 1) * LANES]
    tail = [key[:, at : at + LANES] for at in range(0, rows, LANES)]
    tail.append(jnp.zeros((TAIL - len(tail), LANES), jnp.float32))
    out_ref[out_ref.shape[0] - TAIL :, :] = jnp.concatenate(tail, axis=0).astype(jnp.bfloat16)


def pack_own_kernel(per_group, emb_ref, target_ref, cluster_ref, out_ref, key_ref):
    key = (target_ref[...] // per_group * CLUSTERS + cluster_ref[...] + 1).astype(jnp.float32)
    key_ref[...] = key
    put_block(emb_ref[...], key, out_ref)


def pack_kernel(emb_ref, key_ref, out_ref):
    put_block(emb_ref[...], key_ref[...], out_ref)


def block_shape(embeddings):
    return jax.ShapeDtypeStruct((embeddings.size // LANES + TAIL, LANES), jnp.bfloat16)


def pack_own(embeddings, target, cluster, per_group):
    rows = embeddings.shape[0]
    return pl.pallas_call(
        functools.partial(pack_own_kernel, per_group),
        out_shape=[block_shape(embeddings), jax.ShapeDtypeStruct((1, rows), jnp.float32)],
        compiler_params=pltpu.CompilerParams(vmem_limit_bytes=VMEM_SMALL),
        name="pack_own",
    )(embeddings, target.reshape(1, rows), cluster.reshape(1, rows))


def pack(embeddings, keys):
    return pl.pallas_call(
        pack_kernel,
        out_shape=block_shape(embeddings),
        compiler_params=pltpu.CompilerParams(vmem_limit_bytes=VMEM_SMALL),
        name="pack",
    )(embeddings, keys)


def unpack(pieces, rows):
    panels = [ref[at : at + rows, :] for ref in pieces for at in range(0, ref.shape[0] - rows + 1, rows)]
    tail = pieces[-1][pieces[-1].shape[0] - TAIL :, :].astype(jnp.float32)
    keys = [tail[at : at + 1, :] for at in range(rows // LANES)]
    return jnp.concatenate(panels, axis=1), jnp.concatenate(keys, axis=1)


def score_kernel(counts, n_cols, pairs, want_rows, known, outs, *refs):
    n_rows = len(counts) if want_rows else 0
    *blocks, cols_in, col_outs, row_outs = take(refs, counts + n_cols + (bool(known), len(outs), n_rows))
    plane, cols = blocks[: len(counts)], blocks[len(counts) :]
    rows = col_outs[0].shape[2]
    best = [jnp.full((1, rows), -1.0, jnp.float32)] * len(n_cols)
    for at, col in enumerate(known):
        best[col] = cols_in[0][at]
    cols = [unpack(pieces, rows) for pieces in cols]
    for k, pieces in enumerate(plane):
        block, keys = unpack(pieces, rows)
        row_keys = jnp.transpose(jnp.broadcast_to(keys, (LANES, rows)))
        row_keys = jnp.concatenate([row_keys] * (rows // LANES), axis=1)
        row_best = None
        for at, same in [(at, same) for one, at, same in pairs if one == k]:
            col, col_keys = cols[at]
            scores = lax.dot_general(
                block, col, (((1,), (1,)), ((), ())), preferred_element_type=jnp.float32
            )
            allowed = row_keys == col_keys
            if same:
                one = lax.broadcasted_iota(jnp.int32, scores.shape, 0)
                other = lax.broadcasted_iota(jnp.int32, scores.shape, 1)
                allowed = allowed & (one != other)
            masked = jnp.where(allowed, scores, -1.0)
            best[at] = jnp.maximum(best[at], jnp.max(masked, axis=0, keepdims=True))
            if at in want_rows:
                for lane in range(0, rows, LANES):
                    part = masked[:, lane : lane + LANES]
                    row_best = part if row_best is None else jnp.maximum(row_best, part)
        if row_best is not None:
            row_outs[k][0] = jnp.max(jnp.transpose(row_best), axis=0, keepdims=True)
    for ref, held in zip(col_outs, outs):
        for at, col in enumerate(held):
            ref[at] = best[col]


def take(refs, counts):
    groups, at = [], 0
    for count in counts:
        groups.append(refs[at : at + count])
        at += count
    return groups


def score(name, rows, plane, cols, pairs, want_rows, outs, known=(), cols_in=()):
    size = sum(piece.size for piece in cols[0])
    counts = tuple(len(pieces) for pieces in plane)
    n_cols = tuple(len(pieces) for pieces in cols)
    kernel = functools.partial(
        score_kernel, counts, n_cols, tuple(pairs), tuple(want_rows), tuple(known), tuple(outs)
    )
    shapes = [len(held) for held in outs] + [1] * (len(plane) if want_rows else 0)
    return pl.pallas_call(
        kernel,
        out_shape=[jax.ShapeDtypeStruct((count, 1, rows), jnp.float32) for count in shapes],
        compiler_params=pltpu.CompilerParams(vmem_limit_bytes=VMEM),
        cost_estimate=pl.CostEstimate(
            flops=2 * len(pairs) * rows * size,
            bytes_accessed=2 * (len(plane) + len(cols)) * size,
            transcendentals=0,
        ),
        name=name,
    )(*[piece for pieces in (*plane, *cols) for piece in pieces], *cols_in)


def join_kernel(n, *refs):
    for at in range(n):
        refs[n + 1 + at][...] = jnp.maximum(refs[at][...], refs[n][at])


def join(here, got):
    return pl.pallas_call(
        functools.partial(join_kernel, len(here)),
        out_shape=[jax.ShapeDtypeStruct((1, x.shape[-1]), x.dtype) for x in here],
        compiler_params=pltpu.CompilerParams(vmem_limit_bytes=VMEM_SMALL),
        name="join",
    )(*[x.reshape(1, -1) for x in here], got)


def plane_shift(x, mask):
    size = lax.axis_size("blk")
    return lax.ppermute(x, "blk", [(i, i ^ mask) for i in range(size)])


def grp_shift(x, shift, mask=0):
    groups, size = lax.axis_size("grp"), lax.axis_size("blk")
    if not mask:
        return lax.ppermute(x, "grp", [(z, (z + shift) % groups) for z in range(groups)])
    pairs = [
        (z * size + i, (z + shift) % groups * size + (i ^ mask)) for z in range(groups) for i in range(size)
    ]
    return lax.ppermute(x, ("grp", "blk"), pairs)


def cut(block, rows):
    half = block.shape[0] // rows // 2 * rows
    return block[:half], block[half:]


def fetch_plane(packed, rows, per_group):
    plane = {0: (packed,)}
    halves = {}
    for mask in sorted(range(2, per_group, 2), key=lambda mask: mask.bit_count()):
        low, high = mask & -mask, 1 << (mask.bit_length() - 1)
        if low == high:
            block = plane_shift(packed, mask)
            plane[mask] = (block,)
            halves[mask] = cut(block, rows)
        else:
            plane[mask] = halves[mask] = (
                plane_shift(halves[mask ^ low][0], low),
                plane_shift(halves[mask ^ high][1], high),
            )
    return plane


def body(embeddings, target, cluster):
    groups = lax.axis_size("grp")
    per_group = lax.axis_size("blk")
    rows = embeddings.shape[0]
    one_off_raw = grp_shift(embeddings, 1)
    half_way_raw = grp_shift(one_off_raw, 1)
    packed, keys = pack_own(embeddings, target, cluster, per_group)
    plane = fetch_plane(packed, rows, per_group)
    one_off_keys, half_way_keys = lax.optimization_barrier((grp_shift(keys, 1), grp_shift(keys, 2)))
    one_off = pack(one_off_raw, one_off_keys)
    half_way = pack(half_way_raw, half_way_keys)
    own_then = lax.optimization_barrier((packed, one_off_keys))[0]
    own_twin = plane_shift(own_then, 1)
    direct = [mask for mask, pieces in plane.items() if len(pieces) == 1]
    relayed = [mask for mask, pieces in plane.items() if len(pieces) > 1]

    cols = [(packed,), (own_twin,), (one_off,), [plane_shift(piece, 1) for piece in cut(one_off, rows)]]
    every = range(len(cols))
    best, *rows_direct = score(
        "compare_direct",
        rows,
        [plane[mask] for mask in direct],
        cols,
        [(k, at, k == at == 0) for k in range(len(direct)) for at in every],
        (2, 3),
        [tuple(every)],
    )
    early = [plane_shift(best, mask) for best, mask in zip(rows_direct[1:], direct[1:])]
    best = lax.optimization_barrier((best, early))[0]
    own, one_off_best, twins, *rows_relayed = score(
        "compare_relayed",
        rows,
        [plane[mask] for mask in relayed],
        cols,
        [(k, at, False) for k in range(len(relayed)) for at in every],
        (2, 3),
        [(0,), (2,), (1, 3)],
        known=every,
        cols_in=[best],
    )
    own, one_off_best = join([own, one_off_best], plane_shift(twins, 1))
    found = [own.reshape(1, 1, -1), rows_direct[0]]
    early += [plane_shift(best, mask) for best, mask in zip(rows_relayed, relayed)]
    found.append(grp_shift(one_off_best.reshape(1, 1, -1), -1))

    blocks = list(plane.values())
    pairs = [(k, 0, False) for k in range(len(blocks))]
    half_then = lax.optimization_barrier((half_way, own))[0]
    half_twin = lax.optimization_barrier((plane_shift(half_then, 1), early))[0]
    (half_best,) = score("compare_half_way", rows, blocks, [(half_way,)], pairs, (), [(0,)])
    (twin_best,) = score("compare_twin", rows, blocks, [(half_twin,)], pairs, (), [(0,)])
    (half_best,) = join([half_best], plane_shift(twin_best, 1))
    found.append(grp_shift(half_best.reshape(1, 1, -1), groups // 2))
    return functools.reduce(jnp.maximum, found + early).reshape(-1)


def solution(mesh):
    return jax.shard_map(
        body,
        mesh=mesh,
        in_specs=(P(("grp", "blk"), None), P(("grp", "blk"), None), P(("grp", "blk"))),
        out_specs=P(("grp", "blk")),
        check_vma=False,
    )
```

```python
import functools

import jax
import jax.numpy as jnp
from jax import lax
from jax.experimental import pallas as pl
from jax.experimental.pallas import tpu as pltpu
from jax.sharding import PartitionSpec as P

CLUSTERS = 64
LANES = 128
TAIL = 16
VMEM = 24 << 20
VMEM_SMALL = 8 << 20


def put_block(x, key, out_ref):
    rows, width = x.shape
    x = x.astype(jnp.float32)
    scale = lax.rsqrt(jnp.sum(x * x, axis=1, keepdims=True) + 1e-06)
    normed = (x * scale).astype(jnp.bfloat16)
    for at in range(width // LANES):
        out_ref[at * rows : (at + 1) * rows, :] = normed[:, at * LANES : (at + 1) * LANES]
    tail = [key[:, at : at + LANES] for at in range(0, rows, LANES)]
    tail.append(jnp.zeros((TAIL - len(tail), LANES), jnp.float32))
    out_ref[out_ref.shape[0] - TAIL :, :] = jnp.concatenate(tail, axis=0).astype(jnp.bfloat16)


def pack_own_kernel(per_group, emb_ref, target_ref, cluster_ref, out_ref, key_ref):
    key = (target_ref[...] // per_group * CLUSTERS + cluster_ref[...] + 1).astype(jnp.float32)
    key_ref[...] = key
    put_block(emb_ref[...], key, out_ref)


def pack_kernel(emb_ref, key_ref, out_ref):
    put_block(emb_ref[...], key_ref[...], out_ref)


def block_shape(embeddings):
    return jax.ShapeDtypeStruct((embeddings.size // LANES + TAIL, LANES), jnp.bfloat16)


def pack_own(embeddings, target, cluster, per_group):
    rows = embeddings.shape[0]
    return pl.pallas_call(
        functools.partial(pack_own_kernel, per_group),
        out_shape=[block_shape(embeddings), jax.ShapeDtypeStruct((1, rows), jnp.float32)],
        compiler_params=pltpu.CompilerParams(vmem_limit_bytes=VMEM_SMALL),
        name="pack_own",
    )(embeddings, target.reshape(1, rows), cluster.reshape(1, rows))


def pack(embeddings, keys):
    return pl.pallas_call(
        pack_kernel,
        out_shape=block_shape(embeddings),
        compiler_params=pltpu.CompilerParams(vmem_limit_bytes=VMEM_SMALL),
        name="pack",
    )(embeddings, keys)


def unpack(pieces, rows):
    panels = [ref[at : at + rows, :] for ref in pieces for at in range(0, ref.shape[0] - rows + 1, rows)]
    tail = pieces[-1][pieces[-1].shape[0] - TAIL :, :].astype(jnp.float32)
    keys = [tail[at : at + 1, :] for at in range(rows // LANES)]
    return jnp.concatenate(panels, axis=1), jnp.concatenate(keys, axis=1)


def score_kernel(counts, n_cols, pairs, want_rows, known, outs, *refs):
    n_rows = len(counts) if want_rows else 0
    *blocks, cols_in, col_outs, row_outs = take(refs, counts + n_cols + (bool(known), len(outs), n_rows))
    plane, cols = blocks[: len(counts)], blocks[len(counts) :]
    rows = col_outs[0].shape[2]
    best = [jnp.full((1, rows), -1.0, jnp.float32)] * len(n_cols)
    for at, col in enumerate(known):
        best[col] = cols_in[0][at]
    cols = [unpack(pieces, rows) for pieces in cols]
    for k, pieces in enumerate(plane):
        block, keys = unpack(pieces, rows)
        row_keys = jnp.transpose(jnp.broadcast_to(keys, (LANES, rows)))
        row_keys = jnp.concatenate([row_keys] * (rows // LANES), axis=1)
        row_best = None
        for at, same in [(at, same) for one, at, same in pairs if one == k]:
            col, col_keys = cols[at]
            scores = lax.dot_general(
                block, col, (((1,), (1,)), ((), ())), preferred_element_type=jnp.float32
            )
            allowed = row_keys == col_keys
            if same:
                one = lax.broadcasted_iota(jnp.int32, scores.shape, 0)
                other = lax.broadcasted_iota(jnp.int32, scores.shape, 1)
                allowed = allowed & (one != other)
            masked = jnp.where(allowed, scores, -1.0)
            best[at] = jnp.maximum(best[at], jnp.max(masked, axis=0, keepdims=True))
            if at in want_rows:
                for lane in range(0, rows, LANES):
                    part = masked[:, lane : lane + LANES]
                    row_best = part if row_best is None else jnp.maximum(row_best, part)
        if row_best is not None:
            row_outs[k][0] = jnp.max(jnp.transpose(row_best), axis=0, keepdims=True)
    for ref, held in zip(col_outs, outs):
        for at, col in enumerate(held):
            ref[at] = best[col]


def take(refs, counts):
    groups, at = [], 0
    for count in counts:
        groups.append(refs[at : at + count])
        at += count
    return groups


def score(name, rows, plane, cols, pairs, want_rows, outs, known=(), cols_in=()):
    size = sum(piece.size for piece in cols[0])
    counts = tuple(len(pieces) for pieces in plane)
    n_cols = tuple(len(pieces) for pieces in cols)
    kernel = functools.partial(
        score_kernel, counts, n_cols, tuple(pairs), tuple(want_rows), tuple(known), tuple(outs)
    )
    shapes = [len(held) for held in outs] + [1] * (len(plane) if want_rows else 0)
    return pl.pallas_call(
        kernel,
        out_shape=[jax.ShapeDtypeStruct((count, 1, rows), jnp.float32) for count in shapes],
        compiler_params=pltpu.CompilerParams(vmem_limit_bytes=VMEM),
        cost_estimate=pl.CostEstimate(
            flops=2 * len(pairs) * rows * size,
            bytes_accessed=2 * (len(plane) + len(cols)) * size,
            transcendentals=0,
        ),
        name=name,
    )(*[piece for pieces in (*plane, *cols) for piece in pieces], *cols_in)


def join_kernel(n, *refs):
    for at in range(n):
        refs[n + 1 + at][...] = jnp.maximum(refs[at][...], refs[n][at])


def join(here, got):
    return pl.pallas_call(
        functools.partial(join_kernel, len(here)),
        out_shape=[jax.ShapeDtypeStruct((1, x.shape[-1]), x.dtype) for x in here],
        compiler_params=pltpu.CompilerParams(vmem_limit_bytes=VMEM_SMALL),
        name="join",
    )(*[x.reshape(1, -1) for x in here], got)


def plane_shift(x, mask):
    size = lax.axis_size("blk")
    return lax.ppermute(x, "blk", [(i, i ^ mask) for i in range(size)])


def grp_shift(x, shift, mask=0):
    groups, size = lax.axis_size("grp"), lax.axis_size("blk")
    if not mask:
        return lax.ppermute(x, "grp", [(z, (z + shift) % groups) for z in range(groups)])
    pairs = [
        (z * size + i, (z + shift) % groups * size + (i ^ mask)) for z in range(groups) for i in range(size)
    ]
    return lax.ppermute(x, ("grp", "blk"), pairs)


def cut(block, rows):
    half = block.shape[0] // rows // 2 * rows
    return block[:half], block[half:]


def fetch_plane(packed, rows, per_group):
    plane = {0: (packed,)}
    halves = {}
    for mask in sorted(range(2, per_group, 2), key=lambda mask: mask.bit_count()):
        low, high = mask & -mask, 1 << (mask.bit_length() - 1)
        if low == high:
            block = plane_shift(packed, mask)
            plane[mask] = (block,)
            halves[mask] = cut(block, rows)
        else:
            plane[mask] = halves[mask] = (
                plane_shift(halves[mask ^ low][0], low),
                plane_shift(halves[mask ^ high][1], high),
            )
    return plane


def body(embeddings, target, cluster):
    groups = lax.axis_size("grp")
    per_group = lax.axis_size("blk")
    rows = embeddings.shape[0]
    one_off_raw = grp_shift(embeddings, 1)
    half_way_raw = grp_shift(one_off_raw, 1)
    packed, keys = pack_own(embeddings, target, cluster, per_group)
    plane = fetch_plane(packed, rows, per_group)
    one_off_keys, half_way_keys = lax.optimization_barrier((grp_shift(keys, 1), grp_shift(keys, 2)))
    one_off = pack(one_off_raw, one_off_keys)
    half_way = pack(half_way_raw, half_way_keys)
    own_then = lax.optimization_barrier((packed, one_off_keys))[0]
    own_twin = plane_shift(own_then, 1)
    direct = [mask for mask, pieces in plane.items() if len(pieces) == 1]
    relayed = [mask for mask, pieces in plane.items() if len(pieces) > 1]

    cols = [(packed,), (own_twin,), (one_off,), [plane_shift(piece, 1) for piece in cut(one_off, rows)]]
    every = range(len(cols))
    best, *rows_direct = score(
        "compare_direct",
        rows,
        [plane[mask] for mask in direct],
        cols,
        [(k, at, k == at == 0) for k in range(len(direct)) for at in every],
        (2, 3),
        [tuple(every)],
    )
    early = [plane_shift(best, mask) for best, mask in zip(rows_direct[1:], direct[1:])]
    best = lax.optimization_barrier((best, early[0]))[0]
    own, one_off_best, twins, *rows_relayed = score(
        "compare_relayed",
        rows,
        [plane[mask] for mask in relayed],
        cols,
        [(k, at, False) for k in range(len(relayed)) for at in every],
        (2, 3),
        [(0,), (2,), (1, 3)],
        known=every,
        cols_in=[best],
    )
    twins = lax.optimization_barrier((twins, early))[0]
    own, one_off_best = join([own, one_off_best], plane_shift(twins, 1))
    found = [own.reshape(1, 1, -1), rows_direct[0]]
    early += [plane_shift(best, mask) for best, mask in zip(rows_relayed, relayed)]
    found.append(grp_shift(one_off_best.reshape(1, 1, -1), -1))

    blocks = list(plane.values())
    pairs = [(k, 0, False) for k in range(len(blocks))]
    half_then = lax.optimization_barrier((half_way, own))[0]
    half_twin = [plane_shift(piece, 1) for piece in cut(half_then, rows)]
    half_twin = lax.optimization_barrier((half_twin, early))[0]
    for name, block, mask in (("compare_half_way", [half_way], 0), ("compare_twin", half_twin, 1)):
        (half_best,) = score(name, rows, blocks, [block], pairs, (), [(0,)])
        found.append(grp_shift(half_best, groups // 2, mask))
    return functools.reduce(jnp.maximum, found + early).reshape(-1)


def solution(mesh):
    return jax.shard_map(
        body,
        mesh=mesh,
        in_specs=(P(("grp", "blk"), None), P(("grp", "blk"), None), P(("grp", "blk"))),
        out_specs=P(("grp", "blk")),
        check_vma=False,
    )
```
